128 devices in a mesh: seq: 32 (over y, x, core), exp: 4 (over z).
Axes of the slice: x: 4, y: 4, z: 4, core: 2. Of those that a mesh axis runs over, the one named last changes fastest.
Arguments:
- stream: bfloat16 [16384, 4096], P(('exp', 'seq')), may hold values from -6 to 6
- query_input: bfloat16 [16384, 4096], P(('exp', 'seq')), may hold values from -9 to 9
- key_input: bfloat16 [16384, 4096], P(('exp', 'seq')), may hold values from -4.5 to 4.5
- value_input: bfloat16 [16384, 4096], P(('exp', 'seq')), may hold values from -12 to 12
- sample_id: int32 [16384], replicated, may hold values from 0 to 31, never falling along the last dimension, each value on 1 to 1024 neighbouring positions
- timestep: int32 [32], replicated, may hold values from 0 to 999
- class_id: int32 [32], replicated, may hold values from 0 to 999
- class_table: bfloat16 [1000, 4096], P(None, 'seq'), may hold values from -6 to 6
- mod_weight: bfloat16 [4096, 16384], P(None, ('seq', 'exp')), may hold values from -0.09375 to 0.09375
- router_weight: bfloat16 [4096, 32], replicated, may hold values from -0.09375 to 0.09375
- expert_in: bfloat16 [32, 4096, 4096], P('seq', None, 'exp'), may hold values from -0.09375 to 0.09375
- expert_out: bfloat16 [32, 4096, 4096], P('seq', 'exp'), may hold values from -0.09375 to 0.09375
- picked: int32 [32, 128, 2], P(None, ('exp', 'seq')), may hold values from 0 to 127, as said below
- counts: int32 [32, 128], P(None, ('exp', 'seq')), may hold values from 1 to 2, as said below
Outputs:
- block_output: bfloat16 [16384, 4096], P(('exp', 'seq'))
The draws below stay inside these ranges and needn't reach their ends.
Inputs may be any that keep to these rules, and one draw needn't show every extreme that they name: For j < counts[e, b] the entries picked[e, b, j] are distinct; entries from counts[e, b] on are ignored. `counts`: in every draw one expert has 2 used slots in every block.
All inputs are finite; a program needn't handle non-finite values.
Results may differ from the reference program's by a relative error of at most 0.006.
Values may be sent and summed in bfloat16 or wider, within the bound.
A program may use at most 128 MiB of HBM per device.

```python
import math
import jax
import jax.numpy as jnp
import numpy as np
from jax import lax

D = 4096
FF = 4096
CLASSES = 1000
TOK_DEV = 128
SRC_CAP = 2
MOST = 1024
EXPERTS = 32
TOKENS = 16384
BLOCKS = 128
SAMPLES = 32
N_SEQ = 32


def draw_query_input(key, part):
    key = jax.random.fold_in(key, 11)
    result = jnp.clip(1.5 * jax.random.normal(key, (TOKENS, D), jnp.float32), -6.0, 6.0)
    return result.astype(jnp.bfloat16)


def draw_key_input(key, part):
    key = jax.random.fold_in(key, 12)
    result = jnp.clip(jax.random.normal(key, (TOKENS, D), jnp.float32), -4.5, 4.5)
    return result.astype(jnp.bfloat16)


def draw_picked(key, part):
    key = jax.random.fold_in(key, 21)
    scores = jax.random.randint(key, (EXPERTS, BLOCKS, TOK_DEV), 0, 2 ** 20) * TOK_DEV + jnp.arange(TOK_DEV, dtype=jnp.int32)
    ranking = jnp.argsort(scores, axis=-1)
    return ranking[:, :, :SRC_CAP].astype(jnp.int32)


def draw_counts(key, part):
    key = jax.random.fold_in(key, 22)
    first_key, second_key = jax.random.split(key)
    spread = jax.random.randint(first_key, (EXPERTS, BLOCKS), 1, SRC_CAP + 1)
    full_expert = jax.random.randint(second_key, (), 0, EXPERTS)
    result = jnp.where(jnp.arange(EXPERTS)[:, None] == full_expert, SRC_CAP, spread)
    return result.astype(jnp.int32)


def set_ends(entries, stream_key, smallest, top_value):
    shape = entries.shape
    place = [jax.random.randint(jax.random.fold_in(stream_key, axis), (), 0, shape[axis]) for axis in range(len(shape))]
    entries = entries.at[tuple(place)].set(smallest)
    longest = shape.index(max(shape))
    place[longest] = (place[longest] + 1) % shape[longest]
    return entries.at[tuple(place)].set(top_value)


def shard_levels(rng, shape, pieces, least, high):
    gain, own = 1.0, jax.random.fold_in(rng, 6)
    for axis_at, shards_of in pieces:
        heights = jnp.exp(jax.random.uniform(jax.random.fold_in(own, axis_at), (shards_of,), jnp.float32, least / len(pieces), high / len(pieces)))
        gain = gain * jnp.repeat(heights, shape[axis_at] // shards_of).reshape([-1 if axis == axis_at else 1 for axis in range(len(shape))])
    return gain


def length_profile(number_of, total, bound, lean):
    weights = [(1 << 20) // math.isqrt(standing ** lean) + 1 for standing in range(2, number_of + 1)]
    surplus, given = total - bound - (number_of - 1), [1] * (number_of - 1)
    while surplus > 0:
        movable = [i for i in range(number_of - 1) if given[i] < bound]
        mass, remaining = sum([weights[i] for i in movable]), surplus
        for i in movable:
            extra = min(bound - given[i], max(1, remaining * weights[i] // mass), surplus)
            given[i] = given[i] + extra
            surplus = surplus - extra
    return np.array([bound] + given)


def ragged_sizes(key, count, total, reach, slope):
    if count == 2:
        one = jax.random.randint(key, (), max(1, total - reach), min(reach, total - 1) + 1)
        return jnp.stack([one, total - one])
    tallies = jnp.asarray(length_profile(count, total, reach, slope), jnp.int32)
    couples = (count - 1) // 2
    donor, receiver = tallies[1:1 + 2 * couples:2], tallies[2:2 + 2 * couples:2]
    slack = jnp.minimum(donor - 1, reach - receiver)
    moved = jax.random.randint(jax.random.fold_in(key, 1), (couples,), 0, 1 << 20) % (slack + 1)
    tallies = tallies.at[1:1 + 2 * couples:2].set(donor - moved).at[2:2 + 2 * couples:2].set(receiver + moved)
    return tallies[jax.random.permutation(jax.random.fold_in(key, 2), count)]


def centred(key, shape, scale, most, cuts=(), held_as=jnp.bfloat16):
    array = jax.random.normal(key, shape, jnp.float32) * scale
    if len(cuts) > 0:
        array = shard_levels(key, shape, cuts, -0.22, 0.18) * array
    return jnp.clip(array, min=-most, max=most).astype(held_as)


def setup_inputs(seed: int = 0) -> dict:
    key_of = jax.random.split(jax.random.key(seed), 15)
    return {
        "stream": centred(key_of[0], (TOKENS, D), 1.0, 6.0, ((0, 128),)),
        "query_input": draw_query_input(jax.random.fold_in(key_of[14], 71), 0),
        "key_input": draw_key_input(jax.random.fold_in(key_of[14], 71), 0),
        "value_input": centred(key_of[3], (TOKENS, D), 2.0, 12.0, ((0, 128),)),
        "sample_id": jnp.searchsorted(jnp.cumsum(ragged_sizes(key_of[4], SAMPLES, TOKENS, MOST, 0)), jnp.arange(TOKENS), side="right").astype(jnp.int32),
        "timestep": set_ends(jax.random.randint(key_of[5], (SAMPLES,), 0, 1000), jax.random.fold_in(key_of[5], 1), 0, 999).astype(jnp.int32),
        "class_id": set_ends(jax.random.randint(key_of[6], (SAMPLES,), 0, CLASSES), jax.random.fold_in(key_of[6], 1), 0, CLASSES - 1).astype(jnp.int32),
        "class_table": centred(key_of[7], (CLASSES, D), 1.0, 6.0, ((1, 32),)),
        "mod_weight": centred(key_of[8], (D, 4 * D), D ** -0.5, 0.09375, ((1, 128),)),
        "router_weight": centred(key_of[9], (D, EXPERTS), D ** -0.5, 0.09375),
        "expert_in": centred(key_of[10], (EXPERTS, D, FF), D ** -0.5, 0.09375, ((0, 32), (2, 4))),
        "expert_out": centred(key_of[11], (EXPERTS, FF, D), FF ** -0.5, 0.09375, ((0, 32), (1, 4))),
        "picked": draw_picked(jax.random.fold_in(key_of[14], 71), 0),
        "counts": draw_counts(jax.random.fold_in(key_of[14], 71), 0),
    }


EPS = 1e-06

def embed_time(timestep, width):
    half_width = width // 2
    frequency = jnp.exp(-math.log(10000.0) * jnp.arange(half_width, dtype=jnp.float32) / half_width)
    angles = timestep.astype(jnp.float32)[:, None] * frequency[None, :]
    return jnp.concatenate([jnp.cos(angles), jnp.sin(angles)], axis=1)

def conditioning(timestep, class_id, class_table):
    table_rows = jnp.take(class_table, class_id, axis=0).astype(jnp.float32)
    return jax.nn.silu(embed_time(timestep, class_table.shape[1]) + table_rows).astype(jnp.bfloat16)

def attend(query_input, key_input, value_input, sample_id):
    token_count = query_input.shape[0]
    head_count = N_SEQ
    head_width = D // N_SEQ
    q_block = min(512, TOK_DEV * N_SEQ)
    key_span = q_block + 2 * MOST
    scale_factor = 1.0 / math.sqrt(head_width)
    query_rows = query_input.reshape(token_count, head_count, head_width)
    key_padded = jnp.pad(key_input, ((MOST, MOST), (0, 0))).reshape(-1, head_count, head_width)
    value_padded = jnp.pad(value_input, ((MOST, MOST), (0, 0))).reshape(-1, head_count, head_width)
    id_padded = jnp.pad(sample_id, (MOST, MOST), constant_values=-1)

    def one_block(offset):
        query_part = lax.dynamic_slice_in_dim(query_rows, offset, q_block, 0).astype(jnp.float32)
        key_part = lax.dynamic_slice_in_dim(key_padded, offset, key_span, 0).astype(jnp.float32)
        value_part = lax.dynamic_slice_in_dim(value_padded, offset, key_span, 0).astype(jnp.float32)
        query_ids = lax.dynamic_slice_in_dim(sample_id, offset, q_block, 0)
        key_ids = lax.dynamic_slice_in_dim(id_padded, offset, key_span, 0)
        scores = jnp.einsum('qhd,khd->hqk', query_part, key_part, precision=lax.Precision.HIGHEST) * scale_factor
        allowed = (query_ids[:, None] == key_ids[None, :])[None]
        scores = jnp.where(allowed, scores, -1e+30)
        highest = lax.optimization_barrier(jnp.max(scores, axis=-1, keepdims=True))
        numer = jnp.where(allowed, jnp.exp(scores - highest), 0.0)
        denominator = lax.optimization_barrier(jnp.sum(numer, axis=-1, keepdims=True))
        weights = (numer / denominator).astype(jnp.bfloat16).astype(jnp.float32)
        result = jnp.einsum('hqk,khd->qhd', weights, value_part, precision=lax.Precision.HIGHEST)
        return result.reshape(q_block, head_count * head_width).astype(jnp.bfloat16)
    offsets = jnp.arange(token_count // q_block, dtype=jnp.int32) * q_block
    return lax.map(one_block, offsets).reshape(token_count, head_count * head_width)

def reference(stream, query_input, key_input, value_input, sample_id, timestep, class_id, class_table, mod_weight, router_weight, expert_in, expert_out, picked, counts):
    condition = conditioning(timestep, class_id, class_table)
    modulation = jnp.dot(condition, mod_weight, preferred_element_type=jnp.float32)
    token_mod = jnp.take(modulation, sample_id, axis=0)
    gate_attn, shift, scale_mod, gate_ffn = jnp.split(token_mod, 4, axis=1)
    attended = attend(query_input, key_input, value_input, sample_id)
    residual = stream.astype(jnp.float32) + gate_attn * attended.astype(jnp.float32)
    average = lax.optimization_barrier(jnp.mean(residual, axis=1, keepdims=True))
    centered = residual - average
    variance = lax.optimization_barrier(jnp.mean(centered * centered, axis=1, keepdims=True))
    normed = (centered * lax.rsqrt(variance + EPS) * (1.0 + scale_mod) + shift).astype(jnp.bfloat16)
    router = jax.nn.sigmoid(jnp.dot(normed, router_weight, preferred_element_type=jnp.float32))
    expert_sum = jnp.zeros(residual.shape, jnp.float32)
    block_start = jnp.arange(BLOCKS, dtype=jnp.int32) * TOK_DEV
    slot_index = jnp.arange(SRC_CAP, dtype=jnp.int32)
    for expert in range(EXPERTS):
        token_index = (picked[expert] + block_start[:, None]).reshape(-1).astype(jnp.int32)
        is_valid = (slot_index[None, :] < counts[expert][:, None]).reshape(-1)
        picked_rows = jnp.take(normed, token_index, axis=0)
        hidden = jax.nn.gelu(jnp.dot(picked_rows, expert_in[expert], preferred_element_type=jnp.float32), approximate=True).astype(jnp.bfloat16)
        expert_rows = jnp.dot(hidden, expert_out[expert], preferred_element_type=jnp.float32).astype(jnp.bfloat16)
        weight_rows = jnp.where(is_valid, router[token_index, expert], 0.0)
        expert_sum = expert_sum.at[token_index].add(weight_rows[:, None] * expert_rows.astype(jnp.float32))
    return (residual + gate_ffn * expert_sum).astype(jnp.bfloat16)
```

```python
import math

import jax
import jax.numpy as jnp
from jax import lax
from jax.experimental import pallas as pl
from jax.experimental.pallas import tpu as pltpu
from jax.sharding import PartitionSpec as P

MOST = 1024


EPS = 1e-06


def with_halo(cells, sides, width):
    for axis, dim in sides:
        count = lax.axis_size(axis)
        ends = count - 1
        head = lax.slice_in_dim(cells, 0, width, axis=dim)
        tail = lax.slice_in_dim(cells, cells.shape[dim] - width, cells.shape[dim], axis=dim)
        cells = jnp.concatenate(
            [
                lax.ppermute(tail, axis, [(i, (i + 1) % count) for i in range(ends)]),
                cells,
                lax.ppermute(head, axis, [((i + 1) % count, i) for i in range(ends)]),
            ],
            axis=dim,
        )
    return cells


Q_ROWS = 256
FAR = 32768.0


def attention_kernel(spans, q_ref, fq_ref, k_ref, fk_ref, v_ref, out_ref):
    step = pl.program_id(0)
    start = spans[0, step]
    parts = spans[1, step]
    head_width = q_ref.shape[1]
    factor = math.log2(math.e) / math.sqrt(head_width)
    most_parts = (2 * MOST + Q_ROWS) // Q_ROWS + 1

    def with_parts(number):
        span = number * Q_ROWS

        @pl.when(parts == number)
        def _():
            first = pl.multiple_of(jnp.minimum(start, k_ref.shape[0] - span), 128)
            rows = pl.ds(first, span)
            query = jnp.concatenate([q_ref[...], fq_ref[...]], axis=1)
            keys = jnp.concatenate([k_ref[rows, :], fk_ref[rows, :]], axis=1)
            scores = lax.dot_general(
                query, keys, (((1,), (1,)), ((), ())), preferred_element_type=jnp.float32
            )
            highest = jnp.max(scores, axis=1, keepdims=True)
            numer = jnp.exp2((scores - highest) * factor).astype(jnp.bfloat16)
            values = jnp.concatenate(
                [v_ref[rows, :], jnp.ones((span, head_width), jnp.bfloat16)], axis=1
            )
            total = jnp.dot(numer, values, preferred_element_type=jnp.float32)
            out_ref[...] = (total[:, :head_width] / total[:, head_width:]).astype(jnp.bfloat16)

    for number in range(2, most_parts + 1):
        with_parts(number)


def local_attention(head_query, keys, values, sample_id, exp_index):
    group, head_width = head_query.shape
    extent = keys.shape[0]
    blocks = group // Q_ROWS
    first_token = exp_index * group
    images = jnp.arange(head_width, dtype=jnp.int32)[None, :]
    query_ids = lax.dynamic_slice_in_dim(sample_id, first_token, group, 0)
    id_padded = jnp.pad(sample_id, (MOST, MOST), constant_values=-1)
    key_ids = lax.dynamic_slice_in_dim(id_padded, first_token, extent, 0)
    query_tags = (query_ids[:, None] == images).astype(jnp.bfloat16)
    key_tags = jnp.where(key_ids[:, None] == images, 0.0, -FAR).astype(jnp.bfloat16)
    begins = jnp.sum(
        (sample_id[None, :] < jnp.arange(33, dtype=jnp.int32)[:, None]).astype(jnp.int32), axis=1
    )
    by_block = query_ids.reshape(blocks, Q_ROWS)
    shown = jnp.arange(33, dtype=jnp.int32)[None, :]
    low = jnp.sum(jnp.where(by_block[:, :1] == shown, begins[None, :], 0), axis=1)
    high = jnp.sum(jnp.where(by_block[:, -1:] + 1 == shown, begins[None, :], 0), axis=1)
    low = (low - first_token + MOST) // 128 * 128
    high = high - first_token + MOST
    parts = jnp.maximum((high - low + Q_ROWS - 1) // Q_ROWS, 2)
    spans = jnp.stack([low, parts]).astype(jnp.int32)
    whole = lambda step, spans: (0, 0)
    part = lambda step, spans: (step, 0)
    return pl.pallas_call(
        attention_kernel,
        grid_spec=pltpu.PrefetchScalarGridSpec(
            num_scalar_prefetch=1,
            grid=(blocks,),
            in_specs=[
                pl.BlockSpec((Q_ROWS, head_width), part),
                pl.BlockSpec((Q_ROWS, head_width), part),
                pl.BlockSpec((extent, head_width), whole),
                pl.BlockSpec((extent, head_width), whole),
                pl.BlockSpec((extent, head_width), whole),
            ],
            out_specs=pl.BlockSpec((Q_ROWS, head_width), part),
        ),
        out_shape=jax.ShapeDtypeStruct((group, head_width), jnp.bfloat16),
        compiler_params=pltpu.CompilerParams(vmem_limit_bytes=40 * 2**20),
        name="attention",
    )(spans, head_query, query_tags, keys, key_tags, values)


def on_device(
    stream,
    query_input,
    key_input,
    value_input,
    sample_id,
    timestep,
    class_id,
    class_table,
    mod_weight,
    router_weight,
    expert_in,
    expert_out,
    picked,
    counts,
):
    seq_count = lax.axis_size("seq")
    exp_count = lax.axis_size("exp")
    seq_index = lax.axis_index("seq")
    exp_index = lax.axis_index("exp")
    tok_local, width = stream.shape
    group = tok_local * seq_count
    owner_block = exp_index * seq_count + seq_index
    column_count = class_table.shape[1]
    half_width = width // 2
    column = seq_index * column_count + jnp.arange(column_count, dtype=jnp.int32)
    first_half = column < half_width
    freq_index = jnp.where(first_half, column, column - half_width).astype(jnp.float32)
    frequency = jnp.exp(-math.log(10000.0) * freq_index / half_width)
    angles = timestep.astype(jnp.float32)[:, None] * frequency[None, :]
    embedded = jnp.where(first_half[None, :], jnp.cos(angles), jnp.sin(angles))
    table_rows = jnp.take(class_table, class_id, axis=0).astype(jnp.float32)
    cond_columns = jax.nn.silu(embedded + table_rows).astype(jnp.bfloat16)
    condition = lax.all_gather(cond_columns, "seq", axis=1, tiled=True)
    local_mod = jnp.dot(condition, mod_weight, preferred_element_type=jnp.float32)
    modulation = lax.all_gather(local_mod, ("seq", "exp"), axis=1, tiled=True)
    head_query, head_key, head_value = (
        lax.all_to_all(query_input, "seq", split_axis=1, concat_axis=0, tiled=True),
        lax.all_to_all(key_input, "seq", split_axis=1, concat_axis=0, tiled=True),
        lax.all_to_all(value_input, "seq", split_axis=1, concat_axis=0, tiled=True),
    )
    sides = (("exp", 0),)
    attended_head = local_attention(
        head_query,
        with_halo(head_key, sides, MOST),
        with_halo(head_value, sides, MOST),
        sample_id,
        exp_index,
    )
    attended = lax.all_to_all(attended_head, "seq", split_axis=0, concat_axis=1, tiled=True)
    own_ids = lax.dynamic_slice_in_dim(sample_id, owner_block * tok_local, tok_local, 0)
    selector = (
        own_ids[:, None] == jnp.arange(modulation.shape[0], dtype=jnp.int32)[None, :]
    ).astype(jnp.float32)
    token_mod = jnp.dot(selector, modulation, precision=lax.Precision.HIGHEST)
    gate_attn, shift, scale_mod, gate_ffn = jnp.split(token_mod, 4, axis=1)
    residual = stream.astype(jnp.float32) + gate_attn * attended.astype(jnp.float32)
    average = jnp.mean(residual, axis=1, keepdims=True)
    centered = residual - average
    variance = jnp.mean(centered * centered, axis=1, keepdims=True)
    normed = (centered * lax.rsqrt(variance + EPS) * (1.0 + scale_mod) + shift).astype(jnp.bfloat16)
    router = jax.nn.sigmoid(jnp.dot(normed, router_weight, preferred_element_type=jnp.float32))
    slots = picked[:, 0, :]
    expert_count, slot_total = slots.shape
    live = jnp.arange(slot_total, dtype=jnp.int32)[None, :] < counts[:, 0][:, None]
    chosen_rows = jnp.take(normed, slots.reshape(-1), axis=0).reshape(
        expert_count, slot_total, width
    )
    chosen_rows = jnp.where(live[:, :, None], chosen_rows, jnp.zeros((), jnp.bfloat16))
    w_first = expert_in[0]
    w_second = expert_out[0]
    arrived = lax.all_to_all(chosen_rows, "seq", split_axis=0, concat_axis=0, tiled=True)
    spread = lax.all_gather(arrived, "exp", axis=0, tiled=True)
    product = jnp.einsum(
        "rcd,df->rcf",
        spread.reshape(-1, slot_total, width),
        w_first,
        preferred_element_type=jnp.float32,
    )
    hidden = jax.nn.gelu(product, approximate=True).astype(jnp.bfloat16)
    hidden = hidden.reshape(-1, hidden.shape[-1])
    partial_rows = jnp.dot(hidden, w_second, preferred_element_type=jnp.float32)
    partial_rows = partial_rows.reshape(exp_count, seq_count, slot_total, width)
    gathered = lax.all_to_all(
        partial_rows.astype(jnp.bfloat16), "exp", split_axis=0, concat_axis=0, tiled=True
    ).astype(partial_rows.dtype)
    summed = jnp.sum(gathered, axis=0).astype(jnp.bfloat16)
    homeward = lax.all_to_all(summed, "seq", split_axis=0, concat_axis=0, tiled=True)
    placement = (slots[:, :, None] == jnp.arange(tok_local, dtype=jnp.int32)[None, None, :]) & live[
        :, :, None
    ]
    weighted = placement.astype(jnp.float32) * jnp.transpose(router)[:, None, :]
    expert_sum = jnp.einsum(
        "ect,ecd->td", weighted, homeward.astype(jnp.float32), precision=lax.Precision.HIGHEST
    )
    return (residual + gate_ffn * expert_sum).astype(jnp.bfloat16)


def solution(mesh):
    return jax.shard_map(
        on_device,
        mesh=mesh,
        in_specs=(
            P(("exp", "seq"), None),
            P(("exp", "seq"), None),
            P(("exp", "seq"), None),
            P(("exp", "seq"), None),
            P(),
            P(),
            P(),
            P(None, "seq"),
            P(None, ("seq", "exp")),
            P(),
            P("seq", None, "exp"),
            P("seq", "exp", None),
            P(None, ("exp", "seq"), None),
            P(None, ("exp", "seq")),
        ),
        out_specs=P(("exp", "seq"), None),
        check_vma=False,
    )
```

```python
import math

import jax
import jax.numpy as jnp
from jax import lax
from jax.experimental import pallas as pl
from jax.experimental.pallas import tpu as pltpu
from jax.sharding import PartitionSpec as P

MOST = 1024


EPS = 1e-06


def with_halo(cells, sides, width):
    for axis, dim in sides:
        count = lax.axis_size(axis)
        ends = count - 1
        head = lax.slice_in_dim(cells, 0, width, axis=dim)
        tail = lax.slice_in_dim(cells, cells.shape[dim] - width, cells.shape[dim], axis=dim)
        cells = jnp.concatenate(
            [
                lax.ppermute(tail, axis, [(i, (i + 1) % count) for i in range(ends)]),
                cells,
                lax.ppermute(head, axis, [((i + 1) % count, i) for i in range(ends)]),
            ],
            axis=dim,
        )
    return cells


Q_ROWS = 256
FAR = 32768.0


def attention_kernel(spans, q_ref, fq_ref, k_ref, fk_ref, v_ref, out_ref):
    step = pl.program_id(0)
    start = spans[0, step]
    parts = spans[1, step]
    head_width = q_ref.shape[1]
    factor = math.log2(math.e) / math.sqrt(head_width)
    most_parts = (2 * MOST + Q_ROWS) // Q_ROWS + 1

    def with_parts(number):
        span = number * Q_ROWS

        @pl.when(parts == number)
        def _():
            first = pl.multiple_of(jnp.minimum(start, k_ref.shape[0] - span), 128)
            rows = pl.ds(first, span)
            query = jnp.concatenate([q_ref[...], fq_ref[...]], axis=1)
            keys = jnp.concatenate([k_ref[rows, :], fk_ref[rows, :]], axis=1)
            scores = lax.dot_general(
                query, keys, (((1,), (1,)), ((), ())), preferred_element_type=jnp.float32
            )
            highest = jnp.max(scores, axis=1, keepdims=True)
            numer = jnp.exp2((scores - highest) * factor).astype(jnp.bfloat16)
            values = jnp.concatenate(
                [v_ref[rows, :], jnp.ones((span, head_width), jnp.bfloat16)], axis=1
            )
            total = jnp.dot(numer, values, preferred_element_type=jnp.float32)
            out_ref[...] = (total[:, :head_width] / total[:, head_width:]).astype(jnp.bfloat16)

    for number in range(2, most_parts + 1):
        with_parts(number)


def local_attention(head_query, keys, values, sample_id, exp_index):
    group, head_width = head_query.shape
    extent = keys.shape[0]
    blocks = group // Q_ROWS
    first_token = exp_index * group
    images = jnp.arange(head_width, dtype=jnp.int32)[None, :]
    query_ids = lax.dynamic_slice_in_dim(sample_id, first_token, group, 0)
    id_padded = jnp.pad(sample_id, (MOST, MOST), constant_values=-1)
    key_ids = lax.dynamic_slice_in_dim(id_padded, first_token, extent, 0)
    query_tags = (query_ids[:, None] == images).astype(jnp.bfloat16)
    key_tags = jnp.where(key_ids[:, None] == images, 0.0, -FAR).astype(jnp.bfloat16)
    begins = jnp.sum(
        (sample_id[None, :] < jnp.arange(33, dtype=jnp.int32)[:, None]).astype(jnp.int32), axis=1
    )
    by_block = query_ids.reshape(blocks, Q_ROWS)
    shown = jnp.arange(33, dtype=jnp.int32)[None, :]
    low = jnp.sum(jnp.where(by_block[:, :1] == shown, begins[None, :], 0), axis=1)
    high = jnp.sum(jnp.where(by_block[:, -1:] + 1 == shown, begins[None, :], 0), axis=1)
    low = (low - first_token + MOST) // 128 * 128
    high = high - first_token + MOST
    parts = jnp.maximum((high - low + Q_ROWS - 1) // Q_ROWS, 2)
    spans = jnp.stack([low, parts]).astype(jnp.int32)
    whole = lambda step, spans: (0, 0)
    part = lambda step, spans: (step, 0)
    return pl.pallas_call(
        attention_kernel,
        grid_spec=pltpu.PrefetchScalarGridSpec(
            num_scalar_prefetch=1,
            grid=(blocks,),
            in_specs=[
                pl.BlockSpec((Q_ROWS, head_width), part),
                pl.BlockSpec((Q_ROWS, head_width), part),
                pl.BlockSpec((extent, head_width), whole),
                pl.BlockSpec((extent, head_width), whole),
                pl.BlockSpec((extent, head_width), whole),
            ],
            out_specs=pl.BlockSpec((Q_ROWS, head_width), part),
        ),
        out_shape=jax.ShapeDtypeStruct((group, head_width), jnp.bfloat16),
        compiler_params=pltpu.CompilerParams(vmem_limit_bytes=40 * 2**20),
        name="attention",
    )(spans, head_query, query_tags, keys, key_tags, values)


MESH = pl.DeviceIdType.MESH
PLANE = 32
TILE = 256
PIECES = 8
HALF = TILE * PIECES
SLOT_ROWS = 64


def shifted(place, offset, sign):
    high = (place // 8 + sign * (offset // 8) + 4) % 4
    middle = (place // 2 % 4 + sign * (offset // 2 % 4) + 4) % 4
    return high * 8 + middle * 2 + (place + offset) % 2


def for_offsets(body):
    def step(index, carry):
        body((index * 13) % PLANE)
        return carry

    lax.fori_loop(1, PLANE, step, 0)


def greet(seq_index, exp_index, ring):
    barrier = pltpu.get_barrier_semaphore()

    def hello(offset):
        pl.semaphore_signal(
            barrier,
            inc=1,
            device_id=(shifted(seq_index, offset, 1), exp_index),
            device_id_type=MESH,
        )

    for_offsets(hello)
    for other in ring:
        pl.semaphore_signal(barrier, inc=1, device_id=(seq_index, other), device_id_type=MESH)
    pl.semaphore_wait(barrier, PLANE - 1 + len(ring))


def rows_of(number, size):
    return pl.ds(pl.multiple_of(number * size, size), size)


def experts_kernel(
    attended_ref,
    stream_in,
    modulation_in,
    w_first_in,
    w_second_in,
    selector_ref,
    target_ref,
    placement_ref,
    router_ref,
    out_ref,
    stream_ref,
    modulation_ref,
    w_first,
    w_second,
    attended,
    token_mod,
    residual,
    normed,
    pick,
    unmix,
    mix,
    outgoing,
    landed,
    gathered,
    lined,
    hidden,
    far_out,
    far_in,
    side_raw,
    side_sum,
    raw_in,
    sum_in,
    held,
    own_total,
    homeward,
    back,
    local_sem,
    a_send,
    a_recv,
    d_send,
    d_recv,
    z_send,
    z_recv,
    r_send,
    r_recv,
    b_send,
    b_recv,
):
    seq_index = lax.axis_index("seq")
    exp_index = lax.axis_index("exp")
    right = (exp_index + 1) % 4
    left = (exp_index + 3) % 4
    width = stream_ref.shape[1]
    tokens = stream_ref.shape[0]
    f32 = jnp.float32
    bf16 = jnp.bfloat16

    greet(seq_index, exp_index, (left, right))

    def plane_copy(source, target, send, recv, peer):
        return pltpu.make_async_remote_copy(
            src_ref=source,
            dst_ref=target,
            send_sem=send,
            recv_sem=recv,
            device_id=(peer, exp_index),
            device_id_type=MESH,
        )

    def ring_copy(source, target, send, recv, other):
        return pltpu.make_async_remote_copy(
            src_ref=source,
            dst_ref=target,
            send_sem=send,
            recv_sem=recv,
            device_id=(seq_index, other),
            device_id_type=MESH,
        )

    def attended_copy(offset):
        peer = shifted(seq_index, offset, 1)
        return plane_copy(
            attended_ref.at[rows_of(peer, tokens)],
            attended.at[seq_index],
            a_send.at[offset],
            a_recv.at[offset],
            peer,
        )

    for_offsets(lambda offset: attended_copy(offset).start())
    own_attended = pltpu.make_async_copy(
        attended_ref.at[rows_of(seq_index, tokens)], attended.at[seq_index], local_sem.at[0]
    )
    own_attended.start()
    load_mod = pltpu.make_async_copy(modulation_in, modulation_ref, local_sem.at[1])
    load_mod.start()
    load_stream = pltpu.make_async_copy(stream_in, stream_ref, local_sem.at[2])
    load_stream.start()
    load_first = pltpu.make_async_copy(w_first_in.at[0], w_first, local_sem.at[3])
    load_first.start()
    load_second = pltpu.make_async_copy(w_second_in.at[0], w_second, local_sem.at[4])
    load_second.start()

    count = PIECES * SLOT_ROWS
    row = lax.broadcasted_iota(jnp.int32, (count, count), 0)
    column = lax.broadcasted_iota(jnp.int32, (count, count), 1)
    by_source = ((row >> 1) & 31) * 16 + (row >> 6) * 2 + (row & 1)
    unmix[...] = jnp.where(by_source == column, 1.0, 0.0).astype(bf16)
    by_piece = ((row >> 1) & 7) * SLOT_ROWS + (row >> 4) * 2 + (row & 1)
    mix[...] = jnp.where(by_piece == column, 1.0, 0.0).astype(bf16)
    column = lax.broadcasted_iota(jnp.int32, pick.shape, 1)
    pick[...] = jnp.where(target_ref[...] == column, 1.0, 0.0).astype(bf16)

    load_mod.wait()
    load_stream.wait()

    def spread_mod(step, carry):
        columns = rows_of(step, 512)
        whole = modulation_ref[:, columns]
        first = whole.astype(bf16)
        rest = whole - first.astype(f32)
        second = rest.astype(bf16)
        third = (rest - second.astype(f32)).astype(bf16)
        token_mod[:, columns] = jnp.dot(
            selector_ref[...],
            jnp.concatenate([first, second, third], axis=0),
            preferred_element_type=f32,
        )
        return carry

    lax.fori_loop(0, 4 * width // 512, spread_mod, 0)

    own_attended.wait()
    for_offsets(lambda offset: attended_copy(offset).wait_recv())

    def norm_rows(step, carry):
        rows = rows_of(step, 16)
        heads = jnp.concatenate([attended[head, rows, :] for head in range(PLANE)], axis=1)
        value = stream_ref[rows, :].astype(f32) + token_mod[rows, :width] * heads.astype(f32)
        residual[rows, :] = value
        average = jnp.mean(value, axis=1, keepdims=True)
        centered = value - average
        variance = jnp.mean(centered * centered, axis=1, keepdims=True)
        shift = token_mod[rows, width : 2 * width]
        scale = token_mod[rows, 2 * width : 3 * width]
        normed[rows, :] = (centered * lax.rsqrt(variance + EPS) * (1.0 + scale) + shift).astype(bf16)
        return carry

    lax.fori_loop(0, tokens // 16, norm_rows, 0)

    def dispatch_copy(half, offset):
        peer = shifted(seq_index, offset, 1)
        return plane_copy(
            outgoing.at[half, rows_of(peer, 16)],
            landed.at[half, rows_of(seq_index, 16)],
            d_send.at[half, offset],
            d_recv.at[half, offset],
            peer,
        )

    for half in range(2):
        stacked = jnp.concatenate(
            [
                normed[:, half * HALF + piece * TILE : half * HALF + (piece + 1) * TILE]
                for piece in range(PIECES)
            ],
            axis=0,
        )
        outgoing[half] = jnp.dot(pick[...], stacked, preferred_element_type=f32).astype(bf16)
        for_offsets(lambda offset: dispatch_copy(half, offset).start())
        landed[half, rows_of(seq_index, 16), :] = outgoing[half, rows_of(seq_index, 16), :]

    logits = jnp.dot(normed[...], router_ref[...], preferred_element_type=f32)
    weighted = placement_ref[...] / (1.0 + jnp.exp(-logits))
    weight_first = weighted.astype(bf16)
    weight_rest = weighted - weight_first.astype(f32)
    weight_second = weight_rest.astype(bf16)
    weight_third = (weight_rest - weight_second.astype(f32)).astype(bf16)
    weight_parts = jnp.concatenate([weight_first, weight_second, weight_third], axis=1)

    def line_up(which, half):
        lined[which * SLOT_ROWS : (which + 1) * SLOT_ROWS, half * HALF : (half + 1) * HALF] = (
            jnp.concatenate(
                [
                    gathered[which, half, piece * SLOT_ROWS : (piece + 1) * SLOT_ROWS, :]
                    for piece in range(PIECES)
                ],
                axis=1,
            )
        )

    for half in range(2):
        for_offsets(lambda offset: dispatch_copy(half, offset).wait_recv())
        gathered[0, half] = jnp.dot(
            unmix[...], landed[half], preferred_element_type=f32
        ).astype(bf16)
        if half == 0:
            own_right_0 = ring_copy(
                gathered.at[0, 0], gathered.at[2, 0], z_send.at[0], z_recv.at[0], right
            )
            own_right_0.start()
        else:
            own_left_1 = ring_copy(
                gathered.at[0, 1], gathered.at[3, 1], z_send.at[1], z_recv.at[1], left
            )
            own_left_1.start()
        line_up(0, half)
    own_right_0.wait_recv()
    on_right_0 = ring_copy(
        gathered.at[2, 0], gathered.at[1, 0], z_send.at[2], z_recv.at[2], right
    )
    on_right_0.start()
    own_left_1.wait_recv()
    on_left_1 = ring_copy(gathered.at[3, 1], gathered.at[1, 1], z_send.at[3], z_recv.at[3], left)
    on_left_1.start()
    own_right_1 = ring_copy(
        gathered.at[0, 1], gathered.at[2, 1], z_send.at[4], z_recv.at[4], right
    )
    own_right_1.start()
    own_left_0 = ring_copy(gathered.at[0, 0], gathered.at[3, 0], z_send.at[5], z_recv.at[5], left)
    own_left_0.start()
    line_up(2, 0)
    line_up(3, 1)
    load_first.wait()
    load_second.wait()

    def first_product(base):
        rows = slice(base, base + 2 * SLOT_ROWS)

        def columns_of(step, carry):
            columns = rows_of(step, 256)
            product = jnp.dot(lined[rows, :], w_first[:, columns], preferred_element_type=f32)
            hidden[rows, columns] = jax.nn.gelu(product, approximate=True).astype(bf16)
            return carry

        lax.fori_loop(0, w_first.shape[1] // 256, columns_of, 0)

    def second_product(base, half, lower, upper):
        rows = slice(base, base + 2 * SLOT_ROWS)

        def columns_of(step, carry):
            columns = rows_of(step, 256)
            product = jnp.dot(
                hidden[rows, :],
                w_second[:, rows_of(step + half * (HALF // 256), 256)],
                preferred_element_type=f32,
            )
            lower[:, columns] = product[:SLOT_ROWS].astype(lower.dtype)
            upper[:, columns] = product[SLOT_ROWS:].astype(upper.dtype)
            return carry

        lax.fori_loop(0, HALF // 256, columns_of, 0)

    on_right_0.wait_recv()
    line_up(1, 0)
    on_left_1.wait_recv()
    line_up(1, 1)
    first_product(0)
    second_product(0, 0, own_total.at[0], far_out.at[0])
    far_right = ring_copy(far_out.at[0], far_in.at[0], r_send.at[0], r_recv.at[0], right)
    far_right.start()
    second_product(0, 1, own_total.at[1], far_out.at[1])
    far_left = ring_copy(far_out.at[1], far_in.at[1], r_send.at[1], r_recv.at[1], left)
    far_left.start()
    own_right_1.wait_recv()
    line_up(2, 1)
    own_left_0.wait_recv()
    line_up(3, 0)
    first_product(2 * SLOT_ROWS)
    second_product(2 * SLOT_ROWS, 0, side_raw.at[0], held.at[0])
    raw_left = ring_copy(side_raw.at[0], raw_in.at[0], r_send.at[2], r_recv.at[2], left)
    raw_left.start()
    second_product(2 * SLOT_ROWS, 1, held.at[1], side_raw.at[1])
    raw_right = ring_copy(side_raw.at[1], raw_in.at[1], r_send.at[3], r_recv.at[3], right)
    raw_right.start()
    far_right.wait_recv()
    side_sum[0] = (held[0] + far_in[0].astype(f32)).astype(bf16)
    sum_right = ring_copy(side_sum.at[0], sum_in.at[0], r_send.at[4], r_recv.at[4], right)
    sum_right.start()
    far_left.wait_recv()
    side_sum[1] = (held[1] + far_in[1].astype(f32)).astype(bf16)
    sum_left = ring_copy(side_sum.at[1], sum_in.at[1], r_send.at[5], r_recv.at[5], left)
    sum_left.start()

    def return_copy(half, offset):
        peer = shifted(seq_index, offset, 1)
        return plane_copy(
            homeward.at[half, rows_of(peer, 16)],
            back.at[half, rows_of(seq_index, 16)],
            b_send.at[half, offset],
            b_recv.at[half, offset],
            peer,
        )

    for half, raw, summed in ((0, raw_left, sum_right), (1, raw_right, sum_left)):
        raw.wait_recv()
        summed.wait_recv()
        total = (
            own_total[half] + raw_in[half].astype(f32) + sum_in[half].astype(f32)
        ).astype(bf16)
        stacked = jnp.concatenate(
            [total[:, piece * TILE : (piece + 1) * TILE] for piece in range(PIECES)], axis=0
        )
        homeward[half] = jnp.dot(mix[...], stacked, preferred_element_type=f32).astype(bf16)
        for_offsets(lambda offset: return_copy(half, offset).start())
        back[half, rows_of(seq_index, 16), :] = homeward[half, rows_of(seq_index, 16), :]

    for half in range(2):
        for_offsets(lambda offset: return_copy(half, offset).wait_recv())
        ordered = jnp.dot(unmix[...], back[half], preferred_element_type=f32).astype(bf16)
        for piece in range(PIECES):
            rows = ordered[piece * SLOT_ROWS : (piece + 1) * SLOT_ROWS, :]
            begin = half * HALF + piece * TILE
            columns = slice(begin, begin + TILE)
            expert_sum = jnp.dot(
                weight_parts, jnp.concatenate([rows, rows, rows], axis=0), preferred_element_type=f32
            )
            gate = token_mod[:, 3 * width + begin : 3 * width + begin + TILE]
            out_ref[:, columns] = (residual[:, columns] + gate * expert_sum).astype(bf16)

    for_offsets(lambda offset: attended_copy(offset).wait_send())
    for half in range(2):
        for_offsets(lambda offset: dispatch_copy(half, offset).wait_send())
        for_offsets(lambda offset: return_copy(half, offset).wait_send())
    for copy in (
        own_right_0,
        own_left_1,
        on_right_0,
        on_left_1,
        own_right_1,
        own_left_0,
        far_right,
        far_left,
        raw_left,
        raw_right,
        sum_right,
        sum_left,
    ):
        copy.wait_send()


def feed_forward(
    attended_head, stream, modulation, expert_in, expert_out, selector, target, placement, router
):
    tokens, width = stream.shape
    bf16 = jnp.bfloat16
    f32 = jnp.float32
    part = expert_in.shape[2]
    block = PIECES * SLOT_ROWS
    anywhere = pl.BlockSpec(memory_space=pl.ANY)
    inside = pl.BlockSpec(memory_space=pltpu.VMEM)
    dma = pltpu.SemaphoreType.DMA
    return pl.pallas_call(
        experts_kernel,
        out_shape=jax.ShapeDtypeStruct((tokens, width), bf16),
        in_specs=[anywhere] * 5 + [inside] * 4,
        out_specs=inside,
        scratch_shapes=[
            pltpu.VMEM((tokens, width), bf16),
            pltpu.VMEM(modulation.shape, f32),
            pltpu.VMEM((width, part), bf16),
            pltpu.VMEM((part, width), bf16),
            pltpu.VMEM((PLANE, tokens, width // PLANE), bf16),
            pltpu.VMEM((tokens, 4 * width), f32),
            pltpu.VMEM((tokens, width), f32),
            pltpu.VMEM((tokens, width), bf16),
            pltpu.VMEM((block, PIECES * tokens), bf16),
            pltpu.VMEM((block, block), bf16),
            pltpu.VMEM((block, block), bf16),
            pltpu.VMEM((2, block, TILE), bf16),
            pltpu.VMEM((2, block, TILE), bf16),
            pltpu.VMEM((4, 2, block, TILE), bf16),
            pltpu.VMEM((4 * SLOT_ROWS, width), bf16),
            pltpu.VMEM((4 * SLOT_ROWS, part), bf16),
            pltpu.VMEM((2, SLOT_ROWS, HALF), bf16),
            pltpu.VMEM((2, SLOT_ROWS, HALF), bf16),
            pltpu.VMEM((2, SLOT_ROWS, HALF), bf16),
            pltpu.VMEM((2, SLOT_ROWS, HALF), bf16),
            pltpu.VMEM((2, SLOT_ROWS, HALF), bf16),
            pltpu.VMEM((2, SLOT_ROWS, HALF), bf16),
            pltpu.VMEM((2, SLOT_ROWS, HALF), f32),
            pltpu.VMEM((2, SLOT_ROWS, HALF), f32),
            pltpu.VMEM((2, block, TILE), bf16),
            pltpu.VMEM((2, block, TILE), bf16),
            dma((5,)),
            dma((PLANE,)),
            dma((PLANE,)),
            dma((2, PLANE)),
            dma((2, PLANE)),
            dma((6,)),
            dma((6,)),
            dma((6,)),
            dma((6,)),
            dma((2, PLANE)),
            dma((2, PLANE)),
        ],
        compiler_params=pltpu.CompilerParams(
            collective_id=1, has_side_effects=True, vmem_limit_bytes=58 * 2**20
        ),
        name="experts",
    )(
        attended_head,
        stream,
        modulation,
        expert_in,
        expert_out,
        selector,
        target,
        placement,
        router,
    )


def on_device(
    stream,
    query_input,
    key_input,
    value_input,
    sample_id,
    timestep,
    class_id,
    class_table,
    mod_weight,
    router_weight,
    expert_in,
    expert_out,
    picked,
    counts,
):
    seq_count = lax.axis_size("seq")
    seq_index = lax.axis_index("seq")
    exp_index = lax.axis_index("exp")
    tok_local, width = stream.shape
    group = tok_local * seq_count
    owner_block = exp_index * seq_count + seq_index
    column_count = class_table.shape[1]
    half_width = width // 2
    column = seq_index * column_count + jnp.arange(column_count, dtype=jnp.int32)
    first_half = column < half_width
    freq_index = jnp.where(first_half, column, column - half_width).astype(jnp.float32)
    frequency = jnp.exp(-math.log(10000.0) * freq_index / half_width)
    angles = timestep.astype(jnp.float32)[:, None] * frequency[None, :]
    embedded = jnp.where(first_half[None, :], jnp.cos(angles), jnp.sin(angles))
    table_rows = jnp.take(class_table, class_id, axis=0).astype(jnp.float32)
    cond_columns = jax.nn.silu(embedded + table_rows).astype(jnp.bfloat16)
    condition = lax.all_gather(cond_columns, "seq", axis=1, tiled=True)
    local_mod = jnp.dot(condition, mod_weight, preferred_element_type=jnp.float32)
    modulation = lax.all_gather(local_mod, ("seq", "exp"), axis=1, tiled=True)
    head_query, head_key, head_value = (
        lax.all_to_all(query_input, "seq", split_axis=1, concat_axis=0, tiled=True),
        lax.all_to_all(key_input, "seq", split_axis=1, concat_axis=0, tiled=True),
        lax.all_to_all(value_input, "seq", split_axis=1, concat_axis=0, tiled=True),
    )
    sides = (("exp", 0),)
    attended_head = local_attention(
        head_query,
        with_halo(head_key, sides, MOST),
        with_halo(head_value, sides, MOST),
        sample_id,
        exp_index,
    )
    own_ids = lax.dynamic_slice_in_dim(sample_id, owner_block * tok_local, tok_local, 0)
    samples = modulation.shape[0]
    selector = (
        own_ids[:, None] == jnp.arange(3 * samples, dtype=jnp.int32)[None, :] % samples
    ).astype(jnp.bfloat16)
    slots = picked[:, 0, :]
    expert_count, slot_total = slots.shape
    live = jnp.arange(slot_total, dtype=jnp.int32)[None, :] < counts[:, 0][:, None]
    chosen = jnp.where(live, slots, -1)
    piece = jnp.arange(PIECES, dtype=jnp.int32)[None, :, None]
    target = jnp.where(live[:, None, :], slots[:, None, :] + piece * tok_local, -1).reshape(-1, 1)
    placement = (
        chosen.reshape(1, -1) == jnp.arange(tok_local, dtype=jnp.int32)[:, None]
    ).astype(jnp.float32)
    return feed_forward(
        attended_head,
        stream,
        modulation,
        expert_in,
        expert_out,
        selector,
        target,
        placement,
        jnp.repeat(router_weight, slot_total, axis=1),
    )


def solution(mesh):
    return jax.shard_map(
        on_device,
        mesh=mesh,
        in_specs=(
            P(("exp", "seq"), None),
            P(("exp", "seq"), None),
            P(("exp", "seq"), None),
            P(("exp", "seq"), None),
            P(),
            P(),
            P(),
            P(None, "seq"),
            P(None, ("seq", "exp")),
            P(),
            P("seq", None, "exp"),
            P("seq", "exp", None),
            P(None, ("exp", "seq"), None),
            P(None, ("exp", "seq")),
        ),
        out_specs=P(("exp", "seq"), None),
        check_vma=False,
    )
```

```python
import math

import jax
import jax.numpy as jnp
from jax import lax
from jax.experimental import pallas as pl
from jax.experimental.pallas import tpu as pltpu
from jax.sharding import PartitionSpec as P

MOST = 1024


EPS = 1e-06


Q_ROWS = 256
FAR = 32768.0


def attention_kernel(spans, q_ref, fq_ref, k_ref, fk_ref, v_ref, out_ref):
    step = pl.program_id(0)
    start = spans[0, step]
    parts = spans[1, step]
    head_width = q_ref.shape[1]
    factor = math.log2(math.e) / math.sqrt(head_width)
    most_parts = (2 * MOST + Q_ROWS) // Q_ROWS + 1

    def with_parts(number):
        span = number * Q_ROWS

        @pl.when(parts == number)
        def _():
            first = pl.multiple_of(jnp.minimum(start, k_ref.shape[0] - span), 128)
            rows = pl.ds(first, span)
            query = jnp.concatenate([q_ref[...], fq_ref[...]], axis=1)
            keys = jnp.concatenate([k_ref[rows, :], fk_ref[rows, :]], axis=1)
            scores = lax.dot_general(
                query, keys, (((1,), (1,)), ((), ())), preferred_element_type=jnp.float32
            )
            highest = jnp.max(scores, axis=1, keepdims=True)
            numer = jnp.exp2((scores - highest) * factor).astype(jnp.bfloat16)
            values = jnp.concatenate(
                [v_ref[rows, :], jnp.ones((span, head_width), jnp.bfloat16)], axis=1
            )
            total = jnp.dot(numer, values, preferred_element_type=jnp.float32)
            out_ref[...] = (total[:, :head_width] / total[:, head_width:]).astype(jnp.bfloat16)

    for number in range(2, most_parts + 1):
        with_parts(number)


def local_attention(spans, head_query, query_tags, keys, key_tags, values):
    group, head_width = head_query.shape
    extent = keys.shape[0]
    blocks = group // Q_ROWS
    whole = lambda step, spans: (0, 0)
    part = lambda step, spans: (step, 0)
    return pl.pallas_call(
        attention_kernel,
        grid_spec=pltpu.PrefetchScalarGridSpec(
            num_scalar_prefetch=1,
            grid=(blocks,),
            in_specs=[
                pl.BlockSpec((Q_ROWS, head_width), part),
                pl.BlockSpec((Q_ROWS, head_width), part),
                pl.BlockSpec((extent, head_width), whole),
                pl.BlockSpec((extent, head_width), whole),
                pl.BlockSpec((extent, head_width), whole),
            ],
            out_specs=pl.BlockSpec((Q_ROWS, head_width), part),
        ),
        out_shape=jax.ShapeDtypeStruct((group, head_width), jnp.bfloat16),
        compiler_params=pltpu.CompilerParams(vmem_limit_bytes=60 * 2**20),
        name="attention",
    )(spans, head_query, query_tags, keys, key_tags, values)


MESH = pl.DeviceIdType.MESH
PLANE = 32
TILE = 256
PIECES = 8
HALF = TILE * PIECES
SLOT_ROWS = 64


def shifted(place, offset, sign):
    high = (place // 8 + sign * (offset // 8) + 4) % 4
    middle = (place // 2 % 4 + sign * (offset // 2 % 4) + 4) % 4
    return high * 8 + middle * 2 + (place + offset) % 2


def for_offsets(body):
    def step(index, carry):
        body((index * 13) % PLANE)
        return carry

    lax.fori_loop(1, PLANE, step, 0)


def greet(seq_index, exp_index, ring):
    barrier = pltpu.get_barrier_semaphore()

    def hello(offset):
        pl.semaphore_signal(
            barrier,
            inc=1,
            device_id=(shifted(seq_index, offset, 1), exp_index),
            device_id_type=MESH,
        )

    for_offsets(hello)
    for other in ring:
        pl.semaphore_signal(barrier, inc=1, device_id=(seq_index, other), device_id_type=MESH)
    pl.semaphore_wait(barrier, PLANE - 1 + len(ring))


def rows_of(number, size):
    return pl.ds(pl.multiple_of(number * size, size), size)


def exchange_kernel(
    query_in,
    key_in,
    value_in,
    weight_in,
    condition_ref,
    ids_ref,
    query_out,
    key_out,
    value_out,
    query_tags_out,
    key_tags_out,
    modulation_out,
    spans_out,
    conditions,
    weight,
    own_modulation,
    query_tags,
    key_tags,
    local_sem,
    c_send,
    c_recv,
    p_send,
    p_recv,
    h_send,
    h_recv,
    m_send,
    m_recv,
):
    seq_index = lax.axis_index("seq")
    exp_index = lax.axis_index("exp")
    tokens = query_in.shape[0]
    group, head_width = query_out.shape
    at_y = seq_index // 8
    at_x = seq_index // 2 % 4
    core = seq_index % 2
    f32 = jnp.float32
    bf16 = jnp.bfloat16

    greet(seq_index, exp_index, [(exp_index + step) % 4 for step in (1, 2, 3)])

    def copy_to(source, target, send, recv, peer, other):
        return pltpu.make_async_remote_copy(
            src_ref=source,
            dst_ref=target,
            send_sem=send,
            recv_sem=recv,
            device_id=(peer, other),
            device_id_type=MESH,
        )

    load_weight = pltpu.make_async_copy(weight_in, weight, local_sem.at[0])
    load_weight.start()

    def condition_copy(offset):
        return copy_to(
            condition_ref,
            conditions.at[seq_index],
            c_send.at[offset],
            c_recv.at[offset],
            shifted(seq_index, offset, 1),
            exp_index,
        )

    for_offsets(lambda offset: condition_copy(offset).start())
    conditions[seq_index] = condition_ref[...]

    arrays = ((key_in, key_out, MOST), (value_in, value_out, MOST), (query_in, query_out, 0))

    def head_copy(which, offset):
        source, target, before = arrays[which]
        peer = shifted(seq_index, offset, 1)
        return copy_to(
            source.at[:, rows_of(peer, head_width)],
            target.at[pl.ds(pl.multiple_of(before + seq_index * tokens, tokens), tokens)],
            p_send.at[which, offset],
            p_recv.at[which, offset],
            peer,
            exp_index,
        )

    def own_head_copy(which):
        source, target, before = arrays[which]
        return pltpu.make_async_copy(
            source.at[:, rows_of(seq_index, head_width)],
            target.at[pl.ds(pl.multiple_of(before + seq_index * tokens, tokens), tokens)],
            local_sem.at[1 + which],
        )

    def send_heads(which):
        own_head_copy(which).start()
        for_offsets(lambda offset: head_copy(which, offset).start())

    def wait_heads(which):
        own_head_copy(which).wait()
        for_offsets(lambda offset: head_copy(which, offset).wait_recv())

    def halo_copies(which):
        target = arrays[which][1]
        return (
            copy_to(
                target.at[pl.ds(MOST, MOST)],
                target.at[pl.ds(MOST + group, MOST)],
                h_send.at[which, 0],
                h_recv.at[which, 0],
                seq_index,
                (exp_index + 3) % 4,
            ),
            copy_to(
                target.at[pl.ds(group, MOST)],
                target.at[pl.ds(0, MOST)],
                h_send.at[which, 1],
                h_recv.at[which, 1],
                seq_index,
                (exp_index + 1) % 4,
            ),
        )

    slot = ((core * 4 + exp_index) * 4 + at_y) * 4 + at_x

    def modulation_copies(phase):
        if phase == 0:
            source, target = own_modulation, modulation_out.at[slot]
            places = [((at_y * 4 + (at_x + d) % 4) * 2 + core, exp_index) for d in (1, 2, 3)]
        elif phase == 1:
            source = modulation_out.at[rows_of(slot // 4, 4)]
            target = source
            places = [((((at_y + d) % 4) * 4 + at_x) * 2 + core, exp_index) for d in (1, 2, 3)]
        elif phase == 2:
            source = modulation_out.at[rows_of(slot // 16, 16)]
            target = source
            places = [(seq_index, (exp_index + d) % 4) for d in (1, 2, 3)]
        else:
            source = modulation_out.at[rows_of(core, 64)]
            target = source
            places = [(at_y * 8 + at_x * 2 + 1 - core, exp_index)]
        return [
            copy_to(source, target, m_send.at[phase, i], m_recv.at[phase, i], peer, other)
            for i, (peer, other) in enumerate(places)
        ]

    def send_modulation(phase):
        for copy in modulation_copies(phase):
            copy.start()

    def wait_modulation(phase):
        for copy in modulation_copies(phase):
            copy.wait_recv()

    send_heads(0)

    for_offsets(lambda offset: condition_copy(offset).wait_recv())
    load_weight.wait()
    condition = jnp.concatenate([conditions[place] for place in range(PLANE)], axis=1)
    own_modulation[...] = jnp.dot(condition, weight[...], preferred_element_type=f32).astype(bf16)
    keep = pltpu.make_async_copy(own_modulation, modulation_out.at[slot], local_sem.at[4])
    keep.start()
    send_modulation(0)
    send_heads(1)

    ids = ids_ref[...]
    lane = lax.broadcasted_iota(jnp.int32, (1, head_width), 1)

    def total(mask):
        return jnp.sum(
            jnp.sum(jnp.where(mask, 1.0, 0.0), axis=0, keepdims=True), axis=1, keepdims=True
        )

    begins = jnp.zeros((1, head_width), f32)
    ends = jnp.zeros((1, head_width), f32)
    for image in range(32):
        begins = begins + jnp.where(lane == image, total(ids < image), 0.0)
        ends = ends + jnp.where(lane == image, total(ids <= image), 0.0)
    begins = begins.astype(jnp.int32)
    ends = ends.astype(jnp.int32)
    first_token = exp_index * group

    def tag_rows(step, carry):
        rows = rows_of(step, Q_ROWS)
        shape = (Q_ROWS, head_width)
        place = lax.broadcasted_iota(jnp.int32, shape, 0) + (first_token - MOST + step * Q_ROWS)
        same = (place >= begins) & (place < ends)
        key_tags[rows, :] = jnp.where(same, 0.0, -FAR).astype(bf16)
        return carry

    def query_tag_rows(step, carry):
        rows = rows_of(step, Q_ROWS)
        shape = (Q_ROWS, head_width)
        place = lax.broadcasted_iota(jnp.int32, shape, 0) + (first_token + step * Q_ROWS)
        same = (place >= begins) & (place < ends)
        query_tags[rows, :] = jnp.where(same, 1.0, 0.0).astype(bf16)
        return carry

    lax.fori_loop(0, key_tags.shape[0] // Q_ROWS, tag_rows, 0)
    lax.fori_loop(0, group // Q_ROWS, query_tag_rows, 0)
    keep_key_tags = pltpu.make_async_copy(key_tags, key_tags_out, local_sem.at[5])
    keep_key_tags.start()
    keep_query_tags = pltpu.make_async_copy(query_tags, query_tags_out, local_sem.at[6])
    keep_query_tags.start()

    low = jnp.zeros((1, head_width), f32)
    high = jnp.zeros((1, head_width), f32)
    for block in range(group // Q_ROWS):
        line = exp_index * (group // 128) + block * (Q_ROWS // 128)
        first = ids_ref[pl.ds(line, 1), 0:1]
        last = ids_ref[pl.ds(line + Q_ROWS // 128 - 1, 1), 127:128]
        low = low + jnp.where(lane == block, total(ids < first), 0.0)
        high = high + jnp.where(lane == block, total(ids <= last), 0.0)
    low = (low.astype(jnp.int32) - first_token + MOST) & ~127
    high = high.astype(jnp.int32) - first_token + MOST
    parts = jnp.maximum((high - low + Q_ROWS - 1) >> 8, 2)
    spans_out[...] = jnp.where(
        lax.broadcasted_iota(jnp.int32, spans_out.shape, 0) == 0, low, parts
    )

    keep.wait()
    wait_modulation(0)
    send_modulation(1)
    wait_modulation(1)
    send_modulation(2)
    wait_heads(0)
    for copy in halo_copies(0):
        copy.start()
    send_heads(2)
    wait_modulation(2)
    send_modulation(3)
    wait_heads(1)
    for copy in halo_copies(1):
        copy.start()
    wait_heads(2)
    wait_modulation(3)
    keep_key_tags.wait()
    keep_query_tags.wait()
    for which in range(2):
        for copy in halo_copies(which):
            copy.wait_recv()
    for_offsets(lambda offset: condition_copy(offset).wait_send())
    for which in range(3):
        for_offsets(lambda offset: head_copy(which, offset).wait_send())
    for which in range(2):
        for copy in halo_copies(which):
            copy.wait_send()
    for phase in range(4):
        for copy in modulation_copies(phase):
            copy.wait_send()


def exchange(query_input, key_input, value_input, mod_weight, cond_columns, sample_id):
    tokens, width = query_input.shape
    head_width = width // PLANE
    group = tokens * PLANE
    extent = group + 2 * MOST
    bf16 = jnp.bfloat16
    samples = cond_columns.shape[0]
    anywhere = pl.BlockSpec(memory_space=pl.ANY)
    inside = pl.BlockSpec(memory_space=pltpu.VMEM)
    dma = pltpu.SemaphoreType.DMA
    return pl.pallas_call(
        exchange_kernel,
        out_shape=(
            jax.ShapeDtypeStruct((group, head_width), bf16),
            jax.ShapeDtypeStruct((extent, head_width), bf16),
            jax.ShapeDtypeStruct((extent, head_width), bf16),
            jax.ShapeDtypeStruct((group, head_width), bf16),
            jax.ShapeDtypeStruct((extent, head_width), bf16),
            jax.ShapeDtypeStruct((4 * PLANE, samples, mod_weight.shape[1]), bf16),
            jax.ShapeDtypeStruct((8, head_width), jnp.int32),
        ),
        in_specs=[anywhere] * 4 + [inside] * 2,
        out_specs=(anywhere,) * 6 + (inside,),
        scratch_shapes=[
            pltpu.VMEM((PLANE, samples, head_width), bf16),
            pltpu.VMEM(mod_weight.shape, bf16),
            pltpu.VMEM((samples, mod_weight.shape[1]), bf16),
            pltpu.VMEM((group, head_width), bf16),
            pltpu.VMEM((extent, head_width), bf16),
            dma((7,)),
            dma((PLANE,)),
            dma((PLANE,)),
            dma((3, PLANE)),
            dma((3, PLANE)),
            dma((2, 2)),
            dma((2, 2)),
            dma((4, 3)),
            dma((4, 3)),
        ],
        compiler_params=pltpu.CompilerParams(
            collective_id=0, has_side_effects=True, vmem_limit_bytes=60 * 2**20
        ),
        name="exchange",
    )(
        query_input,
        key_input,
        value_input,
        mod_weight,
        cond_columns,
        sample_id.reshape(-1, head_width),
    )


def experts_kernel(
    attended_ref,
    stream_in,
    modulation_in,
    w_first_in,
    w_second_in,
    tags_in,
    target_ref,
    placement_ref,
    router_ref,
    out_ref,
    stream_ref,
    modulation_ref,
    selector_ref,
    w_first,
    w_second,
    attended,
    token_mod,
    residual,
    normed,
    pick,
    unmix,
    mix,
    outgoing,
    landed,
    gathered,
    lined,
    hidden,
    far_out,
    far_in,
    side_raw,
    side_sum,
    raw_in,
    sum_in,
    held,
    own_total,
    homeward,
    back,
    router_twice,
    local_sem,
    a_send,
    a_recv,
    d_send,
    d_recv,
    z_send,
    z_recv,
    r_send,
    r_recv,
    b_send,
    b_recv,
):
    seq_index = lax.axis_index("seq")
    exp_index = lax.axis_index("exp")
    right = (exp_index + 1) % 4
    left = (exp_index + 3) % 4
    width = stream_ref.shape[1]
    tokens = stream_ref.shape[0]
    f32 = jnp.float32
    bf16 = jnp.bfloat16

    greet(seq_index, exp_index, (left, right))

    def plane_copy(source, target, send, recv, peer):
        return pltpu.make_async_remote_copy(
            src_ref=source,
            dst_ref=target,
            send_sem=send,
            recv_sem=recv,
            device_id=(peer, exp_index),
            device_id_type=MESH,
        )

    def ring_copy(source, target, send, recv, other):
        return pltpu.make_async_remote_copy(
            src_ref=source,
            dst_ref=target,
            send_sem=send,
            recv_sem=recv,
            device_id=(seq_index, other),
            device_id_type=MESH,
        )

    def attended_copy(offset):
        peer = shifted(seq_index, offset, 1)
        return plane_copy(
            attended_ref.at[rows_of(peer, tokens)],
            attended.at[seq_index],
            a_send.at[offset],
            a_recv.at[offset],
            peer,
        )

    for_offsets(lambda offset: attended_copy(offset).start())
    own_attended = pltpu.make_async_copy(
        attended_ref.at[rows_of(seq_index, tokens)], attended.at[seq_index], local_sem.at[0]
    )
    own_attended.start()
    load_mod = pltpu.make_async_copy(modulation_in, modulation_ref, local_sem.at[1])
    load_mod.start()
    load_stream = pltpu.make_async_copy(stream_in, stream_ref, local_sem.at[2])
    load_stream.start()
    load_tags = pltpu.make_async_copy(
        tags_in.at[rows_of(seq_index, tokens)], selector_ref, local_sem.at[5]
    )
    load_tags.start()
    load_first = pltpu.make_async_copy(w_first_in.at[0], w_first, local_sem.at[3])
    load_first.start()
    load_second = pltpu.make_async_copy(w_second_in.at[0], w_second, local_sem.at[4])
    load_second.start()

    count = PIECES * SLOT_ROWS
    row = lax.broadcasted_iota(jnp.int32, (count, count), 0)
    column = lax.broadcasted_iota(jnp.int32, (count, count), 1)
    by_source = ((row >> 1) & 31) * 16 + (row >> 6) * 2 + (row & 1)
    unmix[...] = jnp.where(by_source == column, 1.0, 0.0).astype(bf16)
    by_piece = ((row >> 1) & 7) * SLOT_ROWS + (row >> 4) * 2 + (row & 1)
    mix[...] = jnp.where(by_piece == column, 1.0, 0.0).astype(bf16)
    column = lax.broadcasted_iota(jnp.int32, pick.shape, 1)
    pick[...] = jnp.where(target_ref[...] == column, 1.0, 0.0).astype(bf16)

    load_mod.wait()
    load_stream.wait()

    load_tags.wait()
    samples = modulation_ref.shape[1]

    def spread_mod(step, carry):
        base = (step % 2 * 16 + step // 8) * 4 + step // 2 % 4
        whole = jnp.concatenate([modulation_ref[base + 16 * part] for part in range(4)], axis=1)
        token_mod[:, rows_of(step, 512)] = jnp.dot(
            selector_ref[:, :samples], whole, preferred_element_type=f32
        )
        return carry

    lax.fori_loop(0, 4 * width // 512, spread_mod, 0)

    double = lax.broadcasted_iota(jnp.int32, (SLOT_ROWS, samples), 0) >> 1
    twice = jnp.where(
        double == lax.broadcasted_iota(jnp.int32, (SLOT_ROWS, samples), 1), 1.0, 0.0
    ).astype(bf16)
    router_twice[...] = jnp.dot(twice, router_ref[...], preferred_element_type=f32).astype(bf16)

    own_attended.wait()
    for_offsets(lambda offset: attended_copy(offset).wait_recv())

    def norm_rows(step, carry):
        rows = rows_of(step, 16)
        heads = jnp.concatenate([attended[head, rows, :] for head in range(PLANE)], axis=1)
        value = stream_ref[rows, :].astype(f32) + token_mod[rows, :width] * heads.astype(f32)
        residual[rows, :] = value
        average = jnp.mean(value, axis=1, keepdims=True)
        centered = value - average
        variance = jnp.mean(centered * centered, axis=1, keepdims=True)
        shift = token_mod[rows, width : 2 * width]
        scale = token_mod[rows, 2 * width : 3 * width]
        normed[rows, :] = (centered * lax.rsqrt(variance + EPS) * (1.0 + scale) + shift).astype(bf16)
        return carry

    lax.fori_loop(0, tokens // 16, norm_rows, 0)

    def dispatch_copy(half, offset):
        peer = shifted(seq_index, offset, 1)
        return plane_copy(
            outgoing.at[half, rows_of(peer, 16)],
            landed.at[half, rows_of(seq_index, 16)],
            d_send.at[half, offset],
            d_recv.at[half, offset],
            peer,
        )

    for half in range(2):
        stacked = jnp.concatenate(
            [
                normed[:, half * HALF + piece * TILE : half * HALF + (piece + 1) * TILE]
                for piece in range(PIECES)
            ],
            axis=0,
        )
        outgoing[half] = jnp.dot(pick[...], stacked, preferred_element_type=f32).astype(bf16)
        for_offsets(lambda offset: dispatch_copy(half, offset).start())
        landed[half, rows_of(seq_index, 16), :] = outgoing[half, rows_of(seq_index, 16), :]

    logits = lax.dot_general(
        normed[...], router_twice[...], (((1,), (1,)), ((), ())), preferred_element_type=f32
    )
    weighted = placement_ref[...] / (1.0 + jnp.exp(-logits))
    weight_first = weighted.astype(bf16)
    weight_rest = weighted - weight_first.astype(f32)
    weight_second = weight_rest.astype(bf16)
    weight_third = (weight_rest - weight_second.astype(f32)).astype(bf16)
    weight_parts = jnp.concatenate([weight_first, weight_second, weight_third], axis=1)

    def line_up(which, half):
        lined[which * SLOT_ROWS : (which + 1) * SLOT_ROWS, half * HALF : (half + 1) * HALF] = (
            jnp.concatenate(
                [
                    gathered[which, half, piece * SLOT_ROWS : (piece + 1) * SLOT_ROWS, :]
                    for piece in range(PIECES)
                ],
                axis=1,
            )
        )

    for half in range(2):
        for_offsets(lambda offset: dispatch_copy(half, offset).wait_recv())
        gathered[0, half] = jnp.dot(
            unmix[...], landed[half], preferred_element_type=f32
        ).astype(bf16)
        if half == 0:
            own_right_0 = ring_copy(
                gathered.at[0, 0], gathered.at[2, 0], z_send.at[0], z_recv.at[0], right
            )
            own_right_0.start()
        else:
            own_left_1 = ring_copy(
                gathered.at[0, 1], gathered.at[3, 1], z_send.at[1], z_recv.at[1], left
            )
            own_left_1.start()
        line_up(0, half)
    own_right_0.wait_recv()
    on_right_0 = ring_copy(
        gathered.at[2, 0], gathered.at[1, 0], z_send.at[2], z_recv.at[2], right
    )
    on_right_0.start()
    own_left_1.wait_recv()
    on_left_1 = ring_copy(gathered.at[3, 1], gathered.at[1, 1], z_send.at[3], z_recv.at[3], left)
    on_left_1.start()
    own_right_1 = ring_copy(
        gathered.at[0, 1], gathered.at[2, 1], z_send.at[4], z_recv.at[4], right
    )
    own_right_1.start()
    own_left_0 = ring_copy(gathered.at[0, 0], gathered.at[3, 0], z_send.at[5], z_recv.at[5], left)
    own_left_0.start()
    line_up(2, 0)
    line_up(3, 1)
    load_first.wait()
    load_second.wait()

    def first_product(base):
        rows = slice(base, base + 2 * SLOT_ROWS)

        def columns_of(step, carry):
            columns = rows_of(step, 256)
            product = jnp.dot(lined[rows, :], w_first[:, columns], preferred_element_type=f32)
            hidden[rows, columns] = jax.nn.gelu(product, approximate=True).astype(bf16)
            return carry

        lax.fori_loop(0, w_first.shape[1] // 256, columns_of, 0)

    def second_product(base, half, lower, upper):
        rows = slice(base, base + 2 * SLOT_ROWS)

        def columns_of(step, carry):
            columns = rows_of(step, 256)
            product = jnp.dot(
                hidden[rows, :],
                w_second[:, rows_of(step + half * (HALF // 256), 256)],
                preferred_element_type=f32,
            )
            lower[:, columns] = product[:SLOT_ROWS].astype(lower.dtype)
            upper[:, columns] = product[SLOT_ROWS:].astype(upper.dtype)
            return carry

        lax.fori_loop(0, HALF // 256, columns_of, 0)

    on_right_0.wait_recv()
    line_up(1, 0)
    on_left_1.wait_recv()
    line_up(1, 1)
    first_product(0)
    second_product(0, 0, own_total.at[0], far_out.at[0])
    far_right = ring_copy(far_out.at[0], far_in.at[0], r_send.at[0], r_recv.at[0], right)
    far_right.start()
    second_product(0, 1, own_total.at[1], far_out.at[1])
    far_left = ring_copy(far_out.at[1], far_in.at[1], r_send.at[1], r_recv.at[1], left)
    far_left.start()
    own_right_1.wait_recv()
    line_up(2, 1)
    own_left_0.wait_recv()
    line_up(3, 0)
    first_product(2 * SLOT_ROWS)
    second_product(2 * SLOT_ROWS, 0, side_raw.at[0], held.at[0])
    raw_left = ring_copy(side_raw.at[0], raw_in.at[0], r_send.at[2], r_recv.at[2], left)
    raw_left.start()
    second_product(2 * SLOT_ROWS, 1, held.at[1], side_raw.at[1])
    raw_right = ring_copy(side_raw.at[1], raw_in.at[1], r_send.at[3], r_recv.at[3], right)
    raw_right.start()
    far_right.wait_recv()
    side_sum[0] = (held[0] + far_in[0].astype(f32)).astype(bf16)
    sum_right = ring_copy(side_sum.at[0], sum_in.at[0], r_send.at[4], r_recv.at[4], right)
    sum_right.start()
    far_left.wait_recv()
    side_sum[1] = (held[1] + far_in[1].astype(f32)).astype(bf16)
    sum_left = ring_copy(side_sum.at[1], sum_in.at[1], r_send.at[5], r_recv.at[5], left)
    sum_left.start()

    def return_copy(half, offset):
        peer = shifted(seq_index, offset, 1)
        return plane_copy(
            homeward.at[half, rows_of(peer, 16)],
            back.at[half, rows_of(seq_index, 16)],
            b_send.at[half, offset],
            b_recv.at[half, offset],
            peer,
        )

    for half, raw, summed in ((0, raw_left, sum_right), (1, raw_right, sum_left)):
        raw.wait_recv()
        summed.wait_recv()
        total = (
            own_total[half] + raw_in[half].astype(f32) + sum_in[half].astype(f32)
        ).astype(bf16)
        stacked = jnp.concatenate(
            [total[:, piece * TILE : (piece + 1) * TILE] for piece in range(PIECES)], axis=0
        )
        homeward[half] = jnp.dot(mix[...], stacked, preferred_element_type=f32).astype(bf16)
        for_offsets(lambda offset: return_copy(half, offset).start())
        back[half, rows_of(seq_index, 16), :] = homeward[half, rows_of(seq_index, 16), :]

    for half in range(2):
        for_offsets(lambda offset: return_copy(half, offset).wait_recv())
        ordered = jnp.dot(unmix[...], back[half], preferred_element_type=f32).astype(bf16)
        for piece in range(PIECES):
            rows = ordered[piece * SLOT_ROWS : (piece + 1) * SLOT_ROWS, :]
            begin = half * HALF + piece * TILE
            columns = slice(begin, begin + TILE)
            expert_sum = jnp.dot(
                weight_parts, jnp.concatenate([rows, rows, rows], axis=0), preferred_element_type=f32
            )
            gate = token_mod[:, 3 * width + begin : 3 * width + begin + TILE]
            out_ref[:, columns] = (residual[:, columns] + gate * expert_sum).astype(bf16)

    for_offsets(lambda offset: attended_copy(offset).wait_send())
    for half in range(2):
        for_offsets(lambda offset: dispatch_copy(half, offset).wait_send())
        for_offsets(lambda offset: return_copy(half, offset).wait_send())
    for copy in (
        own_right_0,
        own_left_1,
        on_right_0,
        on_left_1,
        own_right_1,
        own_left_0,
        far_right,
        far_left,
        raw_left,
        raw_right,
        sum_right,
        sum_left,
    ):
        copy.wait_send()


def feed_forward(
    attended_head, stream, modulation, expert_in, expert_out, query_tags, target, placement, router
):
    tokens, width = stream.shape
    bf16 = jnp.bfloat16
    f32 = jnp.float32
    part = expert_in.shape[2]
    block = PIECES * SLOT_ROWS
    anywhere = pl.BlockSpec(memory_space=pl.ANY)
    inside = pl.BlockSpec(memory_space=pltpu.VMEM)
    dma = pltpu.SemaphoreType.DMA
    return pl.pallas_call(
        experts_kernel,
        out_shape=jax.ShapeDtypeStruct((tokens, width), bf16),
        in_specs=[anywhere] * 6 + [inside] * 3,
        out_specs=inside,
        scratch_shapes=[
            pltpu.VMEM((tokens, width), bf16),
            pltpu.VMEM(modulation.shape, bf16),
            pltpu.VMEM((tokens, width // PLANE), bf16),
            pltpu.VMEM((width, part), bf16),
            pltpu.VMEM((part, width), bf16),
            pltpu.VMEM((PLANE, tokens, width // PLANE), bf16),
            pltpu.VMEM((tokens, 4 * width), f32),
            pltpu.VMEM((tokens, width), f32),
            pltpu.VMEM((tokens, width), bf16),
            pltpu.VMEM((block, PIECES * tokens), bf16),
            pltpu.VMEM((block, block), bf16),
            pltpu.VMEM((block, block), bf16),
            pltpu.VMEM((2, block, TILE), bf16),
            pltpu.VMEM((2, block, TILE), bf16),
            pltpu.VMEM((4, 2, block, TILE), bf16),
            pltpu.VMEM((4 * SLOT_ROWS, width), bf16),
            pltpu.VMEM((4 * SLOT_ROWS, part), bf16),
            pltpu.VMEM((2, SLOT_ROWS, HALF), bf16),
            pltpu.VMEM((2, SLOT_ROWS, HALF), bf16),
            pltpu.VMEM((2, SLOT_ROWS, HALF), bf16),
            pltpu.VMEM((2, SLOT_ROWS, HALF), bf16),
            pltpu.VMEM((2, SLOT_ROWS, HALF), bf16),
            pltpu.VMEM((2, SLOT_ROWS, HALF), bf16),
            pltpu.VMEM((2, SLOT_ROWS, HALF), f32),
            pltpu.VMEM((2, SLOT_ROWS, HALF), f32),
            pltpu.VMEM((2, block, TILE), bf16),
            pltpu.VMEM((2, block, TILE), bf16),
            pltpu.VMEM((SLOT_ROWS, width), bf16),
            dma((6,)),
            dma((PLANE,)),
            dma((PLANE,)),
            dma((2, PLANE)),
            dma((2, PLANE)),
            dma((6,)),
            dma((6,)),
            dma((6,)),
            dma((6,)),
            dma((2, PLANE)),
            dma((2, PLANE)),
        ],
        compiler_params=pltpu.CompilerParams(
            collective_id=1, has_side_effects=True, vmem_limit_bytes=58 * 2**20
        ),
        name="experts",
    )(
        attended_head,
        stream,
        modulation,
        expert_in,
        expert_out,
        query_tags,
        target,
        placement,
        router,
    )


def on_device(
    stream,
    query_input,
    key_input,
    value_input,
    sample_id,
    timestep,
    class_id,
    class_table,
    mod_weight,
    router_weight,
    expert_in,
    expert_out,
    picked,
    counts,
):
    seq_index = lax.axis_index("seq")
    tok_local, width = stream.shape
    column_count = class_table.shape[1]
    half_width = width // 2
    column = seq_index * column_count + jnp.arange(column_count, dtype=jnp.int32)
    first_half = column < half_width
    freq_index = jnp.where(first_half, column, column - half_width).astype(jnp.float32)
    frequency = jnp.exp(-math.log(10000.0) * freq_index / half_width)
    angles = timestep.astype(jnp.float32)[:, None] * frequency[None, :]
    embedded = jnp.where(first_half[None, :], jnp.cos(angles), jnp.sin(angles))
    table_rows = jnp.take(class_table, class_id, axis=0).astype(jnp.float32)
    cond_columns = jax.nn.silu(embedded + table_rows).astype(jnp.bfloat16)
    head_query, keys, values, query_tags, key_tags, modulation, spans = exchange(
        query_input, key_input, value_input, mod_weight, cond_columns, sample_id
    )
    attended_head = local_attention(spans, head_query, query_tags, keys, key_tags, values)
    slots = picked[:, 0, :]
    expert_count, slot_total = slots.shape
    live = jnp.arange(slot_total, dtype=jnp.int32)[None, :] < counts[:, 0][:, None]
    chosen = jnp.where(live, slots, -1)
    piece = jnp.arange(PIECES, dtype=jnp.int32)[None, :, None]
    target = jnp.where(live[:, None, :], slots[:, None, :] + piece * tok_local, -1).reshape(-1, 1)
    placement = (
        chosen.reshape(1, -1) == jnp.arange(tok_local, dtype=jnp.int32)[:, None]
    ).astype(jnp.float32)
    return feed_forward(
        attended_head,
        stream,
        modulation,
        expert_in,
        expert_out,
        query_tags,
        target,
        placement,
        router_weight.T,
    )


def solution(mesh):
    return jax.shard_map(
        on_device,
        mesh=mesh,
        in_specs=(
            P(("exp", "seq"), None),
            P(("exp", "seq"), None),
            P(("exp", "seq"), None),
            P(("exp", "seq"), None),
            P(),
            P(),
            P(),
            P(None, "seq"),
            P(None, ("seq", "exp")),
            P(),
            P("seq", None, "exp"),
            P("seq", "exp", None),
            P(None, ("exp", "seq"), None),
            P(None, ("exp", "seq")),
        ),
        out_specs=P(("exp", "seq"), None),
        check_vma=False,
    )
```

```python
import math

import jax
import jax.numpy as jnp
from jax import lax
from jax.experimental import pallas as pl
from jax.experimental.pallas import tpu as pltpu
from jax.sharding import PartitionSpec as P

MOST = 1024


EPS = 1e-06


Q_ROWS = 256
FAR = 32768.0


def attention_kernel(spans, q_ref, fq_ref, k_ref, fk_ref, v_ref, out_ref):
    step = pl.program_id(0)
    start = spans[0, step]
    parts = spans[1, step]
    head_width = q_ref.shape[1]
    factor = math.log2(math.e) / math.sqrt(head_width)
    most_parts = (2 * MOST + Q_ROWS) // Q_ROWS + 1

    def with_parts(number):
        span = number * Q_ROWS

        @pl.when(parts == number)
        def _():
            first = pl.multiple_of(jnp.minimum(start, k_ref.shape[0] - span), 128)
            rows = pl.ds(first, span)
            query = jnp.concatenate([q_ref[...], fq_ref[...]], axis=1)
            keys = jnp.concatenate([k_ref[rows, :], fk_ref[rows, :]], axis=1)
            scores = lax.dot_general(
                query, keys, (((1,), (1,)), ((), ())), preferred_element_type=jnp.float32
            )
            highest = jnp.max(scores, axis=1, keepdims=True)
            numer = jnp.exp2((scores - highest) * factor).astype(jnp.bfloat16)
            values = jnp.concatenate(
                [v_ref[rows, :], jnp.ones((span, head_width), jnp.bfloat16)], axis=1
            )
            total = jnp.dot(numer, values, preferred_element_type=jnp.float32)
            out_ref[...] = (total[:, :head_width] / total[:, head_width:]).astype(jnp.bfloat16)

    for number in range(2, most_parts + 1):
        with_parts(number)


def local_attention(spans, head_query, query_tags, keys, key_tags, values):
    group, head_width = head_query.shape
    extent = keys.shape[0]
    blocks = group // Q_ROWS
    whole = lambda step, spans: (0, 0)
    part = lambda step, spans: (step, 0)
    return pl.pallas_call(
        attention_kernel,
        grid_spec=pltpu.PrefetchScalarGridSpec(
            num_scalar_prefetch=1,
            grid=(blocks,),
            in_specs=[
                pl.BlockSpec((Q_ROWS, head_width), part),
                pl.BlockSpec((Q_ROWS, head_width), part),
                pl.BlockSpec((extent, head_width), whole),
                pl.BlockSpec((extent, head_width), whole),
                pl.BlockSpec((extent, head_width), whole),
            ],
            out_specs=pl.BlockSpec((Q_ROWS, head_width), part),
        ),
        out_shape=jax.ShapeDtypeStruct((group, head_width), jnp.bfloat16),
        compiler_params=pltpu.CompilerParams(vmem_limit_bytes=60 * 2**20),
        name="attention",
    )(spans, head_query, query_tags, keys, key_tags, values)


MESH = pl.DeviceIdType.MESH
PLANE = 32
TILE = 256
PIECES = 8
HALF = TILE * PIECES
SLOT_ROWS = 64


OFFSETS = sorted(range(1, PLANE), key=lambda offset: (offset * 13) % PLANE)


def greet(seq_index, exp_index, ring):
    barrier = pltpu.get_barrier_semaphore()
    for offset in OFFSETS:
        pl.semaphore_signal(
            barrier,
            inc=1,
            device_id=(seq_index ^ offset, exp_index),
            device_id_type=MESH,
        )
    for other in ring:
        pl.semaphore_signal(barrier, inc=1, device_id=(seq_index, other), device_id_type=MESH)
    pl.semaphore_wait(barrier, PLANE - 1 + len(ring))


def wait_for(part, semaphore):
    pltpu.make_async_copy(part, part, semaphore).wait()


def rows_of(number, size):
    return pl.ds(pl.multiple_of(number * size, size), size)


def exchange_kernel(
    query_in,
    key_in,
    value_in,
    weight_in,
    class_table_ref,
    class_id_ref,
    timestep_ref,
    ids_ref,
    query_out,
    key_out,
    value_out,
    query_tags_out,
    key_tags_out,
    modulation_out,
    spans_out,
    own_condition,
    conditions,
    weight,
    own_modulation,
    query_tags,
    key_tags,
    local_sem,
    c_sem,
    p_send,
    p_recv,
    h_send,
    h_recv,
    m_send,
    m_recv,
):
    seq_index = lax.axis_index("seq")
    exp_index = lax.axis_index("exp")
    tokens = query_in.shape[0]
    group, head_width = query_out.shape
    at_y = seq_index // 8
    at_x = seq_index // 2 % 4
    core = seq_index % 2
    f32 = jnp.float32
    bf16 = jnp.bfloat16

    greet(seq_index, exp_index, [(exp_index + step) % 4 for step in (1, 2, 3)])

    def copy_to(source, target, send, recv, peer, other):
        return pltpu.make_async_remote_copy(
            src_ref=source,
            dst_ref=target,
            send_sem=send,
            recv_sem=recv,
            device_id=(peer, other),
            device_id_type=MESH,
        )

    arrays = ((key_in, key_out, MOST), (value_in, value_out, MOST), (query_in, query_out, 0))

    def send_heads(which):
        source, target, before = arrays[which]
        place = target.at[pl.ds(pl.multiple_of(before + seq_index * tokens, tokens), tokens)]
        for offset in OFFSETS:
            peer = seq_index ^ offset
            copy_to(
                source.at[:, rows_of(peer, head_width)],
                place,
                p_send.at[which],
                p_recv.at[which],
                peer,
                exp_index,
            ).start()
        pltpu.make_async_copy(
            source.at[:, rows_of(seq_index, head_width)], place, p_recv.at[which]
        ).start()

    def wait_heads(which):
        _, target, before = arrays[which]
        wait_for(target.at[pl.ds(before, group)], p_recv.at[which])

    def halo_copies(which):
        target = arrays[which][1]
        return (
            copy_to(
                target.at[pl.ds(MOST, MOST)],
                target.at[pl.ds(MOST + group, MOST)],
                h_send.at[which, 0],
                h_recv.at[which, 0],
                seq_index,
                (exp_index + 3) % 4,
            ),
            copy_to(
                target.at[pl.ds(group, MOST)],
                target.at[pl.ds(0, MOST)],
                h_send.at[which, 1],
                h_recv.at[which, 1],
                seq_index,
                (exp_index + 1) % 4,
            ),
        )

    slot = ((core * 4 + exp_index) * 4 + at_y) * 4 + at_x

    def modulation_copies(phase):
        if phase == 0:
            source, target = own_modulation, modulation_out.at[slot]
            places = [((at_y * 4 + (at_x + d) % 4) * 2 + core, exp_index) for d in (1, 2, 3)]
        elif phase == 1:
            source = modulation_out.at[rows_of(slot // 4, 4)]
            target = source
            places = [((((at_y + d) % 4) * 4 + at_x) * 2 + core, exp_index) for d in (1, 2, 3)]
        elif phase == 2:
            source = modulation_out.at[rows_of(slot // 16, 16)]
            target = source
            places = [(seq_index, (exp_index + d) % 4) for d in (1, 2, 3)]
        else:
            source = modulation_out.at[rows_of(core, 64)]
            target = source
            places = [(at_y * 8 + at_x * 2 + 1 - core, exp_index)]
        return [
            copy_to(source, target, m_send.at[phase, i], m_recv.at[phase, i], peer, other)
            for i, (peer, other) in enumerate(places)
        ]

    def send_modulation(phase):
        for copy in modulation_copies(phase):
            copy.start()

    def wait_modulation(phase):
        for copy in modulation_copies(phase):
            copy.wait_recv()

    send_heads(0)
    load_weight = pltpu.make_async_copy(weight_in, weight, local_sem.at[0])
    load_weight.start()

    samples = timestep_ref.shape[1]
    diagonal = lax.broadcasted_iota(jnp.int32, (samples, samples), 0) == lax.broadcasted_iota(
        jnp.int32, (samples, samples), 1
    )

    def upright(row):
        return jnp.sum(jnp.where(diagonal, row.astype(f32), 0.0), axis=1, keepdims=True)

    classes = class_table_ref.shape[0]
    chosen_class = jnp.where(
        lax.broadcasted_iota(jnp.int32, (samples, classes), 1).astype(f32)
        == upright(class_id_ref[...]),
        1.0,
        0.0,
    ).astype(bf16)
    table_rows = jnp.dot(chosen_class, class_table_ref[...], preferred_element_type=f32)
    half_columns = PLANE * head_width // 2
    column = seq_index * head_width + lax.broadcasted_iota(jnp.int32, (1, head_width), 1)
    freq_index = jnp.where(column < half_columns, column, column - half_columns).astype(f32)
    frequency = jnp.exp(-math.log(10000.0) * freq_index / half_columns)
    angles = upright(timestep_ref[...]) * frequency
    embedded = jnp.where(column < half_columns, jnp.cos(angles), jnp.sin(angles))
    value = embedded + table_rows
    own_condition[...] = (value / (1.0 + jnp.exp(-value))).astype(bf16)

    for offset in OFFSETS:
        copy_to(
            own_condition,
            conditions.at[seq_index],
            c_sem.at[0],
            c_sem.at[1],
            seq_index ^ offset,
            exp_index,
        ).start()
    pltpu.make_async_copy(own_condition, conditions.at[seq_index], c_sem.at[1]).start()
    wait_for(conditions, c_sem.at[1])
    load_weight.wait()
    condition = jnp.concatenate([conditions[place] for place in range(PLANE)], axis=1)
    own_modulation[...] = jnp.dot(condition, weight[...], preferred_element_type=f32).astype(bf16)
    keep = pltpu.make_async_copy(own_modulation, modulation_out.at[slot], local_sem.at[4])
    keep.start()
    send_modulation(0)
    send_heads(1)

    ids = ids_ref[...]
    lane = lax.broadcasted_iota(jnp.int32, (1, head_width), 1)

    def total(mask):
        return jnp.sum(
            jnp.sum(jnp.where(mask, 1.0, 0.0), axis=0, keepdims=True), axis=1, keepdims=True
        )

    begins = jnp.zeros((1, head_width), f32)
    ends = jnp.zeros((1, head_width), f32)
    for image in range(32):
        begins = begins + jnp.where(lane == image, total(ids < image), 0.0)
        ends = ends + jnp.where(lane == image, total(ids <= image), 0.0)
    begins = begins.astype(jnp.int32)
    ends = ends.astype(jnp.int32)
    first_token = exp_index * group

    def tag_rows(step, carry):
        rows = rows_of(step, Q_ROWS)
        shape = (Q_ROWS, head_width)
        place = lax.broadcasted_iota(jnp.int32, shape, 0) + (first_token - MOST + step * Q_ROWS)
        same = (place >= begins) & (place < ends)
        key_tags[rows, :] = jnp.where(same, 0.0, -FAR).astype(bf16)
        return carry

    def query_tag_rows(step, carry):
        rows = rows_of(step, Q_ROWS)
        shape = (Q_ROWS, head_width)
        place = lax.broadcasted_iota(jnp.int32, shape, 0) + (first_token + step * Q_ROWS)
        same = (place >= begins) & (place < ends)
        query_tags[rows, :] = jnp.where(same, 1.0, 0.0).astype(bf16)
        return carry

    lax.fori_loop(0, key_tags.shape[0] // Q_ROWS, tag_rows, 0)
    lax.fori_loop(0, group // Q_ROWS, query_tag_rows, 0)
    keep_key_tags = pltpu.make_async_copy(key_tags, key_tags_out, local_sem.at[5])
    keep_key_tags.start()
    keep_query_tags = pltpu.make_async_copy(query_tags, query_tags_out, local_sem.at[6])
    keep_query_tags.start()

    low = jnp.zeros((1, head_width), f32)
    high = jnp.zeros((1, head_width), f32)
    for block in range(group // Q_ROWS):
        line = exp_index * (group // 128) + block * (Q_ROWS // 128)
        first = ids_ref[pl.ds(line, 1), 0:1]
        last = ids_ref[pl.ds(line + Q_ROWS // 128 - 1, 1), 127:128]
        low = low + jnp.where(lane == block, total(ids < first), 0.0)
        high = high + jnp.where(lane == block, total(ids <= last), 0.0)
    low = (low.astype(jnp.int32) - first_token + MOST) & ~127
    high = high.astype(jnp.int32) - first_token + MOST
    parts = jnp.maximum((high - low + Q_ROWS - 1) >> 8, 2)
    spans_out[...] = jnp.where(
        lax.broadcasted_iota(jnp.int32, spans_out.shape, 0) == 0, low, parts
    )

    keep.wait()
    wait_modulation(0)
    send_modulation(1)
    wait_modulation(1)
    send_modulation(2)
    wait_heads(0)
    for copy in halo_copies(0):
        copy.start()
    send_heads(2)
    wait_modulation(2)
    send_modulation(3)
    wait_heads(1)
    for copy in halo_copies(1):
        copy.start()
    wait_heads(2)
    wait_modulation(3)
    keep_key_tags.wait()
    keep_query_tags.wait()
    for which in range(2):
        for copy in halo_copies(which):
            copy.wait_recv()
    wait_for(conditions.at[pl.ds(0, PLANE - 1)], c_sem.at[0])
    for which in range(3):
        wait_for(query_out.at[pl.ds(0, group - tokens)], p_send.at[which])
    for which in range(2):
        for copy in halo_copies(which):
            copy.wait_send()
    for phase in range(4):
        for copy in modulation_copies(phase):
            copy.wait_send()


def exchange(
    query_input, key_input, value_input, mod_weight, class_table, class_id, timestep, sample_id
):
    tokens, width = query_input.shape
    head_width = width // PLANE
    group = tokens * PLANE
    extent = group + 2 * MOST
    bf16 = jnp.bfloat16
    samples = class_id.shape[0]
    anywhere = pl.BlockSpec(memory_space=pl.ANY)
    inside = pl.BlockSpec(memory_space=pltpu.VMEM)
    dma = pltpu.SemaphoreType.DMA
    return pl.pallas_call(
        exchange_kernel,
        out_shape=(
            jax.ShapeDtypeStruct((group, head_width), bf16),
            jax.ShapeDtypeStruct((extent, head_width), bf16),
            jax.ShapeDtypeStruct((extent, head_width), bf16),
            jax.ShapeDtypeStruct((group, head_width), bf16),
            jax.ShapeDtypeStruct((extent, head_width), bf16),
            jax.ShapeDtypeStruct((4 * PLANE, samples, mod_weight.shape[1]), bf16),
            jax.ShapeDtypeStruct((8, head_width), jnp.int32),
        ),
        in_specs=[anywhere] * 4 + [inside] * 4,
        out_specs=(anywhere,) * 6 + (inside,),
        scratch_shapes=[
            pltpu.VMEM((samples, head_width), bf16),
            pltpu.VMEM((PLANE, samples, head_width), bf16),
            pltpu.VMEM(mod_weight.shape, bf16),
            pltpu.VMEM((samples, mod_weight.shape[1]), bf16),
            pltpu.VMEM((group, head_width), bf16),
            pltpu.VMEM((extent, head_width), bf16),
            dma((7,)),
            dma((2,)),
            dma((3,)),
            dma((3,)),
            dma((2, 2)),
            dma((2, 2)),
            dma((4, 3)),
            dma((4, 3)),
        ],
        compiler_params=pltpu.CompilerParams(
            collective_id=0, has_side_effects=True, vmem_limit_bytes=60 * 2**20
        ),
        name="exchange",
    )(
        query_input,
        key_input,
        value_input,
        mod_weight,
        class_table,
        class_id.reshape(1, -1),
        timestep.reshape(1, -1),
        sample_id.reshape(-1, head_width),
    )


def experts_kernel(
    attended_ref,
    stream_in,
    modulation_in,
    w_first_in,
    w_second_in,
    tags_in,
    picks_ref,
    used_ref,
    router_ref,
    out_ref,
    stream_ref,
    modulation_ref,
    selector_ref,
    w_first,
    w_second,
    attended,
    token_mod,
    residual,
    normed,
    pick,
    unmix,
    mix,
    outgoing,
    landed,
    gathered,
    lined,
    hidden,
    far_out,
    far_in,
    side_raw,
    side_sum,
    raw_in,
    sum_in,
    held,
    own_total,
    homeward,
    back,
    router_twice,
    local_sem,
    a_sem,
    d_sem,
    z_send,
    z_recv,
    r_send,
    r_recv,
    b_sem,
):
    seq_index = lax.axis_index("seq")
    exp_index = lax.axis_index("exp")
    right = (exp_index + 1) % 4
    left = (exp_index + 3) % 4
    width = stream_ref.shape[1]
    tokens = stream_ref.shape[0]
    f32 = jnp.float32
    bf16 = jnp.bfloat16

    greet(seq_index, exp_index, (left, right))

    def plane_copy(source, target, send, recv, peer):
        return pltpu.make_async_remote_copy(
            src_ref=source,
            dst_ref=target,
            send_sem=send,
            recv_sem=recv,
            device_id=(peer, exp_index),
            device_id_type=MESH,
        )

    def ring_copy(source, target, send, recv, other):
        return pltpu.make_async_remote_copy(
            src_ref=source,
            dst_ref=target,
            send_sem=send,
            recv_sem=recv,
            device_id=(seq_index, other),
            device_id_type=MESH,
        )

    for offset in OFFSETS:
        peer = seq_index ^ offset
        plane_copy(
            attended_ref.at[rows_of(peer, tokens)],
            attended.at[seq_index],
            a_sem.at[0],
            a_sem.at[1],
            peer,
        ).start()
    pltpu.make_async_copy(
        attended_ref.at[rows_of(seq_index, tokens)], attended.at[seq_index], a_sem.at[1]
    ).start()
    load_mod = pltpu.make_async_copy(modulation_in, modulation_ref, local_sem.at[1])
    load_mod.start()
    load_stream = pltpu.make_async_copy(stream_in, stream_ref, local_sem.at[2])
    load_stream.start()
    load_tags = pltpu.make_async_copy(
        tags_in.at[rows_of(seq_index, tokens)], selector_ref, local_sem.at[5]
    )
    load_tags.start()
    load_first = pltpu.make_async_copy(w_first_in.at[0], w_first, local_sem.at[3])
    load_first.start()
    load_second = pltpu.make_async_copy(w_second_in.at[0], w_second, local_sem.at[4])
    load_second.start()

    count = PIECES * SLOT_ROWS
    row = lax.broadcasted_iota(jnp.int32, (count, count), 0)
    column = lax.broadcasted_iota(jnp.int32, (count, count), 1)
    by_source = (row & 31) * 16 + (row >> 6) * 2 + ((row >> 5) & 1)
    unmix[...] = jnp.where(by_source == column, 1.0, 0.0).astype(bf16)
    by_piece = ((row >> 1) & 7) * SLOT_ROWS + (row & 1) * PLANE + (row >> 4)
    mix[...] = jnp.where(by_piece == column, 1.0, 0.0).astype(bf16)
    column = lax.broadcasted_iota(jnp.int32, pick.shape, 1)
    used = used_ref[...]
    chosen = jnp.concatenate(
        [
            jnp.where(used > 0, picks_ref[0:1, :], -1),
            jnp.where(used > 1, picks_ref[1:2, :], -1),
        ],
        axis=1,
    ).astype(f32)
    row = lax.broadcasted_iota(jnp.int32, (count, SLOT_ROWS), 0)
    slot = lax.broadcasted_iota(jnp.int32, (count, SLOT_ROWS), 1)
    mine = slot == (row & 1) * PLANE + (row >> 4)
    token = jnp.sum(jnp.where(mine, chosen, 0.0), axis=1, keepdims=True)
    piece = (lax.broadcasted_iota(jnp.int32, (count, 1), 0) >> 1) & 7
    target = jnp.where(token < 0.0, -1.0, token + (piece * tokens).astype(f32))
    pick[...] = jnp.where(column.astype(f32) == target, 1.0, 0.0).astype(bf16)

    load_mod.wait()
    load_stream.wait()

    load_tags.wait()
    samples = modulation_ref.shape[1]

    def spread_mod(step, carry):
        base = (step % 2 * 16 + step // 8) * 4 + step // 2 % 4
        whole = jnp.concatenate([modulation_ref[base + 16 * part] for part in range(4)], axis=1)
        token_mod[:, rows_of(step, 512)] = jnp.dot(
            selector_ref[:, :samples], whole, preferred_element_type=f32
        )
        return carry

    lax.fori_loop(0, 3 * width // 512, spread_mod, 0)

    double = lax.broadcasted_iota(jnp.int32, (SLOT_ROWS, samples), 0) & 31
    twice = jnp.where(
        double == lax.broadcasted_iota(jnp.int32, (SLOT_ROWS, samples), 1), 1.0, 0.0
    ).astype(bf16)
    router_twice[...] = jnp.dot(twice, router_ref[...], preferred_element_type=f32).astype(bf16)

    wait_for(attended, a_sem.at[1])

    def norm_rows(step, carry):
        rows = rows_of(step, 16)
        heads = jnp.concatenate([attended[head, rows, :] for head in range(PLANE)], axis=1)
        value = stream_ref[rows, :].astype(f32) + token_mod[rows, :width] * heads.astype(f32)
        residual[rows, :] = value
        average = jnp.mean(value, axis=1, keepdims=True)
        centered = value - average
        variance = jnp.mean(centered * centered, axis=1, keepdims=True)
        shift = token_mod[rows, width : 2 * width]
        scale = token_mod[rows, 2 * width : 3 * width]
        normed[rows, :] = (centered * lax.rsqrt(variance + EPS) * (1.0 + scale) + shift).astype(bf16)
        return carry

    lax.fori_loop(0, tokens // 16, norm_rows, 0)

    def plane_send(source, target, sems, half):
        place = target.at[half, rows_of(seq_index, 16)]
        for offset in OFFSETS:
            peer = seq_index ^ offset
            plane_copy(
                source.at[half, rows_of(peer, 16)], place, sems.at[half, 0], sems.at[half, 1], peer
            ).start()
        pltpu.make_async_copy(
            source.at[half, rows_of(seq_index, 16)], place, sems.at[half, 1]
        ).start()

    for half in range(2):
        stacked = jnp.concatenate(
            [
                normed[:, half * HALF + piece * TILE : half * HALF + (piece + 1) * TILE]
                for piece in range(PIECES)
            ],
            axis=0,
        )
        outgoing[half] = jnp.dot(pick[...], stacked, preferred_element_type=f32).astype(bf16)
        plane_send(outgoing, landed, d_sem, half)

    logits = lax.dot_general(
        normed[...], router_twice[...], (((1,), (1,)), ((), ())), preferred_element_type=f32
    )
    place = lax.broadcasted_iota(jnp.int32, (tokens, SLOT_ROWS), 0).astype(f32) == chosen
    weighted = jnp.where(place, 1.0 / (1.0 + jnp.exp(-logits)), 0.0)
    lax.fori_loop(3 * width // 512, 4 * width // 512, spread_mod, 0)
    weight_first = weighted.astype(bf16)
    weight_rest = weighted - weight_first.astype(f32)
    weight_second = weight_rest.astype(bf16)
    weight_third = (weight_rest - weight_second.astype(f32)).astype(bf16)
    weight_parts = jnp.concatenate([weight_first, weight_second, weight_third], axis=1)

    def line_up(which, half):
        lined[which * SLOT_ROWS : (which + 1) * SLOT_ROWS, half * HALF : (half + 1) * HALF] = (
            jnp.concatenate(
                [
                    gathered[which, half, piece * SLOT_ROWS : (piece + 1) * SLOT_ROWS, :]
                    for piece in range(PIECES)
                ],
                axis=1,
            )
        )

    for half in range(2):
        wait_for(landed.at[half], d_sem.at[half, 1])
        gathered[0, half] = jnp.dot(
            unmix[...], landed[half], preferred_element_type=f32
        ).astype(bf16)
        if half == 0:
            own_right_0 = ring_copy(
                gathered.at[0, 0], gathered.at[2, 0], z_send.at[0], z_recv.at[0], right
            )
            own_right_0.start()
        else:
            own_left_1 = ring_copy(
                gathered.at[0, 1], gathered.at[3, 1], z_send.at[1], z_recv.at[1], left
            )
            own_left_1.start()
        line_up(0, half)
    own_right_0.wait_recv()
    on_right_0 = ring_copy(
        gathered.at[2, 0], gathered.at[1, 0], z_send.at[2], z_recv.at[2], right
    )
    on_right_0.start()
    own_left_1.wait_recv()
    on_left_1 = ring_copy(gathered.at[3, 1], gathered.at[1, 1], z_send.at[3], z_recv.at[3], left)
    on_left_1.start()
    own_right_1 = ring_copy(
        gathered.at[0, 1], gathered.at[2, 1], z_send.at[4], z_recv.at[4], right
    )
    own_right_1.start()
    own_left_0 = ring_copy(gathered.at[0, 0], gathered.at[3, 0], z_send.at[5], z_recv.at[5], left)
    own_left_0.start()
    line_up(2, 0)
    line_up(3, 1)
    load_first.wait()
    load_second.wait()

    def first_product(base):
        rows = slice(base, base + 2 * SLOT_ROWS)

        def columns_of(step, carry):
            columns = rows_of(step, 256)
            product = jnp.dot(lined[rows, :], w_first[:, columns], preferred_element_type=f32)
            hidden[rows, columns] = jax.nn.gelu(product, approximate=True).astype(bf16)
            return carry

        lax.fori_loop(0, w_first.shape[1] // 256, columns_of, 0)

    def second_product(base, half, lower, upper):
        rows = slice(base, base + 2 * SLOT_ROWS)

        def columns_of(step, carry):
            columns = rows_of(step, 256)
            product = jnp.dot(
                hidden[rows, :],
                w_second[:, rows_of(step + half * (HALF // 256), 256)],
                preferred_element_type=f32,
            )
            lower[:, columns] = product[:SLOT_ROWS].astype(lower.dtype)
            upper[:, columns] = product[SLOT_ROWS:].astype(upper.dtype)
            return carry

        lax.fori_loop(0, HALF // 256, columns_of, 0)

    on_right_0.wait_recv()
    line_up(1, 0)
    on_left_1.wait_recv()
    line_up(1, 1)
    first_product(0)
    second_product(0, 0, own_total.at[0], far_out.at[0])
    far_right = ring_copy(far_out.at[0], far_in.at[0], r_send.at[0], r_recv.at[0], right)
    far_right.start()
    second_product(0, 1, own_total.at[1], far_out.at[1])
    far_left = ring_copy(far_out.at[1], far_in.at[1], r_send.at[1], r_recv.at[1], left)
    far_left.start()
    own_right_1.wait_recv()
    line_up(2, 1)
    own_left_0.wait_recv()
    line_up(3, 0)
    first_product(2 * SLOT_ROWS)
    second_product(2 * SLOT_ROWS, 0, side_raw.at[0], held.at[0])
    raw_left = ring_copy(side_raw.at[0], raw_in.at[0], r_send.at[2], r_recv.at[2], left)
    raw_left.start()
    second_product(2 * SLOT_ROWS, 1, held.at[1], side_raw.at[1])
    raw_right = ring_copy(side_raw.at[1], raw_in.at[1], r_send.at[3], r_recv.at[3], right)
    raw_right.start()
    far_right.wait_recv()
    side_sum[0] = (held[0] + far_in[0].astype(f32)).astype(bf16)
    sum_right = ring_copy(side_sum.at[0], sum_in.at[0], r_send.at[4], r_recv.at[4], right)
    sum_right.start()
    far_left.wait_recv()
    side_sum[1] = (held[1] + far_in[1].astype(f32)).astype(bf16)
    sum_left = ring_copy(side_sum.at[1], sum_in.at[1], r_send.at[5], r_recv.at[5], left)
    sum_left.start()

    for half, raw, summed in ((0, raw_left, sum_right), (1, raw_right, sum_left)):
        raw.wait_recv()
        summed.wait_recv()
        total = (
            own_total[half] + raw_in[half].astype(f32) + sum_in[half].astype(f32)
        ).astype(bf16)
        stacked = jnp.concatenate(
            [total[:, piece * TILE : (piece + 1) * TILE] for piece in range(PIECES)], axis=0
        )
        homeward[half] = jnp.dot(mix[...], stacked, preferred_element_type=f32).astype(bf16)
        plane_send(homeward, back, b_sem, half)

    for half in range(2):
        wait_for(back.at[half], b_sem.at[half, 1])
        ordered = jnp.dot(unmix[...], back[half], preferred_element_type=f32).astype(bf16)
        for piece in range(PIECES):
            rows = ordered[piece * SLOT_ROWS : (piece + 1) * SLOT_ROWS, :]
            begin = half * HALF + piece * TILE
            columns = slice(begin, begin + TILE)
            expert_sum = jnp.dot(
                weight_parts, jnp.concatenate([rows, rows, rows], axis=0), preferred_element_type=f32
            )
            gate = token_mod[:, 3 * width + begin : 3 * width + begin + TILE]
            out_ref[:, columns] = (residual[:, columns] + gate * expert_sum).astype(bf16)

    wait_for(attended.at[pl.ds(0, PLANE - 1)], a_sem.at[0])
    for half in range(2):
        wait_for(landed.at[half, pl.ds(0, 16 * (PLANE - 1))], d_sem.at[half, 0])
        wait_for(back.at[half, pl.ds(0, 16 * (PLANE - 1))], b_sem.at[half, 0])
    for copy in (
        own_right_0,
        own_left_1,
        on_right_0,
        on_left_1,
        own_right_1,
        own_left_0,
        far_right,
        far_left,
        raw_left,
        raw_right,
        sum_right,
        sum_left,
    ):
        copy.wait_send()


def feed_forward(
    attended_head, stream, modulation, expert_in, expert_out, query_tags, picks, used, router
):
    tokens, width = stream.shape
    bf16 = jnp.bfloat16
    f32 = jnp.float32
    part = expert_in.shape[2]
    block = PIECES * SLOT_ROWS
    anywhere = pl.BlockSpec(memory_space=pl.ANY)
    inside = pl.BlockSpec(memory_space=pltpu.VMEM)
    dma = pltpu.SemaphoreType.DMA
    return pl.pallas_call(
        experts_kernel,
        out_shape=jax.ShapeDtypeStruct((tokens, width), bf16),
        in_specs=[anywhere] * 6 + [inside] * 3,
        out_specs=inside,
        scratch_shapes=[
            pltpu.VMEM((tokens, width), bf16),
            pltpu.VMEM(modulation.shape, bf16),
            pltpu.VMEM((tokens, width // PLANE), bf16),
            pltpu.VMEM((width, part), bf16),
            pltpu.VMEM((part, width), bf16),
            pltpu.VMEM((PLANE, tokens, width // PLANE), bf16),
            pltpu.VMEM((tokens, 4 * width), f32),
            pltpu.VMEM((tokens, width), f32),
            pltpu.VMEM((tokens, width), bf16),
            pltpu.VMEM((block, PIECES * tokens), bf16),
            pltpu.VMEM((block, block), bf16),
            pltpu.VMEM((block, block), bf16),
            pltpu.VMEM((2, block, TILE), bf16),
            pltpu.VMEM((2, block, TILE), bf16),
            pltpu.VMEM((4, 2, block, TILE), bf16),
            pltpu.VMEM((4 * SLOT_ROWS, width), bf16),
            pltpu.VMEM((4 * SLOT_ROWS, part), bf16),
            pltpu.VMEM((2, SLOT_ROWS, HALF), bf16),
            pltpu.VMEM((2, SLOT_ROWS, HALF), bf16),
            pltpu.VMEM((2, SLOT_ROWS, HALF), bf16),
            pltpu.VMEM((2, SLOT_ROWS, HALF), bf16),
            pltpu.VMEM((2, SLOT_ROWS, HALF), bf16),
            pltpu.VMEM((2, SLOT_ROWS, HALF), bf16),
            pltpu.VMEM((2, SLOT_ROWS, HALF), f32),
            pltpu.VMEM((2, SLOT_ROWS, HALF), f32),
            pltpu.VMEM((2, block, TILE), bf16),
            pltpu.VMEM((2, block, TILE), bf16),
            pltpu.VMEM((SLOT_ROWS, width), bf16),
            dma((6,)),
            dma((2,)),
            dma((2, 2)),
            dma((6,)),
            dma((6,)),
            dma((6,)),
            dma((6,)),
            dma((2, 2)),
        ],
        compiler_params=pltpu.CompilerParams(
            collective_id=1, has_side_effects=True, vmem_limit_bytes=58 * 2**20
        ),
        name="experts",
    )(
        attended_head,
        stream,
        modulation,
        expert_in,
        expert_out,
        query_tags,
        picks,
        used,
        router,
    )


def on_device(
    stream,
    query_input,
    key_input,
    value_input,
    sample_id,
    timestep,
    class_id,
    class_table,
    mod_weight,
    router_weight,
    expert_in,
    expert_out,
    picked,
    counts,
):
    head_query, keys, values, query_tags, key_tags, modulation, spans = exchange(
        query_input,
        key_input,
        value_input,
        mod_weight,
        class_table,
        class_id,
        timestep,
        sample_id,
    )
    attended_head = local_attention(spans, head_query, query_tags, keys, key_tags, values)
    return feed_forward(
        attended_head,
        stream,
        modulation,
        expert_in,
        expert_out,
        query_tags,
        picked[:, 0, :].T,
        counts.T,
        router_weight.T,
    )


def solution(mesh):
    return jax.shard_map(
        on_device,
        mesh=mesh,
        in_specs=(
            P(("exp", "seq"), None),
            P(("exp", "seq"), None),
            P(("exp", "seq"), None),
            P(("exp", "seq"), None),
            P(),
            P(),
            P(),
            P(None, "seq"),
            P(None, ("seq", "exp")),
            P(),
            P("seq", None, "exp"),
            P("seq", "exp", None),
            P(None, ("exp", "seq"), None),
            P(None, ("exp", "seq")),
        ),
        out_specs=P(("exp", "seq"), None),
        check_vma=False,
    )
```

```python
import math

import jax
import jax.numpy as jnp
from jax import lax
from jax.experimental import pallas as pl
from jax.experimental.pallas import tpu as pltpu
from jax.sharding import PartitionSpec as P

MOST = 1024


EPS = 1e-06


Q_ROWS = 512
KEY_STEP = 256
FAR = 32768.0


def attention_kernel(spans, q_ref, fq_ref, k_ref, fk_ref, v_ref, out_ref):
    step = pl.program_id(0)
    start = spans[0, step]
    parts = spans[1, step]
    head_width = q_ref.shape[1]
    factor = math.log2(math.e) / math.sqrt(head_width)
    least_parts = Q_ROWS // KEY_STEP
    most_parts = (2 * MOST + Q_ROWS) // KEY_STEP + 1

    def with_parts(number):
        span = number * KEY_STEP

        @pl.when(parts == number)
        def _():
            first = pl.multiple_of(jnp.minimum(start, k_ref.shape[0] - span), 128)
            rows = pl.ds(first, span)
            keys = jnp.concatenate([k_ref[rows, :], fk_ref[rows, :]], axis=1)
            values = jnp.concatenate(
                [v_ref[rows, :], jnp.ones((span, head_width), jnp.bfloat16)], axis=1
            )
            for line in range(0, Q_ROWS, KEY_STEP):
                lines = slice(line, line + KEY_STEP)
                query = jnp.concatenate([q_ref[lines, :], fq_ref[lines, :]], axis=1)
                scores = lax.dot_general(
                    query, keys, (((1,), (1,)), ((), ())), preferred_element_type=jnp.float32
                )
                highest = jnp.max(scores, axis=1, keepdims=True)
                numer = jnp.exp2((scores - highest) * factor).astype(jnp.bfloat16)
                total = jnp.dot(numer, values, preferred_element_type=jnp.float32)
                out_ref[lines, :] = (total[:, :head_width] / total[:, head_width:]).astype(
                    jnp.bfloat16
                )

    for number in range(least_parts, most_parts + 1):
        with_parts(number)


def local_attention(spans, head_query, query_tags, keys, key_tags, values):
    group, head_width = head_query.shape
    extent = keys.shape[0]
    blocks = group // Q_ROWS
    whole = lambda step, spans: (0, 0)
    part = lambda step, spans: (step, 0)
    return pl.pallas_call(
        attention_kernel,
        grid_spec=pltpu.PrefetchScalarGridSpec(
            num_scalar_prefetch=1,
            grid=(blocks,),
            in_specs=[
                pl.BlockSpec((Q_ROWS, head_width), part),
                pl.BlockSpec((Q_ROWS, head_width), part),
                pl.BlockSpec((extent, head_width), whole),
                pl.BlockSpec((extent, head_width), whole),
                pl.BlockSpec((extent, head_width), whole),
            ],
            out_specs=pl.BlockSpec((Q_ROWS, head_width), part),
        ),
        out_shape=jax.ShapeDtypeStruct((group, head_width), jnp.bfloat16),
        compiler_params=pltpu.CompilerParams(vmem_limit_bytes=60 * 2**20),
        name="attention",
    )(spans, head_query, query_tags, keys, key_tags, values)


MESH = pl.DeviceIdType.MESH
PLANE = 32
TILE = 256
PIECES = 8
HALF = TILE * PIECES
SLOT_ROWS = 64


OFFSETS = sorted(range(1, PLANE), key=lambda offset: (offset * 13) % PLANE)


def greet(seq_index, exp_index, ring):
    barrier = pltpu.get_barrier_semaphore()
    for offset in OFFSETS:
        pl.semaphore_signal(
            barrier,
            inc=1,
            device_id=(seq_index ^ offset, exp_index),
            device_id_type=MESH,
        )
    for other in ring:
        pl.semaphore_signal(barrier, inc=1, device_id=(seq_index, other), device_id_type=MESH)
    pl.semaphore_wait(barrier, PLANE - 1 + len(ring))


def wait_for(part, semaphore):
    pltpu.make_async_copy(part, part, semaphore).wait()


def rows_of(number, size):
    return pl.ds(pl.multiple_of(number * size, size), size)


def exchange_kernel(
    query_in,
    key_in,
    value_in,
    weight_in,
    class_table_ref,
    class_id_ref,
    timestep_ref,
    ids_ref,
    query_out,
    key_out,
    value_out,
    query_tags_out,
    key_tags_out,
    modulation_out,
    spans_out,
    own_condition,
    conditions,
    weight,
    own_modulation,
    query_tags,
    key_tags,
    local_sem,
    c_sem,
    p_send,
    p_recv,
    h_send,
    h_recv,
    m_send,
    m_recv,
):
    seq_index = lax.axis_index("seq")
    exp_index = lax.axis_index("exp")
    tokens = query_in.shape[0]
    group, head_width = query_out.shape
    at_y = seq_index // 8
    at_x = seq_index // 2 % 4
    core = seq_index % 2
    f32 = jnp.float32
    bf16 = jnp.bfloat16

    greet(seq_index, exp_index, [(exp_index + step) % 4 for step in (1, 2, 3)])

    def copy_to(source, target, send, recv, peer, other):
        return pltpu.make_async_remote_copy(
            src_ref=source,
            dst_ref=target,
            send_sem=send,
            recv_sem=recv,
            device_id=(peer, other),
            device_id_type=MESH,
        )

    arrays = ((key_in, key_out, MOST), (value_in, value_out, MOST), (query_in, query_out, 0))

    def send_heads(which, part):
        source, target, before = arrays[which]
        place = target.at[pl.ds(pl.multiple_of(before + seq_index * tokens, tokens), tokens)]
        for offset in OFFSETS[part::2]:
            peer = seq_index ^ offset
            copy_to(
                source.at[:, rows_of(peer, head_width)],
                place,
                p_send.at[which],
                p_recv.at[which],
                peer,
                exp_index,
            ).start()
        if part == 0:
            pltpu.make_async_copy(
                source.at[:, rows_of(seq_index, head_width)], place, p_recv.at[which]
            ).start()

    def wait_heads(which):
        _, target, before = arrays[which]
        wait_for(target.at[pl.ds(before, group)], p_recv.at[which])

    def halo_copies(which):
        target = arrays[which][1]
        return (
            copy_to(
                target.at[pl.ds(MOST, MOST)],
                target.at[pl.ds(MOST + group, MOST)],
                h_send.at[which, 0],
                h_recv.at[which, 0],
                seq_index,
                (exp_index + 3) % 4,
            ),
            copy_to(
                target.at[pl.ds(group, MOST)],
                target.at[pl.ds(0, MOST)],
                h_send.at[which, 1],
                h_recv.at[which, 1],
                seq_index,
                (exp_index + 1) % 4,
            ),
        )

    slot = ((core * 4 + exp_index) * 4 + at_y) * 4 + at_x

    def modulation_copies(phase):
        if phase == 0:
            source, target = own_modulation, modulation_out.at[slot]
            places = [((at_y * 4 + (at_x + d) % 4) * 2 + core, exp_index) for d in (1, 2, 3)]
        elif phase == 1:
            source = modulation_out.at[rows_of(slot // 4, 4)]
            target = source
            places = [((((at_y + d) % 4) * 4 + at_x) * 2 + core, exp_index) for d in (1, 2, 3)]
        elif phase == 2:
            source = modulation_out.at[rows_of(slot // 16, 16)]
            target = source
            places = [(seq_index, (exp_index + d) % 4) for d in (1, 2, 3)]
        else:
            source = modulation_out.at[rows_of(core, 64)]
            target = source
            places = [(at_y * 8 + at_x * 2 + 1 - core, exp_index)]
        return [
            copy_to(source, target, m_send.at[phase, i], m_recv.at[phase, i], peer, other)
            for i, (peer, other) in enumerate(places)
        ]

    def send_modulation(phase):
        for copy in modulation_copies(phase):
            copy.start()

    def wait_modulation(phase):
        for copy in modulation_copies(phase):
            copy.wait_recv()

    send_heads(0, 0)
    load_weight = pltpu.make_async_copy(weight_in, weight, local_sem.at[0])
    load_weight.start()

    samples = timestep_ref.shape[1]
    diagonal = lax.broadcasted_iota(jnp.int32, (samples, samples), 0) == lax.broadcasted_iota(
        jnp.int32, (samples, samples), 1
    )

    def upright(row):
        return jnp.sum(jnp.where(diagonal, row.astype(f32), 0.0), axis=1, keepdims=True)

    classes = class_table_ref.shape[0]
    chosen_class = jnp.where(
        lax.broadcasted_iota(jnp.int32, (samples, classes), 1).astype(f32)
        == upright(class_id_ref[...]),
        1.0,
        0.0,
    ).astype(bf16)
    table_rows = jnp.dot(chosen_class, class_table_ref[...], preferred_element_type=f32)
    half_columns = PLANE * head_width // 2
    column = seq_index * head_width + lax.broadcasted_iota(jnp.int32, (1, head_width), 1)
    freq_index = jnp.where(column < half_columns, column, column - half_columns).astype(f32)
    frequency = jnp.exp(-math.log(10000.0) * freq_index / half_columns)
    angles = upright(timestep_ref[...]) * frequency
    embedded = jnp.where(column < half_columns, jnp.cos(angles), jnp.sin(angles))
    value = embedded + table_rows
    own_condition[...] = (value / (1.0 + jnp.exp(-value))).astype(bf16)

    for offset in OFFSETS:
        copy_to(
            own_condition,
            conditions.at[seq_index],
            c_sem.at[0],
            c_sem.at[1],
            seq_index ^ offset,
            exp_index,
        ).start()
    pltpu.make_async_copy(own_condition, conditions.at[seq_index], c_sem.at[1]).start()
    send_heads(0, 1)
    wait_for(conditions, c_sem.at[1])
    load_weight.wait()
    condition = jnp.concatenate([conditions[place] for place in range(PLANE)], axis=1)
    own_modulation[...] = jnp.dot(condition, weight[...], preferred_element_type=f32).astype(bf16)
    keep = pltpu.make_async_copy(own_modulation, modulation_out.at[slot], local_sem.at[4])
    keep.start()
    send_modulation(0)
    send_heads(1, 0)

    ids = ids_ref[...]
    lane = lax.broadcasted_iota(jnp.int32, (1, head_width), 1)

    def total(mask):
        return jnp.sum(
            jnp.sum(jnp.where(mask, 1.0, 0.0), axis=0, keepdims=True), axis=1, keepdims=True
        )

    begins = jnp.zeros((1, head_width), f32)
    ends = jnp.zeros((1, head_width), f32)
    for image in range(32):
        begins = begins + jnp.where(lane == image, total(ids < image), 0.0)
        ends = ends + jnp.where(lane == image, total(ids <= image), 0.0)
    begins = begins.astype(jnp.int32)
    ends = ends.astype(jnp.int32)
    first_token = exp_index * group

    def tag_rows(step, carry):
        rows = rows_of(step, Q_ROWS)
        shape = (Q_ROWS, head_width)
        place = lax.broadcasted_iota(jnp.int32, shape, 0) + (first_token - MOST + step * Q_ROWS)
        same = (place >= begins) & (place < ends)
        key_tags[rows, :] = jnp.where(same, 0.0, -FAR).astype(bf16)
        return carry

    def query_tag_rows(step, carry):
        rows = rows_of(step, Q_ROWS)
        shape = (Q_ROWS, head_width)
        place = lax.broadcasted_iota(jnp.int32, shape, 0) + (first_token + step * Q_ROWS)
        same = (place >= begins) & (place < ends)
        query_tags[rows, :] = jnp.where(same, 1.0, 0.0).astype(bf16)
        return carry

    lax.fori_loop(0, key_tags.shape[0] // Q_ROWS, tag_rows, 0)
    lax.fori_loop(0, group // Q_ROWS, query_tag_rows, 0)
    keep_key_tags = pltpu.make_async_copy(key_tags, key_tags_out, local_sem.at[5])
    keep_key_tags.start()
    keep_query_tags = pltpu.make_async_copy(query_tags, query_tags_out, local_sem.at[6])
    keep_query_tags.start()

    keep.wait()
    wait_modulation(0)
    send_modulation(1)
    send_heads(1, 1)
    wait_modulation(1)
    send_modulation(2)
    wait_heads(0)
    for copy in halo_copies(0):
        copy.start()
    send_heads(2, 0)
    wait_modulation(2)
    send_modulation(3)

    low = jnp.zeros((1, head_width), f32)
    high = jnp.zeros((1, head_width), f32)
    for block in range(group // Q_ROWS):
        line = exp_index * (group // 128) + block * (Q_ROWS // 128)
        first = ids_ref[pl.ds(line, 1), 0:1]
        last = ids_ref[pl.ds(line + Q_ROWS // 128 - 1, 1), 127:128]
        low = low + jnp.where(lane == block, total(ids < first), 0.0)
        high = high + jnp.where(lane == block, total(ids <= last), 0.0)
    low = (low.astype(jnp.int32) - first_token + MOST) & ~127
    high = high.astype(jnp.int32) - first_token + MOST
    parts = jnp.maximum((high - low + KEY_STEP - 1) // KEY_STEP, Q_ROWS // KEY_STEP)
    spans_out[...] = jnp.where(
        lax.broadcasted_iota(jnp.int32, spans_out.shape, 0) == 0, low, parts
    )

    wait_heads(1)
    for copy in halo_copies(1):
        copy.start()
    send_heads(2, 1)
    wait_heads(2)
    wait_modulation(3)
    keep_key_tags.wait()
    keep_query_tags.wait()
    for which in range(2):
        for copy in halo_copies(which):
            copy.wait_recv()
    wait_for(conditions.at[pl.ds(0, PLANE - 1)], c_sem.at[0])
    for which in range(3):
        wait_for(query_out.at[pl.ds(0, group - tokens)], p_send.at[which])
    for which in range(2):
        for copy in halo_copies(which):
            copy.wait_send()
    for phase in range(4):
        for copy in modulation_copies(phase):
            copy.wait_send()


def exchange(
    query_input, key_input, value_input, mod_weight, class_table, class_id, timestep, sample_id
):
    tokens, width = query_input.shape
    head_width = width // PLANE
    group = tokens * PLANE
    extent = group + 2 * MOST
    bf16 = jnp.bfloat16
    samples = class_id.shape[0]
    anywhere = pl.BlockSpec(memory_space=pl.ANY)
    inside = pl.BlockSpec(memory_space=pltpu.VMEM)
    dma = pltpu.SemaphoreType.DMA
    return pl.pallas_call(
        exchange_kernel,
        out_shape=(
            jax.ShapeDtypeStruct((group, head_width), bf16),
            jax.ShapeDtypeStruct((extent, head_width), bf16),
            jax.ShapeDtypeStruct((extent, head_width), bf16),
            jax.ShapeDtypeStruct((group, head_width), bf16),
            jax.ShapeDtypeStruct((extent, head_width), bf16),
            jax.ShapeDtypeStruct((4 * PLANE, samples, mod_weight.shape[1]), bf16),
            jax.ShapeDtypeStruct((8, head_width), jnp.int32),
        ),
        in_specs=[anywhere] * 4 + [inside] * 4,
        out_specs=(anywhere,) * 6 + (inside,),
        scratch_shapes=[
            pltpu.VMEM((samples, head_width), bf16),
            pltpu.VMEM((PLANE, samples, head_width), bf16),
            pltpu.VMEM(mod_weight.shape, bf16),
            pltpu.VMEM((samples, mod_weight.shape[1]), bf16),
            pltpu.VMEM((group, head_width), bf16),
            pltpu.VMEM((extent, head_width), bf16),
            dma((7,)),
            dma((2,)),
            dma((3,)),
            dma((3,)),
            dma((2, 2)),
            dma((2, 2)),
            dma((4, 3)),
            dma((4, 3)),
        ],
        compiler_params=pltpu.CompilerParams(
            collective_id=0, has_side_effects=True, vmem_limit_bytes=60 * 2**20
        ),
        name="exchange",
    )(
        query_input,
        key_input,
        value_input,
        mod_weight,
        class_table,
        class_id.reshape(1, -1),
        timestep.reshape(1, -1),
        sample_id.reshape(-1, head_width),
    )


def experts_kernel(
    attended_ref,
    stream_in,
    modulation_in,
    w_first_in,
    w_second_in,
    tags_in,
    picks_ref,
    used_ref,
    router_ref,
    out_ref,
    stream_ref,
    modulation_ref,
    selector_ref,
    w_first,
    w_second,
    attended,
    token_mod,
    residual,
    normed,
    pick,
    unmix,
    mix,
    outgoing,
    landed,
    gathered,
    lined,
    hidden,
    far_out,
    far_in,
    side_raw,
    side_sum,
    raw_in,
    sum_in,
    held,
    own_total,
    homeward,
    back,
    router_twice,
    local_sem,
    a_sem,
    d_sem,
    z_send,
    z_recv,
    r_send,
    r_recv,
    b_sem,
):
    seq_index = lax.axis_index("seq")
    exp_index = lax.axis_index("exp")
    right = (exp_index + 1) % 4
    left = (exp_index + 3) % 4
    width = stream_ref.shape[1]
    tokens = stream_ref.shape[0]
    f32 = jnp.float32
    bf16 = jnp.bfloat16

    greet(seq_index, exp_index, (left, right))

    def plane_copy(source, target, send, recv, peer):
        return pltpu.make_async_remote_copy(
            src_ref=source,
            dst_ref=target,
            send_sem=send,
            recv_sem=recv,
            device_id=(peer, exp_index),
            device_id_type=MESH,
        )

    def ring_copy(source, target, send, recv, other):
        return pltpu.make_async_remote_copy(
            src_ref=source,
            dst_ref=target,
            send_sem=send,
            recv_sem=recv,
            device_id=(seq_index, other),
            device_id_type=MESH,
        )

    for offset in OFFSETS:
        peer = seq_index ^ offset
        plane_copy(
            attended_ref.at[rows_of(peer, tokens)],
            attended.at[seq_index],
            a_sem.at[0],
            a_sem.at[1],
            peer,
        ).start()
    pltpu.make_async_copy(
        attended_ref.at[rows_of(seq_index, tokens)], attended.at[seq_index], a_sem.at[1]
    ).start()
    load_mod = pltpu.make_async_copy(modulation_in, modulation_ref, local_sem.at[1])
    load_mod.start()
    load_stream = pltpu.make_async_copy(stream_in, stream_ref, local_sem.at[2])
    load_stream.start()
    load_tags = pltpu.make_async_copy(
        tags_in.at[rows_of(seq_index, tokens)], selector_ref, local_sem.at[5]
    )
    load_tags.start()
    load_first = pltpu.make_async_copy(w_first_in.at[0], w_first, local_sem.at[3])
    load_first.start()
    load_second = pltpu.make_async_copy(w_second_in.at[0], w_second, local_sem.at[4])
    load_second.start()

    count = PIECES * SLOT_ROWS
    row = lax.broadcasted_iota(jnp.int32, (count, count), 0)
    column = lax.broadcasted_iota(jnp.int32, (count, count), 1)
    by_source = (row & 31) * 16 + (row >> 6) * 2 + ((row >> 5) & 1)
    unmix[...] = jnp.where(by_source == column, 1.0, 0.0).astype(bf16)
    by_piece = ((row >> 1) & 7) * SLOT_ROWS + (row & 1) * PLANE + (row >> 4)
    mix[...] = jnp.where(by_piece == column, 1.0, 0.0).astype(bf16)
    column = lax.broadcasted_iota(jnp.int32, pick.shape, 1)
    used = used_ref[...]
    chosen = jnp.concatenate(
        [
            jnp.where(used > 0, picks_ref[0:1, :], -1),
            jnp.where(used > 1, picks_ref[1:2, :], -1),
        ],
        axis=1,
    ).astype(f32)
    row = lax.broadcasted_iota(jnp.int32, (count, SLOT_ROWS), 0)
    slot = lax.broadcasted_iota(jnp.int32, (count, SLOT_ROWS), 1)
    mine = slot == (row & 1) * PLANE + (row >> 4)
    token = jnp.sum(jnp.where(mine, chosen, 0.0), axis=1, keepdims=True)
    piece = (lax.broadcasted_iota(jnp.int32, (count, 1), 0) >> 1) & 7
    target = jnp.where(token < 0.0, -1.0, token + (piece * tokens).astype(f32))
    pick[...] = jnp.where(column.astype(f32) == target, 1.0, 0.0).astype(bf16)

    load_mod.wait()
    load_stream.wait()

    load_tags.wait()
    samples = modulation_ref.shape[1]

    def spread_mod(step, carry):
        base = (step % 2 * 16 + step // 8) * 4 + step // 2 % 4
        whole = jnp.concatenate([modulation_ref[base + 16 * part] for part in range(4)], axis=1)
        token_mod[:, rows_of(step, 512)] = jnp.dot(
            selector_ref[:, :samples], whole, preferred_element_type=f32
        )
        return carry

    lax.fori_loop(0, 3 * width // 512, spread_mod, 0)

    double = lax.broadcasted_iota(jnp.int32, (SLOT_ROWS, samples), 0) & 31
    twice = jnp.where(
        double == lax.broadcasted_iota(jnp.int32, (SLOT_ROWS, samples), 1), 1.0, 0.0
    ).astype(bf16)
    router_twice[...] = jnp.dot(twice, router_ref[...], preferred_element_type=f32).astype(bf16)

    wait_for(attended, a_sem.at[1])

    def norm_rows(step, carry):
        rows = rows_of(step, 16)
        heads = jnp.concatenate([attended[head, rows, :] for head in range(PLANE)], axis=1)
        value = stream_ref[rows, :].astype(f32) + token_mod[rows, :width] * heads.astype(f32)
        residual[rows, :] = value
        average = jnp.mean(value, axis=1, keepdims=True)
        centered = value - average
        variance = jnp.mean(centered * centered, axis=1, keepdims=True)
        shift = token_mod[rows, width : 2 * width]
        scale = token_mod[rows, 2 * width : 3 * width]
        normed[rows, :] = (centered * lax.rsqrt(variance + EPS) * (1.0 + scale) + shift).astype(bf16)
        return carry

    lax.fori_loop(0, tokens // 16, norm_rows, 0)

    def plane_send(source, target, sems, half):
        place = target.at[half, rows_of(seq_index, 16)]
        for offset in OFFSETS:
            peer = seq_index ^ offset
            plane_copy(
                source.at[half, rows_of(peer, 16)], place, sems.at[half, 0], sems.at[half, 1], peer
            ).start()
        pltpu.make_async_copy(
            source.at[half, rows_of(seq_index, 16)], place, sems.at[half, 1]
        ).start()

    for half in range(2):
        stacked = jnp.concatenate(
            [
                normed[:, half * HALF + piece * TILE : half * HALF + (piece + 1) * TILE]
                for piece in range(PIECES)
            ],
            axis=0,
        )
        outgoing[half] = jnp.dot(pick[...], stacked, preferred_element_type=f32).astype(bf16)
        plane_send(outgoing, landed, d_sem, half)

    logits = lax.dot_general(
        normed[...], router_twice[...], (((1,), (1,)), ((), ())), preferred_element_type=f32
    )
    place = lax.broadcasted_iota(jnp.int32, (tokens, SLOT_ROWS), 0).astype(f32) == chosen
    weighted = jnp.where(place, 1.0 / (1.0 + jnp.exp(-logits)), 0.0)
    lax.fori_loop(3 * width // 512, 4 * width // 512, spread_mod, 0)
    weight_first = weighted.astype(bf16)
    weight_rest = weighted - weight_first.astype(f32)
    weight_second = weight_rest.astype(bf16)
    weight_third = (weight_rest - weight_second.astype(f32)).astype(bf16)
    weight_parts = jnp.concatenate([weight_first, weight_second, weight_third], axis=1)

    def line_up(which, half):
        lined[which * SLOT_ROWS : (which + 1) * SLOT_ROWS, half * HALF : (half + 1) * HALF] = (
            jnp.concatenate(
                [
                    gathered[which, half, piece * SLOT_ROWS : (piece + 1) * SLOT_ROWS, :]
                    for piece in range(PIECES)
                ],
                axis=1,
            )
        )

    for half in range(2):
        wait_for(landed.at[half], d_sem.at[half, 1])
        gathered[0, half] = jnp.dot(
            unmix[...], landed[half], preferred_element_type=f32
        ).astype(bf16)
        if half == 0:
            own_right_0 = ring_copy(
                gathered.at[0, 0], gathered.at[2, 0], z_send.at[0], z_recv.at[0], right
            )
            own_right_0.start()
        else:
            own_left_1 = ring_copy(
                gathered.at[0, 1], gathered.at[3, 1], z_send.at[1], z_recv.at[1], left
            )
            own_left_1.start()
        line_up(0, half)
    own_right_0.wait_recv()
    on_right_0 = ring_copy(
        gathered.at[2, 0], gathered.at[1, 0], z_send.at[2], z_recv.at[2], right
    )
    on_right_0.start()
    own_left_1.wait_recv()
    on_left_1 = ring_copy(gathered.at[3, 1], gathered.at[1, 1], z_send.at[3], z_recv.at[3], left)
    on_left_1.start()
    own_right_1 = ring_copy(
        gathered.at[0, 1], gathered.at[2, 1], z_send.at[4], z_recv.at[4], right
    )
    own_right_1.start()
    own_left_0 = ring_copy(gathered.at[0, 0], gathered.at[3, 0], z_send.at[5], z_recv.at[5], left)
    own_left_0.start()
    line_up(2, 0)
    line_up(3, 1)
    load_first.wait()
    load_second.wait()

    def first_product(base):
        rows = slice(base, base + 2 * SLOT_ROWS)

        def columns_of(step, carry):
            columns = rows_of(step, 256)
            product = jnp.dot(lined[rows, :], w_first[:, columns], preferred_element_type=f32)
            hidden[rows, columns] = jax.nn.gelu(product, approximate=True).astype(bf16)
            return carry

        lax.fori_loop(0, w_first.shape[1] // 256, columns_of, 0)

    def second_product(base, half, lower, upper):
        rows = slice(base, base + 2 * SLOT_ROWS)

        def columns_of(step, carry):
            columns = rows_of(step, 256)
            product = jnp.dot(
                hidden[rows, :],
                w_second[:, rows_of(step + half * (HALF // 256), 256)],
                preferred_element_type=f32,
            )
            lower[:, columns] = product[:SLOT_ROWS].astype(lower.dtype)
            upper[:, columns] = product[SLOT_ROWS:].astype(upper.dtype)
            return carry

        lax.fori_loop(0, HALF // 256, columns_of, 0)

    on_right_0.wait_recv()
    line_up(1, 0)
    on_left_1.wait_recv()
    line_up(1, 1)
    first_product(0)
    second_product(0, 0, own_total.at[0], far_out.at[0])
    far_right = ring_copy(far_out.at[0], far_in.at[0], r_send.at[0], r_recv.at[0], right)
    far_right.start()
    second_product(0, 1, own_total.at[1], far_out.at[1])
    far_left = ring_copy(far_out.at[1], far_in.at[1], r_send.at[1], r_recv.at[1], left)
    far_left.start()
    own_right_1.wait_recv()
    line_up(2, 1)
    own_left_0.wait_recv()
    line_up(3, 0)
    first_product(2 * SLOT_ROWS)
    second_product(2 * SLOT_ROWS, 0, side_raw.at[0], held.at[0])
    raw_left = ring_copy(side_raw.at[0], raw_in.at[0], r_send.at[2], r_recv.at[2], left)
    raw_left.start()
    second_product(2 * SLOT_ROWS, 1, held.at[1], side_raw.at[1])
    raw_right = ring_copy(side_raw.at[1], raw_in.at[1], r_send.at[3], r_recv.at[3], right)
    raw_right.start()
    far_right.wait_recv()
    side_sum[0] = (held[0] + far_in[0].astype(f32)).astype(bf16)
    sum_right = ring_copy(side_sum.at[0], sum_in.at[0], r_send.at[4], r_recv.at[4], right)
    sum_right.start()
    far_left.wait_recv()
    side_sum[1] = (held[1] + far_in[1].astype(f32)).astype(bf16)
    sum_left = ring_copy(side_sum.at[1], sum_in.at[1], r_send.at[5], r_recv.at[5], left)
    sum_left.start()

    for half, raw, summed in ((0, raw_left, sum_right), (1, raw_right, sum_left)):
        raw.wait_recv()
        summed.wait_recv()
        total = (
            own_total[half] + raw_in[half].astype(f32) + sum_in[half].astype(f32)
        ).astype(bf16)
        stacked = jnp.concatenate(
            [total[:, piece * TILE : (piece + 1) * TILE] for piece in range(PIECES)], axis=0
        )
        homeward[half] = jnp.dot(mix[...], stacked, preferred_element_type=f32).astype(bf16)
        plane_send(homeward, back, b_sem, half)

    for half in range(2):
        wait_for(back.at[half], b_sem.at[half, 1])
        ordered = jnp.dot(unmix[...], back[half], preferred_element_type=f32).astype(bf16)
        for piece in range(PIECES):
            rows = ordered[piece * SLOT_ROWS : (piece + 1) * SLOT_ROWS, :]
            begin = half * HALF + piece * TILE
            columns = slice(begin, begin + TILE)
            expert_sum = jnp.dot(
                weight_parts, jnp.concatenate([rows, rows, rows], axis=0), preferred_element_type=f32
            )
            gate = token_mod[:, 3 * width + begin : 3 * width + begin + TILE]
            out_ref[:, columns] = (residual[:, columns] + gate * expert_sum).astype(bf16)

    wait_for(attended.at[pl.ds(0, PLANE - 1)], a_sem.at[0])
    for half in range(2):
        wait_for(landed.at[half, pl.ds(0, 16 * (PLANE - 1))], d_sem.at[half, 0])
        wait_for(back.at[half, pl.ds(0, 16 * (PLANE - 1))], b_sem.at[half, 0])
    for copy in (
        own_right_0,
        own_left_1,
        on_right_0,
        on_left_1,
        own_right_1,
        own_left_0,
        far_right,
        far_left,
        raw_left,
        raw_right,
        sum_right,
        sum_left,
    ):
        copy.wait_send()


def feed_forward(
    attended_head, stream, modulation, expert_in, expert_out, query_tags, picks, used, router
):
    tokens, width = stream.shape
    bf16 = jnp.bfloat16
    f32 = jnp.float32
    part = expert_in.shape[2]
    block = PIECES * SLOT_ROWS
    anywhere = pl.BlockSpec(memory_space=pl.ANY)
    inside = pl.BlockSpec(memory_space=pltpu.VMEM)
    dma = pltpu.SemaphoreType.DMA
    return pl.pallas_call(
        experts_kernel,
        out_shape=jax.ShapeDtypeStruct((tokens, width), bf16),
        in_specs=[anywhere] * 6 + [inside] * 3,
        out_specs=inside,
        scratch_shapes=[
            pltpu.VMEM((tokens, width), bf16),
            pltpu.VMEM(modulation.shape, bf16),
            pltpu.VMEM((tokens, width // PLANE), bf16),
            pltpu.VMEM((width, part), bf16),
            pltpu.VMEM((part, width), bf16),
            pltpu.VMEM((PLANE, tokens, width // PLANE), bf16),
            pltpu.VMEM((tokens, 4 * width), f32),
            pltpu.VMEM((tokens, width), f32),
            pltpu.VMEM((tokens, width), bf16),
            pltpu.VMEM((block, PIECES * tokens), bf16),
            pltpu.VMEM((block, block), bf16),
            pltpu.VMEM((block, block), bf16),
            pltpu.VMEM((2, block, TILE), bf16),
            pltpu.VMEM((2, block, TILE), bf16),
            pltpu.VMEM((4, 2, block, TILE), bf16),
            pltpu.VMEM((4 * SLOT_ROWS, width), bf16),
            pltpu.VMEM((4 * SLOT_ROWS, part), bf16),
            pltpu.VMEM((2, SLOT_ROWS, HALF), bf16),
            pltpu.VMEM((2, SLOT_ROWS, HALF), bf16),
            pltpu.VMEM((2, SLOT_ROWS, HALF), bf16),
            pltpu.VMEM((2, SLOT_ROWS, HALF), bf16),
            pltpu.VMEM((2, SLOT_ROWS, HALF), bf16),
            pltpu.VMEM((2, SLOT_ROWS, HALF), bf16),
            pltpu.VMEM((2, SLOT_ROWS, HALF), f32),
            pltpu.VMEM((2, SLOT_ROWS, HALF), f32),
            pltpu.VMEM((2, block, TILE), bf16),
            pltpu.VMEM((2, block, TILE), bf16),
            pltpu.VMEM((SLOT_ROWS, width), bf16),
            dma((6,)),
            dma((2,)),
            dma((2, 2)),
            dma((6,)),
            dma((6,)),
            dma((6,)),
            dma((6,)),
            dma((2, 2)),
        ],
        compiler_params=pltpu.CompilerParams(
            collective_id=1, has_side_effects=True, vmem_limit_bytes=58 * 2**20
        ),
        name="experts",
    )(
        attended_head,
        stream,
        modulation,
        expert_in,
        expert_out,
        query_tags,
        picks,
        used,
        router,
    )


def on_device(
    stream,
    query_input,
    key_input,
    value_input,
    sample_id,
    timestep,
    class_id,
    class_table,
    mod_weight,
    router_weight,
    expert_in,
    expert_out,
    picked,
    counts,
):
    head_query, keys, values, query_tags, key_tags, modulation, spans = exchange(
        query_input,
        key_input,
        value_input,
        mod_weight,
        class_table,
        class_id,
        timestep,
        sample_id,
    )
    attended_head = local_attention(spans, head_query, query_tags, keys, key_tags, values)
    return feed_forward(
        attended_head,
        stream,
        modulation,
        expert_in,
        expert_out,
        query_tags,
        picked[:, 0, :].T,
        counts.T,
        router_weight.T,
    )


def solution(mesh):
    return jax.shard_map(
        on_device,
        mesh=mesh,
        in_specs=(
            P(("exp", "seq"), None),
            P(("exp", "seq"), None),
            P(("exp", "seq"), None),
            P(("exp", "seq"), None),
            P(),
            P(),
            P(),
            P(None, "seq"),
            P(None, ("seq", "exp")),
            P(),
            P("seq", None, "exp"),
            P("seq", "exp", None),
            P(None, ("exp", "seq"), None),
            P(None, ("exp", "seq")),
        ),
        out_specs=P(("exp", "seq"), None),
        check_vma=False,
    )
```

```python
import math

import jax
import jax.numpy as jnp
from jax import lax
from jax.experimental import pallas as pl
from jax.experimental.pallas import tpu as pltpu
from jax.sharding import PartitionSpec as P

MOST = 1024


EPS = 1e-06


Q_ROWS = 512
KEY_STEP = 256
FAR = 32768.0


def attention_kernel(spans, q_ref, fq_ref, k_ref, fk_ref, v_ref, out_ref):
    step = pl.program_id(0)
    start = spans[0, step]
    parts = spans[1, step]
    head_width = q_ref.shape[1]
    factor = math.log2(math.e) / math.sqrt(head_width)
    least_parts = Q_ROWS // KEY_STEP
    most_parts = (2 * MOST + Q_ROWS) // KEY_STEP + 1

    def with_parts(number):
        span = number * KEY_STEP

        @pl.when(parts == number)
        def _():
            first = pl.multiple_of(jnp.minimum(start, k_ref.shape[0] - span), 128)
            rows = pl.ds(first, span)
            keys = jnp.concatenate([k_ref[rows, :], fk_ref[rows, :]], axis=1)
            values = jnp.concatenate(
                [v_ref[rows, :], jnp.ones((span, head_width), jnp.bfloat16)], axis=1
            )
            for line in range(0, Q_ROWS, KEY_STEP):
                lines = slice(line, line + KEY_STEP)
                query = jnp.concatenate([q_ref[lines, :], fq_ref[lines, :]], axis=1)
                scores = lax.dot_general(
                    query, keys, (((1,), (1,)), ((), ())), preferred_element_type=jnp.float32
                )
                highest = jnp.max(scores, axis=1, keepdims=True)
                numer = jnp.exp2((scores - highest) * factor).astype(jnp.bfloat16)
                total = jnp.dot(numer, values, preferred_element_type=jnp.float32)
                out_ref[lines, :] = (total[:, :head_width] / total[:, head_width:]).astype(
                    jnp.bfloat16
                )

    for number in range(least_parts, most_parts + 1):
        with_parts(number)


def local_attention(spans, head_query, query_tags, keys, key_tags, values):
    group, head_width = head_query.shape
    extent = keys.shape[0]
    blocks = group // Q_ROWS
    whole = lambda step, spans: (0, 0)
    part = lambda step, spans: (step, 0)
    return pl.pallas_call(
        attention_kernel,
        grid_spec=pltpu.PrefetchScalarGridSpec(
            num_scalar_prefetch=1,
            grid=(blocks,),
            in_specs=[
                pl.BlockSpec((Q_ROWS, head_width), part),
                pl.BlockSpec((Q_ROWS, head_width), part),
                pl.BlockSpec((extent, head_width), whole),
                pl.BlockSpec((extent, head_width), whole),
                pl.BlockSpec((extent, head_width), whole),
            ],
            out_specs=pl.BlockSpec((Q_ROWS, head_width), part),
        ),
        out_shape=jax.ShapeDtypeStruct((group, head_width), jnp.bfloat16),
        compiler_params=pltpu.CompilerParams(vmem_limit_bytes=60 * 2**20),
        name="attention",
    )(spans, head_query, query_tags, keys, key_tags, values)


MESH = pl.DeviceIdType.MESH
PLANE = 32
TILE = 256
PIECES = 8
HALF = TILE * PIECES
SLOT_ROWS = 64


OFFSETS = [(number * 13) % PLANE for number in range(1, PLANE)]


def mirrored(offset):
    other = (0, 3, 2, 1)
    return other[offset // 8] * 8 + other[offset // 2 % 4] * 2 + offset % 2


def partners(seq_index, offsets):
    core = seq_index % 2
    return [
        seq_index ^ (offset + core * (mirrored(offset) - offset)) for offset in offsets
    ]


def greet(seq_index, exp_index, ring):
    barrier = pltpu.get_barrier_semaphore()
    for offset in OFFSETS:
        pl.semaphore_signal(
            barrier,
            inc=1,
            device_id=(seq_index ^ offset, exp_index),
            device_id_type=MESH,
        )
    for other in ring:
        pl.semaphore_signal(barrier, inc=1, device_id=(seq_index, other), device_id_type=MESH)
    pl.semaphore_wait(barrier, PLANE - 1 + len(ring))


def wait_for(part, semaphore):
    pltpu.make_async_copy(part, part, semaphore).wait()


def rows_of(number, size):
    return pl.ds(pl.multiple_of(number * size, size), size)


def exchange_kernel(
    query_in,
    key_in,
    value_in,
    weight_in,
    class_table_ref,
    class_id_ref,
    timestep_ref,
    ids_ref,
    query_out,
    key_out,
    value_out,
    query_tags_out,
    key_tags_out,
    modulation_out,
    spans_out,
    own_condition,
    conditions,
    weight,
    own_modulation,
    query_tags,
    key_tags,
    local_sem,
    c_sem,
    p_send,
    p_recv,
    h_send,
    h_recv,
    m_send,
    m_recv,
):
    seq_index = lax.axis_index("seq")
    exp_index = lax.axis_index("exp")
    tokens = query_in.shape[0]
    group, head_width = query_out.shape
    at_y = seq_index // 8
    at_x = seq_index // 2 % 4
    core = seq_index % 2
    f32 = jnp.float32
    bf16 = jnp.bfloat16

    greet(seq_index, exp_index, [(exp_index + step) % 4 for step in (1, 2, 3)])

    def copy_to(source, target, send, recv, peer, other):
        return pltpu.make_async_remote_copy(
            src_ref=source,
            dst_ref=target,
            send_sem=send,
            recv_sem=recv,
            device_id=(peer, other),
            device_id_type=MESH,
        )

    arrays = ((key_in, key_out, MOST), (value_in, value_out, MOST), (query_in, query_out, 0))

    def send_heads(which, part):
        source, target, before = arrays[which]
        place = target.at[pl.ds(pl.multiple_of(before + seq_index * tokens, tokens), tokens)]
        for peer in partners(seq_index, OFFSETS[15:] if part else OFFSETS[:15]):
            copy_to(
                source.at[:, rows_of(peer, head_width)],
                place,
                p_send.at[which],
                p_recv.at[which],
                peer,
                exp_index,
            ).start()
        if part == 0:
            pltpu.make_async_copy(
                source.at[:, rows_of(seq_index, head_width)], place, p_recv.at[which]
            ).start()

    def wait_heads(which):
        _, target, before = arrays[which]
        wait_for(target.at[pl.ds(before, group)], p_recv.at[which])

    def halo_copies(which):
        target = arrays[which][1]
        return (
            copy_to(
                target.at[pl.ds(MOST, MOST)],
                target.at[pl.ds(MOST + group, MOST)],
                h_send.at[which, 0],
                h_recv.at[which, 0],
                seq_index,
                (exp_index + 3) % 4,
            ),
            copy_to(
                target.at[pl.ds(group, MOST)],
                target.at[pl.ds(0, MOST)],
                h_send.at[which, 1],
                h_recv.at[which, 1],
                seq_index,
                (exp_index + 1) % 4,
            ),
        )

    slot = ((core * 4 + exp_index) * 4 + at_y) * 4 + at_x

    def modulation_copies(phase):
        if phase == 0:
            source, target = own_modulation, modulation_out.at[slot]
            places = [((at_y * 4 + (at_x + d) % 4) * 2 + core, exp_index) for d in (1, 2, 3)]
        elif phase == 1:
            source = modulation_out.at[rows_of(slot // 4, 4)]
            target = source
            places = [((((at_y + d) % 4) * 4 + at_x) * 2 + core, exp_index) for d in (1, 2, 3)]
        elif phase == 2:
            source = modulation_out.at[rows_of(slot // 16, 16)]
            target = source
            places = [(seq_index, (exp_index + d) % 4) for d in (1, 2, 3)]
        else:
            source = modulation_out.at[rows_of(core, 64)]
            target = source
            places = [(at_y * 8 + at_x * 2 + 1 - core, exp_index)]
        return [
            copy_to(source, target, m_send.at[phase, i], m_recv.at[phase, i], peer, other)
            for i, (peer, other) in enumerate(places)
        ]

    def send_modulation(phase):
        for copy in modulation_copies(phase):
            copy.start()

    def wait_modulation(phase):
        for copy in modulation_copies(phase):
            copy.wait_recv()

    send_heads(0, 0)
    load_weight = pltpu.make_async_copy(weight_in, weight, local_sem.at[0])
    load_weight.start()

    samples = timestep_ref.shape[1]
    diagonal = lax.broadcasted_iota(jnp.int32, (samples, samples), 0) == lax.broadcasted_iota(
        jnp.int32, (samples, samples), 1
    )

    def upright(row):
        return jnp.sum(jnp.where(diagonal, row.astype(f32), 0.0), axis=1, keepdims=True)

    classes = class_table_ref.shape[0]
    chosen_class = jnp.where(
        lax.broadcasted_iota(jnp.int32, (samples, classes), 1).astype(f32)
        == upright(class_id_ref[...]),
        1.0,
        0.0,
    ).astype(bf16)
    table_rows = jnp.dot(chosen_class, class_table_ref[...], preferred_element_type=f32)
    half_columns = PLANE * head_width // 2
    column = seq_index * head_width + lax.broadcasted_iota(jnp.int32, (1, head_width), 1)
    freq_index = jnp.where(column < half_columns, column, column - half_columns).astype(f32)
    frequency = jnp.exp(-math.log(10000.0) * freq_index / half_columns)
    angles = upright(timestep_ref[...]) * frequency
    embedded = jnp.where(column < half_columns, jnp.cos(angles), jnp.sin(angles))
    value = embedded + table_rows
    own_condition[...] = (value / (1.0 + jnp.exp(-value))).astype(bf16)

    for peer in partners(seq_index, OFFSETS):
        copy_to(
            own_condition,
            conditions.at[seq_index],
            c_sem.at[0],
            c_sem.at[1],
            peer,
            exp_index,
        ).start()
    pltpu.make_async_copy(own_condition, conditions.at[seq_index], c_sem.at[1]).start()
    send_heads(0, 1)
    wait_for(conditions, c_sem.at[1])
    load_weight.wait()
    condition = jnp.concatenate([conditions[place] for place in range(PLANE)], axis=1)
    own_modulation[...] = jnp.dot(condition, weight[...], preferred_element_type=f32).astype(bf16)
    keep = pltpu.make_async_copy(own_modulation, modulation_out.at[slot], local_sem.at[4])
    keep.start()
    send_modulation(0)
    send_heads(1, 0)

    ids = ids_ref[...]
    lane = lax.broadcasted_iota(jnp.int32, (1, head_width), 1)

    def total(mask):
        return jnp.sum(
            jnp.sum(jnp.where(mask, 1.0, 0.0), axis=0, keepdims=True), axis=1, keepdims=True
        )

    begins = jnp.zeros((1, head_width), f32)
    ends = jnp.zeros((1, head_width), f32)
    for image in range(32):
        begins = begins + jnp.where(lane == image, total(ids < image), 0.0)
        ends = ends + jnp.where(lane == image, total(ids <= image), 0.0)
    begins = begins.astype(jnp.int32)
    ends = ends.astype(jnp.int32)
    first_token = exp_index * group

    def tag_rows(step, carry):
        rows = rows_of(step, Q_ROWS)
        shape = (Q_ROWS, head_width)
        place = lax.broadcasted_iota(jnp.int32, shape, 0) + (first_token - MOST + step * Q_ROWS)
        same = (place >= begins) & (place < ends)
        key_tags[rows, :] = jnp.where(same, 0.0, -FAR).astype(bf16)
        return carry

    def query_tag_rows(step, carry):
        rows = rows_of(step, Q_ROWS)
        shape = (Q_ROWS, head_width)
        place = lax.broadcasted_iota(jnp.int32, shape, 0) + (first_token + step * Q_ROWS)
        same = (place >= begins) & (place < ends)
        query_tags[rows, :] = jnp.where(same, 1.0, 0.0).astype(bf16)
        return carry

    lax.fori_loop(0, key_tags.shape[0] // Q_ROWS, tag_rows, 0)
    lax.fori_loop(0, group // Q_ROWS, query_tag_rows, 0)
    keep_key_tags = pltpu.make_async_copy(key_tags, key_tags_out, local_sem.at[5])
    keep_key_tags.start()
    keep_query_tags = pltpu.make_async_copy(query_tags, query_tags_out, local_sem.at[6])
    keep_query_tags.start()

    keep.wait()
    wait_modulation(0)
    send_modulation(1)
    send_heads(1, 1)
    wait_heads(0)
    for copy in halo_copies(0):
        copy.start()
    send_heads(2, 0)
    wait_modulation(1)
    send_modulation(2)

    low = jnp.zeros((1, head_width), f32)
    high = jnp.zeros((1, head_width), f32)
    for block in range(group // Q_ROWS):
        line = exp_index * (group // 128) + block * (Q_ROWS // 128)
        first = ids_ref[pl.ds(line, 1), 0:1]
        last = ids_ref[pl.ds(line + Q_ROWS // 128 - 1, 1), 127:128]
        low = low + jnp.where(lane == block, total(ids < first), 0.0)
        high = high + jnp.where(lane == block, total(ids <= last), 0.0)
    low = (low.astype(jnp.int32) - first_token + MOST) & ~127
    high = high.astype(jnp.int32) - first_token + MOST
    parts = jnp.maximum((high - low + KEY_STEP - 1) // KEY_STEP, Q_ROWS // KEY_STEP)
    spans_out[...] = jnp.where(
        lax.broadcasted_iota(jnp.int32, spans_out.shape, 0) == 0, low, parts
    )

    wait_heads(1)
    for copy in halo_copies(1):
        copy.start()
    send_heads(2, 1)
    wait_modulation(2)
    send_modulation(3)
    wait_heads(2)
    wait_modulation(3)
    keep_key_tags.wait()
    keep_query_tags.wait()
    for which in range(2):
        for copy in halo_copies(which):
            copy.wait_recv()
    wait_for(conditions.at[pl.ds(0, PLANE - 1)], c_sem.at[0])
    for which in range(3):
        wait_for(query_out.at[pl.ds(0, group - tokens)], p_send.at[which])
    for which in range(2):
        for copy in halo_copies(which):
            copy.wait_send()
    for phase in range(4):
        for copy in modulation_copies(phase):
            copy.wait_send()


def exchange(
    query_input, key_input, value_input, mod_weight, class_table, class_id, timestep, sample_id
):
    tokens, width = query_input.shape
    head_width = width // PLANE
    group = tokens * PLANE
    extent = group + 2 * MOST
    bf16 = jnp.bfloat16
    samples = class_id.shape[0]
    anywhere = pl.BlockSpec(memory_space=pl.ANY)
    inside = pl.BlockSpec(memory_space=pltpu.VMEM)
    dma = pltpu.SemaphoreType.DMA
    return pl.pallas_call(
        exchange_kernel,
        out_shape=(
            jax.ShapeDtypeStruct((group, head_width), bf16),
            jax.ShapeDtypeStruct((extent, head_width), bf16),
            jax.ShapeDtypeStruct((extent, head_width), bf16),
            jax.ShapeDtypeStruct((group, head_width), bf16),
            jax.ShapeDtypeStruct((extent, head_width), bf16),
            jax.ShapeDtypeStruct((4 * PLANE, samples, mod_weight.shape[1]), bf16),
            jax.ShapeDtypeStruct((8, head_width), jnp.int32),
        ),
        in_specs=[anywhere] * 4 + [inside] * 4,
        out_specs=(anywhere,) * 6 + (inside,),
        scratch_shapes=[
            pltpu.VMEM((samples, head_width), bf16),
            pltpu.VMEM((PLANE, samples, head_width), bf16),
            pltpu.VMEM(mod_weight.shape, bf16),
            pltpu.VMEM((samples, mod_weight.shape[1]), bf16),
            pltpu.VMEM((group, head_width), bf16),
            pltpu.VMEM((extent, head_width), bf16),
            dma((7,)),
            dma((2,)),
            dma((3,)),
            dma((3,)),
            dma((2, 2)),
            dma((2, 2)),
            dma((4, 3)),
            dma((4, 3)),
        ],
        compiler_params=pltpu.CompilerParams(
            collective_id=0, has_side_effects=True, vmem_limit_bytes=60 * 2**20
        ),
        name="exchange",
    )(
        query_input,
        key_input,
        value_input,
        mod_weight,
        class_table,
        class_id.reshape(1, -1),
        timestep.reshape(1, -1),
        sample_id.reshape(-1, head_width),
    )


def experts_kernel(
    attended_ref,
    stream_in,
    modulation_in,
    w_first_in,
    w_second_in,
    tags_in,
    picks_ref,
    used_ref,
    router_ref,
    out_ref,
    stream_ref,
    modulation_ref,
    selector_ref,
    w_first,
    w_second,
    attended,
    token_mod,
    residual,
    normed,
    pick,
    unmix,
    mix,
    outgoing,
    landed,
    gathered,
    lined,
    hidden,
    far_out,
    far_in,
    side_raw,
    side_sum,
    raw_in,
    sum_in,
    held,
    own_total,
    homeward,
    back,
    router_twice,
    local_sem,
    a_sem,
    d_sem,
    z_send,
    z_recv,
    r_send,
    r_recv,
    b_sem,
):
    seq_index = lax.axis_index("seq")
    exp_index = lax.axis_index("exp")
    right = (exp_index + 1) % 4
    left = (exp_index + 3) % 4
    width = stream_ref.shape[1]
    tokens = stream_ref.shape[0]
    f32 = jnp.float32
    bf16 = jnp.bfloat16

    greet(seq_index, exp_index, (left, right))

    def plane_copy(source, target, send, recv, peer):
        return pltpu.make_async_remote_copy(
            src_ref=source,
            dst_ref=target,
            send_sem=send,
            recv_sem=recv,
            device_id=(peer, exp_index),
            device_id_type=MESH,
        )

    def ring_copy(source, target, send, recv, other):
        return pltpu.make_async_remote_copy(
            src_ref=source,
            dst_ref=target,
            send_sem=send,
            recv_sem=recv,
            device_id=(seq_index, other),
            device_id_type=MESH,
        )

    for peer in partners(seq_index, OFFSETS):
        plane_copy(
            attended_ref.at[rows_of(peer, tokens)],
            attended.at[seq_index],
            a_sem.at[0],
            a_sem.at[1],
            peer,
        ).start()
    pltpu.make_async_copy(
        attended_ref.at[rows_of(seq_index, tokens)], attended.at[seq_index], a_sem.at[1]
    ).start()
    load_mod = pltpu.make_async_copy(modulation_in, modulation_ref, local_sem.at[1])
    load_mod.start()
    load_stream = pltpu.make_async_copy(stream_in, stream_ref, local_sem.at[2])
    load_stream.start()
    load_tags = pltpu.make_async_copy(
        tags_in.at[rows_of(seq_index, tokens)], selector_ref, local_sem.at[5]
    )
    load_tags.start()
    load_first = pltpu.make_async_copy(w_first_in.at[0], w_first, local_sem.at[3])
    load_first.start()
    load_second = pltpu.make_async_copy(w_second_in.at[0], w_second, local_sem.at[4])
    load_second.start()

    count = PIECES * SLOT_ROWS
    row = lax.broadcasted_iota(jnp.int32, (count, count), 0)
    column = lax.broadcasted_iota(jnp.int32, (count, count), 1)
    by_source = (row & 31) * 16 + (row >> 6) * 2 + ((row >> 5) & 1)
    unmix[...] = jnp.where(by_source == column, 1.0, 0.0).astype(bf16)
    by_piece = ((row >> 1) & 7) * SLOT_ROWS + (row & 1) * PLANE + (row >> 4)
    mix[...] = jnp.where(by_piece == column, 1.0, 0.0).astype(bf16)
    column = lax.broadcasted_iota(jnp.int32, pick.shape, 1)
    used = used_ref[...]
    chosen = jnp.concatenate(
        [
            jnp.where(used > 0, picks_ref[0:1, :], -1),
            jnp.where(used > 1, picks_ref[1:2, :], -1),
        ],
        axis=1,
    ).astype(f32)
    row = lax.broadcasted_iota(jnp.int32, (count, SLOT_ROWS), 0)
    slot = lax.broadcasted_iota(jnp.int32, (count, SLOT_ROWS), 1)
    mine = slot == (row & 1) * PLANE + (row >> 4)
    token = jnp.sum(jnp.where(mine, chosen, 0.0), axis=1, keepdims=True)
    piece = (lax.broadcasted_iota(jnp.int32, (count, 1), 0) >> 1) & 7
    target = jnp.where(token < 0.0, -1.0, token + (piece * tokens).astype(f32))
    pick[...] = jnp.where(column.astype(f32) == target, 1.0, 0.0).astype(bf16)

    load_mod.wait()
    load_stream.wait()

    load_tags.wait()
    samples = modulation_ref.shape[1]

    def spread_mod(step, carry):
        base = (step % 2 * 16 + step // 8) * 4 + step // 2 % 4
        whole = jnp.concatenate([modulation_ref[base + 16 * part] for part in range(4)], axis=1)
        token_mod[:, rows_of(step, 512)] = jnp.dot(
            selector_ref[:, :samples], whole, preferred_element_type=f32
        )
        return carry

    lax.fori_loop(0, 3 * width // 512, spread_mod, 0)

    double = lax.broadcasted_iota(jnp.int32, (SLOT_ROWS, samples), 0) & 31
    twice = jnp.where(
        double == lax.broadcasted_iota(jnp.int32, (SLOT_ROWS, samples), 1), 1.0, 0.0
    ).astype(bf16)
    router_twice[...] = jnp.dot(twice, router_ref[...], preferred_element_type=f32).astype(bf16)

    wait_for(attended, a_sem.at[1])

    def norm_rows(step, carry):
        rows = rows_of(step, 16)
        heads = jnp.concatenate([attended[head, rows, :] for head in range(PLANE)], axis=1)
        value = stream_ref[rows, :].astype(f32) + token_mod[rows, :width] * heads.astype(f32)
        residual[rows, :] = value
        average = jnp.mean(value, axis=1, keepdims=True)
        centered = value - average
        variance = jnp.mean(centered * centered, axis=1, keepdims=True)
        shift = token_mod[rows, width : 2 * width]
        scale = token_mod[rows, 2 * width : 3 * width]
        normed[rows, :] = (centered * lax.rsqrt(variance + EPS) * (1.0 + scale) + shift).astype(bf16)
        return carry

    lax.fori_loop(0, tokens // 16, norm_rows, 0)

    def plane_send(source, target, sems, half):
        place = target.at[half, rows_of(seq_index, 16)]
        for peer in partners(seq_index, OFFSETS):
            plane_copy(
                source.at[half, rows_of(peer, 16)], place, sems.at[half, 0], sems.at[half, 1], peer
            ).start()
        pltpu.make_async_copy(
            source.at[half, rows_of(seq_index, 16)], place, sems.at[half, 1]
        ).start()

    for half in range(2):
        stacked = jnp.concatenate(
            [
                normed[:, half * HALF + piece * TILE : half * HALF + (piece + 1) * TILE]
                for piece in range(PIECES)
            ],
            axis=0,
        )
        outgoing[half] = jnp.dot(pick[...], stacked, preferred_element_type=f32).astype(bf16)
        plane_send(outgoing, landed, d_sem, half)

    logits = lax.dot_general(
        normed[...], router_twice[...], (((1,), (1,)), ((), ())), preferred_element_type=f32
    )
    place = lax.broadcasted_iota(jnp.int32, (tokens, SLOT_ROWS), 0).astype(f32) == chosen
    weighted = jnp.where(place, 1.0 / (1.0 + jnp.exp(-logits)), 0.0)
    lax.fori_loop(3 * width // 512, 4 * width // 512, spread_mod, 0)
    weight_first = weighted.astype(bf16)
    weight_rest = weighted - weight_first.astype(f32)
    weight_second = weight_rest.astype(bf16)
    weight_third = (weight_rest - weight_second.astype(f32)).astype(bf16)
    weight_parts = jnp.concatenate([weight_first, weight_second, weight_third], axis=1)

    def line_up(which, half):
        lined[which * SLOT_ROWS : (which + 1) * SLOT_ROWS, half * HALF : (half + 1) * HALF] = (
            jnp.concatenate(
                [
                    gathered[which, half, piece * SLOT_ROWS : (piece + 1) * SLOT_ROWS, :]
                    for piece in range(PIECES)
                ],
                axis=1,
            )
        )

    ring_copies = []
    for half in range(2):
        wait_for(landed.at[half], d_sem.at[half, 1])
        gathered[0, half] = jnp.dot(
            unmix[...], landed[half], preferred_element_type=f32
        ).astype(bf16)
        to_right = ring_copy(
            gathered.at[0, half], gathered.at[2, half], z_send.at[half], z_recv.at[half], right
        )
        to_right.start()
        to_left = ring_copy(
            gathered.at[0, half],
            gathered.at[3, half],
            z_send.at[2 + half],
            z_recv.at[2 + half],
            left,
        )
        to_left.start()
        ring_copies += [to_right, to_left]
        line_up(0, half)
    own_right_0, own_left_0, own_right_1, own_left_1 = ring_copies
    own_right_0.wait_recv()
    on_right_0 = ring_copy(
        gathered.at[2, 0], gathered.at[1, 0], z_send.at[4], z_recv.at[4], right
    )
    on_right_0.start()
    own_left_1.wait_recv()
    on_left_1 = ring_copy(gathered.at[3, 1], gathered.at[1, 1], z_send.at[5], z_recv.at[5], left)
    on_left_1.start()
    line_up(2, 0)
    line_up(3, 1)
    load_first.wait()
    load_second.wait()

    def first_product(base):
        rows = slice(base, base + 2 * SLOT_ROWS)

        def columns_of(step, carry):
            columns = rows_of(step, 256)
            product = jnp.dot(lined[rows, :], w_first[:, columns], preferred_element_type=f32)
            hidden[rows, columns] = jax.nn.gelu(product, approximate=True).astype(bf16)
            return carry

        lax.fori_loop(0, w_first.shape[1] // 256, columns_of, 0)

    def second_product(base, half, lower, upper):
        rows = slice(base, base + 2 * SLOT_ROWS)

        def columns_of(step, carry):
            columns = rows_of(step, 256)
            product = jnp.dot(
                hidden[rows, :],
                w_second[:, rows_of(step + half * (HALF // 256), 256)],
                preferred_element_type=f32,
            )
            lower[:, columns] = product[:SLOT_ROWS].astype(lower.dtype)
            upper[:, columns] = product[SLOT_ROWS:].astype(upper.dtype)
            return carry

        lax.fori_loop(0, HALF // 256, columns_of, 0)

    own_left_0.wait_recv()
    line_up(3, 0)
    own_right_1.wait_recv()
    line_up(2, 1)
    first_product(2 * SLOT_ROWS)
    second_product(2 * SLOT_ROWS, 0, side_raw.at[0], held.at[0])
    raw_left = ring_copy(side_raw.at[0], raw_in.at[0], r_send.at[2], r_recv.at[2], left)
    raw_left.start()
    second_product(2 * SLOT_ROWS, 1, held.at[1], side_raw.at[1])
    raw_right = ring_copy(side_raw.at[1], raw_in.at[1], r_send.at[3], r_recv.at[3], right)
    raw_right.start()
    on_right_0.wait_recv()
    line_up(1, 0)
    on_left_1.wait_recv()
    line_up(1, 1)
    first_product(0)
    second_product(0, 0, own_total.at[0], far_out.at[0])
    far_right = ring_copy(far_out.at[0], far_in.at[0], r_send.at[0], r_recv.at[0], right)
    far_right.start()
    second_product(0, 1, own_total.at[1], far_out.at[1])
    far_left = ring_copy(far_out.at[1], far_in.at[1], r_send.at[1], r_recv.at[1], left)
    far_left.start()
    far_right.wait_recv()
    side_sum[0] = (held[0] + far_in[0].astype(f32)).astype(bf16)
    sum_right = ring_copy(side_sum.at[0], sum_in.at[0], r_send.at[4], r_recv.at[4], right)
    sum_right.start()
    far_left.wait_recv()
    side_sum[1] = (held[1] + far_in[1].astype(f32)).astype(bf16)
    sum_left = ring_copy(side_sum.at[1], sum_in.at[1], r_send.at[5], r_recv.at[5], left)
    sum_left.start()

    for half, raw, summed in ((0, raw_left, sum_right), (1, raw_right, sum_left)):
        raw.wait_recv()
        summed.wait_recv()
        total = (
            own_total[half] + raw_in[half].astype(f32) + sum_in[half].astype(f32)
        ).astype(bf16)
        stacked = jnp.concatenate(
            [total[:, piece * TILE : (piece + 1) * TILE] for piece in range(PIECES)], axis=0
        )
        homeward[half] = jnp.dot(mix[...], stacked, preferred_element_type=f32).astype(bf16)
        plane_send(homeward, back, b_sem, half)

    for half in range(2):
        wait_for(back.at[half], b_sem.at[half, 1])
        ordered = jnp.dot(unmix[...], back[half], preferred_element_type=f32).astype(bf16)
        for piece in range(PIECES):
            rows = ordered[piece * SLOT_ROWS : (piece + 1) * SLOT_ROWS, :]
            begin = half * HALF + piece * TILE
            columns = slice(begin, begin + TILE)
            expert_sum = jnp.dot(
                weight_parts, jnp.concatenate([rows, rows, rows], axis=0), preferred_element_type=f32
            )
            gate = token_mod[:, 3 * width + begin : 3 * width + begin + TILE]
            out_ref[:, columns] = (residual[:, columns] + gate * expert_sum).astype(bf16)

    wait_for(attended.at[pl.ds(0, PLANE - 1)], a_sem.at[0])
    for half in range(2):
        wait_for(landed.at[half, pl.ds(0, 16 * (PLANE - 1))], d_sem.at[half, 0])
        wait_for(back.at[half, pl.ds(0, 16 * (PLANE - 1))], b_sem.at[half, 0])
    for copy in (
        own_right_0,
        own_left_1,
        on_right_0,
        on_left_1,
        own_right_1,
        own_left_0,
        far_right,
        far_left,
        raw_left,
        raw_right,
        sum_right,
        sum_left,
    ):
        copy.wait_send()


def feed_forward(
    attended_head, stream, modulation, expert_in, expert_out, query_tags, picks, used, router
):
    tokens, width = stream.shape
    bf16 = jnp.bfloat16
    f32 = jnp.float32
    part = expert_in.shape[2]
    block = PIECES * SLOT_ROWS
    anywhere = pl.BlockSpec(memory_space=pl.ANY)
    inside = pl.BlockSpec(memory_space=pltpu.VMEM)
    dma = pltpu.SemaphoreType.DMA
    return pl.pallas_call(
        experts_kernel,
        out_shape=jax.ShapeDtypeStruct((tokens, width), bf16),
        in_specs=[anywhere] * 6 + [inside] * 3,
        out_specs=inside,
        scratch_shapes=[
            pltpu.VMEM((tokens, width), bf16),
            pltpu.VMEM(modulation.shape, bf16),
            pltpu.VMEM((tokens, width // PLANE), bf16),
            pltpu.VMEM((width, part), bf16),
            pltpu.VMEM((part, width), bf16),
            pltpu.VMEM((PLANE, tokens, width // PLANE), bf16),
            pltpu.VMEM((tokens, 4 * width), f32),
            pltpu.VMEM((tokens, width), f32),
            pltpu.VMEM((tokens, width), bf16),
            pltpu.VMEM((block, PIECES * tokens), bf16),
            pltpu.VMEM((block, block), bf16),
            pltpu.VMEM((block, block), bf16),
            pltpu.VMEM((2, block, TILE), bf16),
            pltpu.VMEM((2, block, TILE), bf16),
            pltpu.VMEM((4, 2, block, TILE), bf16),
            pltpu.VMEM((4 * SLOT_ROWS, width), bf16),
            pltpu.VMEM((4 * SLOT_ROWS, part), bf16),
            pltpu.VMEM((2, SLOT_ROWS, HALF), bf16),
            pltpu.VMEM((2, SLOT_ROWS, HALF), bf16),
            pltpu.VMEM((2, SLOT_ROWS, HALF), bf16),
            pltpu.VMEM((2, SLOT_ROWS, HALF), bf16),
            pltpu.VMEM((2, SLOT_ROWS, HALF), bf16),
            pltpu.VMEM((2, SLOT_ROWS, HALF), bf16),
            pltpu.VMEM((2, SLOT_ROWS, HALF), f32),
            pltpu.VMEM((2, SLOT_ROWS, HALF), f32),
            pltpu.VMEM((2, block, TILE), bf16),
            pltpu.VMEM((2, block, TILE), bf16),
            pltpu.VMEM((SLOT_ROWS, width), bf16),
            dma((6,)),
            dma((2,)),
            dma((2, 2)),
            dma((6,)),
            dma((6,)),
            dma((6,)),
            dma((6,)),
            dma((2, 2)),
        ],
        compiler_params=pltpu.CompilerParams(
            collective_id=1, has_side_effects=True, vmem_limit_bytes=58 * 2**20
        ),
        name="experts",
    )(
        attended_head,
        stream,
        modulation,
        expert_in,
        expert_out,
        query_tags,
        picks,
        used,
        router,
    )


def on_device(
    stream,
    query_input,
    key_input,
    value_input,
    sample_id,
    timestep,
    class_id,
    class_table,
    mod_weight,
    router_weight,
    expert_in,
    expert_out,
    picked,
    counts,
):
    head_query, keys, values, query_tags, key_tags, modulation, spans = exchange(
        query_input,
        key_input,
        value_input,
        mod_weight,
        class_table,
        class_id,
        timestep,
        sample_id,
    )
    attended_head = local_attention(spans, head_query, query_tags, keys, key_tags, values)
    return feed_forward(
        attended_head,
        stream,
        modulation,
        expert_in,
        expert_out,
        query_tags,
        picked[:, 0, :].T,
        counts.T,
        router_weight.T,
    )


def solution(mesh):
    return jax.shard_map(
        on_device,
        mesh=mesh,
        in_specs=(
            P(("exp", "seq"), None),
            P(("exp", "seq"), None),
            P(("exp", "seq"), None),
            P(("exp", "seq"), None),
            P(),
            P(),
            P(),
            P(None, "seq"),
            P(None, ("seq", "exp")),
            P(),
            P("seq", None, "exp"),
            P("seq", "exp", None),
            P(None, ("exp", "seq"), None),
            P(None, ("exp", "seq")),
        ),
        out_specs=P(("exp", "seq"), None),
        check_vma=False,
    )
```

```python
import math

import jax
import jax.numpy as jnp
from jax import lax
from jax.experimental import pallas as pl
from jax.experimental.pallas import tpu as pltpu
from jax.sharding import PartitionSpec as P

MOST = 1024


EPS = 1e-06


Q_ROWS = 512
KEY_STEP = 256
FAR = 32768.0


def attention_kernel(spans, q_ref, fq_ref, k_ref, fk_ref, v_ref, out_ref):
    step = pl.program_id(0)
    start = spans[0, step]
    parts = spans[1, step]
    head_width = q_ref.shape[1]
    factor = math.log2(math.e) / math.sqrt(head_width)
    least_parts = Q_ROWS // KEY_STEP
    most_parts = (2 * MOST + Q_ROWS) // KEY_STEP + 1

    def with_parts(number):
        span = number * KEY_STEP

        @pl.when(parts == number)
        def _():
            first = pl.multiple_of(jnp.minimum(start, k_ref.shape[0] - span), 128)
            rows = pl.ds(first, span)
            keys = jnp.concatenate([k_ref[rows, :], fk_ref[rows, :]], axis=1)
            values = jnp.concatenate(
                [v_ref[rows, :], jnp.ones((span, head_width), jnp.bfloat16)], axis=1
            )
            for line in range(0, Q_ROWS, KEY_STEP):
                lines = slice(line, line + KEY_STEP)
                query = jnp.concatenate([q_ref[lines, :], fq_ref[lines, :]], axis=1)
                scores = lax.dot_general(
                    query, keys, (((1,), (1,)), ((), ())), preferred_element_type=jnp.float32
                )
                highest = jnp.max(scores, axis=1, keepdims=True)
                numer = jnp.exp2((scores - highest) * factor).astype(jnp.bfloat16)
                total = jnp.dot(numer, values, preferred_element_type=jnp.float32)
                out_ref[lines, :] = (total[:, :head_width] / total[:, head_width:]).astype(
                    jnp.bfloat16
                )

    for number in range(least_parts, most_parts + 1):
        with_parts(number)


def local_attention(spans, head_query, query_tags, keys, key_tags, values):
    group, head_width = head_query.shape
    extent = keys.shape[0]
    blocks = group // Q_ROWS
    whole = lambda step, spans: (0, 0)
    part = lambda step, spans: (step, 0)
    return pl.pallas_call(
        attention_kernel,
        grid_spec=pltpu.PrefetchScalarGridSpec(
            num_scalar_prefetch=1,
            grid=(blocks,),
            in_specs=[
                pl.BlockSpec((Q_ROWS, head_width), part),
                pl.BlockSpec((Q_ROWS, head_width), part),
                pl.BlockSpec((extent, head_width), whole),
                pl.BlockSpec((extent, head_width), whole),
                pl.BlockSpec((extent, head_width), whole),
            ],
            out_specs=pl.BlockSpec((Q_ROWS, head_width), part),
        ),
        out_shape=jax.ShapeDtypeStruct((group, head_width), jnp.bfloat16),
        compiler_params=pltpu.CompilerParams(vmem_limit_bytes=60 * 2**20),
        name="attention",
    )(spans, head_query, query_tags, keys, key_tags, values)


MESH = pl.DeviceIdType.MESH
PLANE = 32
TILE = 256
PIECES = 8
HALF = TILE * PIECES
SLOT_ROWS = 64


OFFSETS = [(number * 5) % PLANE for number in range(1, PLANE)]


def mirrored(offset):
    other = (0, 3, 2, 1)
    return other[offset // 8] * 8 + other[offset // 2 % 4] * 2 + offset % 2


def partners(seq_index, offsets):
    core = seq_index % 2
    return [
        seq_index ^ (offset + core * (mirrored(offset) - offset)) for offset in offsets
    ]


def greet(seq_index, exp_index, ring):
    barrier = pltpu.get_barrier_semaphore()
    for offset in OFFSETS:
        pl.semaphore_signal(
            barrier,
            inc=1,
            device_id=(seq_index ^ offset, exp_index),
            device_id_type=MESH,
        )
    for other in ring:
        pl.semaphore_signal(barrier, inc=1, device_id=(seq_index, other), device_id_type=MESH)
    pl.semaphore_wait(barrier, PLANE - 1 + len(ring))


def wait_for(part, semaphore):
    pltpu.make_async_copy(part, part, semaphore).wait()


def rows_of(number, size):
    return pl.ds(pl.multiple_of(number * size, size), size)


def exchange_kernel(
    query_in,
    key_in,
    value_in,
    weight_in,
    class_table_ref,
    class_id_ref,
    timestep_ref,
    ids_ref,
    query_out,
    key_out,
    value_out,
    query_tags_out,
    key_tags_out,
    modulation_out,
    spans_out,
    own_condition,
    conditions,
    weight,
    own_modulation,
    query_tags,
    key_tags,
    local_sem,
    c_sem,
    p_send,
    p_recv,
    h_send,
    h_recv,
    m_send,
    m_recv,
):
    seq_index = lax.axis_index("seq")
    exp_index = lax.axis_index("exp")
    tokens = query_in.shape[0]
    group, head_width = query_out.shape
    at_y = seq_index // 8
    at_x = seq_index // 2 % 4
    core = seq_index % 2
    f32 = jnp.float32
    bf16 = jnp.bfloat16

    greet(seq_index, exp_index, [(exp_index + step) % 4 for step in (1, 2, 3)])

    def copy_to(source, target, send, recv, peer, other):
        return pltpu.make_async_remote_copy(
            src_ref=source,
            dst_ref=target,
            send_sem=send,
            recv_sem=recv,
            device_id=(peer, other),
            device_id_type=MESH,
        )

    arrays = ((key_in, key_out, MOST), (value_in, value_out, MOST), (query_in, query_out, 0))

    def send_heads(which, part):
        source, target, before = arrays[which]
        place = target.at[pl.ds(pl.multiple_of(before + seq_index * tokens, tokens), tokens)]
        for peer in partners(seq_index, OFFSETS[15:] if part else OFFSETS[:15]):
            copy_to(
                source.at[:, rows_of(peer, head_width)],
                place,
                p_send.at[which],
                p_recv.at[which],
                peer,
                exp_index,
            ).start()
        if part == 0:
            pltpu.make_async_copy(
                source.at[:, rows_of(seq_index, head_width)], place, p_recv.at[which]
            ).start()

    def wait_heads(which):
        _, target, before = arrays[which]
        wait_for(target.at[pl.ds(before, group)], p_recv.at[which])

    def halo_copies(which):
        target = arrays[which][1]
        return (
            copy_to(
                target.at[pl.ds(MOST, MOST)],
                target.at[pl.ds(MOST + group, MOST)],
                h_send.at[which, 0],
                h_recv.at[which, 0],
                seq_index,
                (exp_index + 3) % 4,
            ),
            copy_to(
                target.at[pl.ds(group, MOST)],
                target.at[pl.ds(0, MOST)],
                h_send.at[which, 1],
                h_recv.at[which, 1],
                seq_index,
                (exp_index + 1) % 4,
            ),
        )

    slot = ((core * 4 + exp_index) * 4 + at_y) * 4 + at_x

    def modulation_copies(phase):
        if phase == 0:
            source, target = own_modulation, modulation_out.at[slot]
            places = [((at_y * 4 + (at_x + d) % 4) * 2 + core, exp_index) for d in (1, 2, 3)]
        elif phase == 1:
            source = modulation_out.at[rows_of(slot // 4, 4)]
            target = source
            places = [((((at_y + d) % 4) * 4 + at_x) * 2 + core, exp_index) for d in (1, 2, 3)]
        else:
            source = modulation_out.at[rows_of(slot // 16, 16)]
            target = source
            places = [(seq_index, (exp_index + d) % 4) for d in (1, 2, 3)]
        return [
            copy_to(source, target, m_send.at[phase, i], m_recv.at[phase, i], peer, other)
            for i, (peer, other) in enumerate(places)
        ]

    def send_modulation(phase):
        for copy in modulation_copies(phase):
            copy.start()

    def wait_modulation(phase):
        for copy in modulation_copies(phase):
            copy.wait_recv()

    send_heads(0, 0)
    load_weight = pltpu.make_async_copy(weight_in, weight, local_sem.at[0])
    load_weight.start()

    samples = timestep_ref.shape[1]
    diagonal = lax.broadcasted_iota(jnp.int32, (samples, samples), 0) == lax.broadcasted_iota(
        jnp.int32, (samples, samples), 1
    )

    def upright(row):
        return jnp.sum(jnp.where(diagonal, row.astype(f32), 0.0), axis=1, keepdims=True)

    classes = class_table_ref.shape[0]
    chosen_class = jnp.where(
        lax.broadcasted_iota(jnp.int32, (samples, classes), 1).astype(f32)
        == upright(class_id_ref[...]),
        1.0,
        0.0,
    ).astype(bf16)
    table_rows = jnp.dot(chosen_class, class_table_ref[...], preferred_element_type=f32)
    half_columns = PLANE * head_width // 2
    column = seq_index * head_width + lax.broadcasted_iota(jnp.int32, (1, head_width), 1)
    freq_index = jnp.where(column < half_columns, column, column - half_columns).astype(f32)
    frequency = jnp.exp(-math.log(10000.0) * freq_index / half_columns)
    angles = upright(timestep_ref[...]) * frequency
    embedded = jnp.where(column < half_columns, jnp.cos(angles), jnp.sin(angles))
    value = embedded + table_rows
    own_condition[...] = (value / (1.0 + jnp.exp(-value))).astype(bf16)

    for peer in partners(seq_index, OFFSETS):
        copy_to(
            own_condition,
            conditions.at[seq_index],
            c_sem.at[0],
            c_sem.at[1],
            peer,
            exp_index,
        ).start()
    pltpu.make_async_copy(own_condition, conditions.at[seq_index], c_sem.at[1]).start()
    send_heads(0, 1)
    wait_for(conditions, c_sem.at[1])
    load_weight.wait()
    condition = jnp.concatenate([conditions[place] for place in range(PLANE)], axis=1)
    own_modulation[...] = jnp.dot(condition, weight[...], preferred_element_type=f32).astype(bf16)
    keep = pltpu.make_async_copy(own_modulation, modulation_out.at[slot], local_sem.at[4])
    keep.start()
    send_modulation(0)
    send_heads(1, 0)

    ids = ids_ref[...]
    lane = lax.broadcasted_iota(jnp.int32, (1, head_width), 1)

    def total(mask):
        return jnp.sum(
            jnp.sum(jnp.where(mask, 1.0, 0.0), axis=0, keepdims=True), axis=1, keepdims=True
        )

    begins = jnp.zeros((1, head_width), f32)
    ends = jnp.zeros((1, head_width), f32)
    for image in range(32):
        begins = begins + jnp.where(lane == image, total(ids < image), 0.0)
        ends = ends + jnp.where(lane == image, total(ids <= image), 0.0)
    begins = begins.astype(jnp.int32)
    ends = ends.astype(jnp.int32)
    first_token = exp_index * group

    def tag_rows(step, carry):
        rows = rows_of(step, Q_ROWS)
        shape = (Q_ROWS, head_width)
        place = lax.broadcasted_iota(jnp.int32, shape, 0) + (first_token - MOST + step * Q_ROWS)
        same = (place >= begins) & (place < ends)
        key_tags[rows, :] = jnp.where(same, 0.0, -FAR).astype(bf16)
        return carry

    def query_tag_rows(step, carry):
        rows = rows_of(step, Q_ROWS)
        shape = (Q_ROWS, head_width)
        place = lax.broadcasted_iota(jnp.int32, shape, 0) + (first_token + step * Q_ROWS)
        same = (place >= begins) & (place < ends)
        query_tags[rows, :] = jnp.where(same, 1.0, 0.0).astype(bf16)
        return carry

    lax.fori_loop(0, key_tags.shape[0] // Q_ROWS, tag_rows, 0)
    lax.fori_loop(0, group // Q_ROWS, query_tag_rows, 0)
    keep_key_tags = pltpu.make_async_copy(key_tags, key_tags_out, local_sem.at[5])
    keep_key_tags.start()
    keep_query_tags = pltpu.make_async_copy(query_tags, query_tags_out, local_sem.at[6])
    keep_query_tags.start()

    keep.wait()
    wait_modulation(0)
    send_modulation(1)
    send_heads(1, 1)
    wait_heads(0)
    for copy in halo_copies(0):
        copy.start()
    send_heads(2, 0)
    wait_modulation(1)
    send_modulation(2)

    low = jnp.zeros((1, head_width), f32)
    high = jnp.zeros((1, head_width), f32)
    for block in range(group // Q_ROWS):
        line = exp_index * (group // 128) + block * (Q_ROWS // 128)
        first = ids_ref[pl.ds(line, 1), 0:1]
        last = ids_ref[pl.ds(line + Q_ROWS // 128 - 1, 1), 127:128]
        low = low + jnp.where(lane == block, total(ids < first), 0.0)
        high = high + jnp.where(lane == block, total(ids <= last), 0.0)
    low = (low.astype(jnp.int32) - first_token + MOST) & ~127
    high = high.astype(jnp.int32) - first_token + MOST
    parts = jnp.maximum((high - low + KEY_STEP - 1) // KEY_STEP, Q_ROWS // KEY_STEP)
    spans_out[...] = jnp.where(
        lax.broadcasted_iota(jnp.int32, spans_out.shape, 0) == 0, low, parts
    )

    wait_heads(1)
    for copy in halo_copies(1):
        copy.start()
    send_heads(2, 1)
    wait_heads(2)
    wait_modulation(2)
    keep_key_tags.wait()
    keep_query_tags.wait()
    for which in range(2):
        for copy in halo_copies(which):
            copy.wait_recv()
    wait_for(conditions.at[pl.ds(0, PLANE - 1)], c_sem.at[0])
    for which in range(3):
        wait_for(query_out.at[pl.ds(0, group - tokens)], p_send.at[which])
    for which in range(2):
        for copy in halo_copies(which):
            copy.wait_send()
    for phase in range(3):
        for copy in modulation_copies(phase):
            copy.wait_send()


def exchange(
    query_input, key_input, value_input, mod_weight, class_table, class_id, timestep, sample_id
):
    tokens, width = query_input.shape
    head_width = width // PLANE
    group = tokens * PLANE
    extent = group + 2 * MOST
    bf16 = jnp.bfloat16
    samples = class_id.shape[0]
    anywhere = pl.BlockSpec(memory_space=pl.ANY)
    inside = pl.BlockSpec(memory_space=pltpu.VMEM)
    dma = pltpu.SemaphoreType.DMA
    return pl.pallas_call(
        exchange_kernel,
        out_shape=(
            jax.ShapeDtypeStruct((group, head_width), bf16),
            jax.ShapeDtypeStruct((extent, head_width), bf16),
            jax.ShapeDtypeStruct((extent, head_width), bf16),
            jax.ShapeDtypeStruct((group, head_width), bf16),
            jax.ShapeDtypeStruct((extent, head_width), bf16),
            jax.ShapeDtypeStruct((4 * PLANE, samples, mod_weight.shape[1]), bf16),
            jax.ShapeDtypeStruct((8, head_width), jnp.int32),
        ),
        in_specs=[anywhere] * 4 + [inside] * 4,
        out_specs=(anywhere,) * 6 + (inside,),
        scratch_shapes=[
            pltpu.VMEM((samples, head_width), bf16),
            pltpu.VMEM((PLANE, samples, head_width), bf16),
            pltpu.VMEM(mod_weight.shape, bf16),
            pltpu.VMEM((samples, mod_weight.shape[1]), bf16),
            pltpu.VMEM((group, head_width), bf16),
            pltpu.VMEM((extent, head_width), bf16),
            dma((7,)),
            dma((2,)),
            dma((3,)),
            dma((3,)),
            dma((2, 2)),
            dma((2, 2)),
            dma((3, 3)),
            dma((3, 3)),
        ],
        compiler_params=pltpu.CompilerParams(
            collective_id=0, has_side_effects=True, vmem_limit_bytes=60 * 2**20
        ),
        name="exchange",
    )(
        query_input,
        key_input,
        value_input,
        mod_weight,
        class_table,
        class_id.reshape(1, -1),
        timestep.reshape(1, -1),
        sample_id.reshape(-1, head_width),
    )


def experts_kernel(
    attended_ref,
    stream_in,
    modulation_in,
    w_first_in,
    w_second_in,
    tags_in,
    picks_ref,
    used_ref,
    router_ref,
    out_ref,
    stream_ref,
    modulation_ref,
    selector_ref,
    w_first,
    w_second,
    attended,
    token_mod,
    residual,
    normed,
    pick,
    unmix,
    mix,
    outgoing,
    landed,
    gathered,
    lined,
    hidden,
    far_out,
    far_in,
    side_raw,
    side_sum,
    raw_in,
    sum_in,
    held,
    own_total,
    homeward,
    back,
    router_twice,
    local_sem,
    s_sem,
    a_sem,
    d_sem,
    z_send,
    z_recv,
    r_send,
    r_recv,
    b_sem,
):
    seq_index = lax.axis_index("seq")
    exp_index = lax.axis_index("exp")
    right = (exp_index + 1) % 4
    left = (exp_index + 3) % 4
    width = stream_ref.shape[1]
    tokens = stream_ref.shape[0]
    f32 = jnp.float32
    bf16 = jnp.bfloat16

    greet(seq_index, exp_index, (left, right))

    def plane_copy(source, target, send, recv, peer):
        return pltpu.make_async_remote_copy(
            src_ref=source,
            dst_ref=target,
            send_sem=send,
            recv_sem=recv,
            device_id=(peer, exp_index),
            device_id_type=MESH,
        )

    def ring_copy(source, target, send, recv, other):
        return pltpu.make_async_remote_copy(
            src_ref=source,
            dst_ref=target,
            send_sem=send,
            recv_sem=recv,
            device_id=(seq_index, other),
            device_id_type=MESH,
        )

    own_half = rows_of(seq_index % 2, modulation_ref.shape[0] // 2)
    load_mod = pltpu.make_async_copy(
        modulation_in.at[own_half], modulation_ref.at[own_half], local_sem.at[1]
    )
    load_mod.start()
    share_mod = plane_copy(
        modulation_in.at[own_half],
        modulation_ref.at[own_half],
        s_sem.at[0],
        s_sem.at[1],
        seq_index ^ 1,
    )
    share_mod.start()
    for peer in partners(seq_index, OFFSETS):
        plane_copy(
            attended_ref.at[rows_of(peer, tokens)],
            attended.at[seq_index],
            a_sem.at[0],
            a_sem.at[1],
            peer,
        ).start()
    pltpu.make_async_copy(
        attended_ref.at[rows_of(seq_index, tokens)], attended.at[seq_index], a_sem.at[1]
    ).start()
    load_stream = pltpu.make_async_copy(stream_in, stream_ref, local_sem.at[2])
    load_stream.start()
    load_tags = pltpu.make_async_copy(
        tags_in.at[rows_of(seq_index, tokens)], selector_ref, local_sem.at[5]
    )
    load_tags.start()
    load_first = pltpu.make_async_copy(w_first_in.at[0], w_first, local_sem.at[3])
    load_first.start()
    load_second = pltpu.make_async_copy(w_second_in.at[0], w_second, local_sem.at[4])
    load_second.start()

    count = PIECES * SLOT_ROWS
    row = lax.broadcasted_iota(jnp.int32, (count, count), 0)
    column = lax.broadcasted_iota(jnp.int32, (count, count), 1)
    by_source = (row & 31) * 16 + (row >> 6) * 2 + ((row >> 5) & 1)
    unmix[...] = jnp.where(by_source == column, 1.0, 0.0).astype(bf16)
    by_piece = ((row >> 1) & 7) * SLOT_ROWS + (row & 1) * PLANE + (row >> 4)
    mix[...] = jnp.where(by_piece == column, 1.0, 0.0).astype(bf16)
    column = lax.broadcasted_iota(jnp.int32, pick.shape, 1)
    used = used_ref[...]
    chosen = jnp.concatenate(
        [
            jnp.where(used > 0, picks_ref[0:1, :], -1),
            jnp.where(used > 1, picks_ref[1:2, :], -1),
        ],
        axis=1,
    ).astype(f32)
    row = lax.broadcasted_iota(jnp.int32, (count, SLOT_ROWS), 0)
    slot = lax.broadcasted_iota(jnp.int32, (count, SLOT_ROWS), 1)
    mine = slot == (row & 1) * PLANE + (row >> 4)
    token = jnp.sum(jnp.where(mine, chosen, 0.0), axis=1, keepdims=True)
    piece = (lax.broadcasted_iota(jnp.int32, (count, 1), 0) >> 1) & 7
    target = jnp.where(token < 0.0, -1.0, token + (piece * tokens).astype(f32))
    pick[...] = jnp.where(column.astype(f32) == target, 1.0, 0.0).astype(bf16)

    load_mod.wait()
    share_mod.wait_recv()
    load_stream.wait()

    load_tags.wait()
    samples = modulation_ref.shape[1]

    def spread_mod(step, carry):
        base = (step % 2 * 16 + step // 8) * 4 + step // 2 % 4
        whole = jnp.concatenate([modulation_ref[base + 16 * part] for part in range(4)], axis=1)
        token_mod[:, rows_of(step, 512)] = jnp.dot(
            selector_ref[:, :samples], whole, preferred_element_type=f32
        )
        return carry

    lax.fori_loop(0, 3 * width // 512, spread_mod, 0)

    double = lax.broadcasted_iota(jnp.int32, (SLOT_ROWS, samples), 0) & 31
    twice = jnp.where(
        double == lax.broadcasted_iota(jnp.int32, (SLOT_ROWS, samples), 1), 1.0, 0.0
    ).astype(bf16)
    router_twice[...] = jnp.dot(twice, router_ref[...], preferred_element_type=f32).astype(bf16)

    wait_for(attended, a_sem.at[1])

    def norm_rows(step, carry):
        rows = rows_of(step, 16)
        heads = jnp.concatenate([attended[head, rows, :] for head in range(PLANE)], axis=1)
        value = stream_ref[rows, :].astype(f32) + token_mod[rows, :width] * heads.astype(f32)
        residual[rows, :] = value
        average = jnp.mean(value, axis=1, keepdims=True)
        centered = value - average
        variance = jnp.mean(centered * centered, axis=1, keepdims=True)
        shift = token_mod[rows, width : 2 * width]
        scale = token_mod[rows, 2 * width : 3 * width]
        normed[rows, :] = (centered * lax.rsqrt(variance + EPS) * (1.0 + scale) + shift).astype(bf16)
        return carry

    lax.fori_loop(0, tokens // 16, norm_rows, 0)

    def plane_send(source, target, sems, half):
        place = target.at[half, rows_of(seq_index, 16)]
        for peer in partners(seq_index, OFFSETS):
            plane_copy(
                source.at[half, rows_of(peer, 16)], place, sems.at[half, 0], sems.at[half, 1], peer
            ).start()
        pltpu.make_async_copy(
            source.at[half, rows_of(seq_index, 16)], place, sems.at[half, 1]
        ).start()

    for half in range(2):
        stacked = jnp.concatenate(
            [
                normed[:, half * HALF + piece * TILE : half * HALF + (piece + 1) * TILE]
                for piece in range(PIECES)
            ],
            axis=0,
        )
        outgoing[half] = jnp.dot(pick[...], stacked, preferred_element_type=f32).astype(bf16)
        plane_send(outgoing, landed, d_sem, half)

    logits = lax.dot_general(
        normed[...], router_twice[...], (((1,), (1,)), ((), ())), preferred_element_type=f32
    )
    place = lax.broadcasted_iota(jnp.int32, (tokens, SLOT_ROWS), 0).astype(f32) == chosen
    weighted = jnp.where(place, 1.0 / (1.0 + jnp.exp(-logits)), 0.0)
    lax.fori_loop(3 * width // 512, 4 * width // 512, spread_mod, 0)
    weight_first = weighted.astype(bf16)
    weight_rest = weighted - weight_first.astype(f32)
    weight_second = weight_rest.astype(bf16)
    weight_third = (weight_rest - weight_second.astype(f32)).astype(bf16)
    weight_parts = jnp.concatenate([weight_first, weight_second, weight_third], axis=1)

    def line_up(which, half):
        lined[which * SLOT_ROWS : (which + 1) * SLOT_ROWS, half * HALF : (half + 1) * HALF] = (
            jnp.concatenate(
                [
                    gathered[which, half, piece * SLOT_ROWS : (piece + 1) * SLOT_ROWS, :]
                    for piece in range(PIECES)
                ],
                axis=1,
            )
        )

    ring_copies = []
    for half in range(2):
        wait_for(landed.at[half], d_sem.at[half, 1])
        gathered[0, half] = jnp.dot(
            unmix[...], landed[half], preferred_element_type=f32
        ).astype(bf16)
        to_right = ring_copy(
            gathered.at[0, half], gathered.at[2, half], z_send.at[half], z_recv.at[half], right
        )
        to_right.start()
        to_left = ring_copy(
            gathered.at[0, half],
            gathered.at[3, half],
            z_send.at[2 + half],
            z_recv.at[2 + half],
            left,
        )
        to_left.start()
        ring_copies += [to_right, to_left]
        line_up(0, half)
    own_right_0, own_left_0, own_right_1, own_left_1 = ring_copies
    own_right_0.wait_recv()
    on_right_0 = ring_copy(
        gathered.at[2, 0], gathered.at[1, 0], z_send.at[4], z_recv.at[4], right
    )
    on_right_0.start()
    own_left_1.wait_recv()
    on_left_1 = ring_copy(gathered.at[3, 1], gathered.at[1, 1], z_send.at[5], z_recv.at[5], left)
    on_left_1.start()
    line_up(2, 0)
    line_up(3, 1)
    load_first.wait()
    load_second.wait()

    def first_product(base):
        rows = slice(base, base + 2 * SLOT_ROWS)

        def columns_of(step, carry):
            columns = rows_of(step, 256)
            product = jnp.dot(lined[rows, :], w_first[:, columns], preferred_element_type=f32)
            hidden[rows, columns] = jax.nn.gelu(product, approximate=True).astype(bf16)
            return carry

        lax.fori_loop(0, w_first.shape[1] // 256, columns_of, 0)

    def second_product(base, half, lower, upper):
        rows = slice(base, base + 2 * SLOT_ROWS)

        def columns_of(step, carry):
            columns = rows_of(step, 256)
            product = jnp.dot(
                hidden[rows, :],
                w_second[:, rows_of(step + half * (HALF // 256), 256)],
                preferred_element_type=f32,
            )
            lower[:, columns] = product[:SLOT_ROWS].astype(lower.dtype)
            upper[:, columns] = product[SLOT_ROWS:].astype(upper.dtype)
            return carry

        lax.fori_loop(0, HALF // 256, columns_of, 0)

    own_left_0.wait_recv()
    line_up(3, 0)
    own_right_1.wait_recv()
    line_up(2, 1)
    first_product(2 * SLOT_ROWS)
    second_product(2 * SLOT_ROWS, 0, side_raw.at[0], held.at[0])
    raw_left = ring_copy(side_raw.at[0], raw_in.at[0], r_send.at[2], r_recv.at[2], left)
    raw_left.start()
    second_product(2 * SLOT_ROWS, 1, held.at[1], side_raw.at[1])
    raw_right = ring_copy(side_raw.at[1], raw_in.at[1], r_send.at[3], r_recv.at[3], right)
    raw_right.start()
    on_right_0.wait_recv()
    line_up(1, 0)
    on_left_1.wait_recv()
    line_up(1, 1)
    first_product(0)
    second_product(0, 0, own_total.at[0], far_out.at[0])
    far_right = ring_copy(far_out.at[0], far_in.at[0], r_send.at[0], r_recv.at[0], right)
    far_right.start()
    second_product(0, 1, own_total.at[1], far_out.at[1])
    far_left = ring_copy(far_out.at[1], far_in.at[1], r_send.at[1], r_recv.at[1], left)
    far_left.start()
    far_right.wait_recv()
    side_sum[0] = (held[0] + far_in[0].astype(f32)).astype(bf16)
    sum_right = ring_copy(side_sum.at[0], sum_in.at[0], r_send.at[4], r_recv.at[4], right)
    sum_right.start()
    far_left.wait_recv()
    side_sum[1] = (held[1] + far_in[1].astype(f32)).astype(bf16)
    sum_left = ring_copy(side_sum.at[1], sum_in.at[1], r_send.at[5], r_recv.at[5], left)
    sum_left.start()

    for half, raw, summed in ((0, raw_left, sum_right), (1, raw_right, sum_left)):
        raw.wait_recv()
        summed.wait_recv()
        total = (
            own_total[half] + raw_in[half].astype(f32) + sum_in[half].astype(f32)
        ).astype(bf16)
        stacked = jnp.concatenate(
            [total[:, piece * TILE : (piece + 1) * TILE] for piece in range(PIECES)], axis=0
        )
        homeward[half] = jnp.dot(mix[...], stacked, preferred_element_type=f32).astype(bf16)
        plane_send(homeward, back, b_sem, half)

    for half in range(2):
        wait_for(back.at[half], b_sem.at[half, 1])
        ordered = jnp.dot(unmix[...], back[half], preferred_element_type=f32).astype(bf16)
        for piece in range(PIECES):
            rows = ordered[piece * SLOT_ROWS : (piece + 1) * SLOT_ROWS, :]
            begin = half * HALF + piece * TILE
            columns = slice(begin, begin + TILE)
            expert_sum = jnp.dot(
                weight_parts, jnp.concatenate([rows, rows, rows], axis=0), preferred_element_type=f32
            )
            gate = token_mod[:, 3 * width + begin : 3 * width + begin + TILE]
            out_ref[:, columns] = (residual[:, columns] + gate * expert_sum).astype(bf16)

    share_mod.wait_send()
    wait_for(attended.at[pl.ds(0, PLANE - 1)], a_sem.at[0])
    for half in range(2):
        wait_for(landed.at[half, pl.ds(0, 16 * (PLANE - 1))], d_sem.at[half, 0])
        wait_for(back.at[half, pl.ds(0, 16 * (PLANE - 1))], b_sem.at[half, 0])
    for copy in (
        own_right_0,
        own_left_1,
        on_right_0,
        on_left_1,
        own_right_1,
        own_left_0,
        far_right,
        far_left,
        raw_left,
        raw_right,
        sum_right,
        sum_left,
    ):
        copy.wait_send()


def feed_forward(
    attended_head, stream, modulation, expert_in, expert_out, query_tags, picks, used, router
):
    tokens, width = stream.shape
    bf16 = jnp.bfloat16
    f32 = jnp.float32
    part = expert_in.shape[2]
    block = PIECES * SLOT_ROWS
    anywhere = pl.BlockSpec(memory_space=pl.ANY)
    inside = pl.BlockSpec(memory_space=pltpu.VMEM)
    dma = pltpu.SemaphoreType.DMA
    return pl.pallas_call(
        experts_kernel,
        out_shape=jax.ShapeDtypeStruct((tokens, width), bf16),
        in_specs=[anywhere] * 6 + [inside] * 3,
        out_specs=inside,
        scratch_shapes=[
            pltpu.VMEM((tokens, width), bf16),
            pltpu.VMEM(modulation.shape, bf16),
            pltpu.VMEM((tokens, width // PLANE), bf16),
            pltpu.VMEM((width, part), bf16),
            pltpu.VMEM((part, width), bf16),
            pltpu.VMEM((PLANE, tokens, width // PLANE), bf16),
            pltpu.VMEM((tokens, 4 * width), f32),
            pltpu.VMEM((tokens, width), f32),
            pltpu.VMEM((tokens, width), bf16),
            pltpu.VMEM((block, PIECES * tokens), bf16),
            pltpu.VMEM((block, block), bf16),
            pltpu.VMEM((block, block), bf16),
            pltpu.VMEM((2, block, TILE), bf16),
            pltpu.VMEM((2, block, TILE), bf16),
            pltpu.VMEM((4, 2, block, TILE), bf16),
            pltpu.VMEM((4 * SLOT_ROWS, width), bf16),
            pltpu.VMEM((4 * SLOT_ROWS, part), bf16),
            pltpu.VMEM((2, SLOT_ROWS, HALF), bf16),
            pltpu.VMEM((2, SLOT_ROWS, HALF), bf16),
            pltpu.VMEM((2, SLOT_ROWS, HALF), bf16),
            pltpu.VMEM((2, SLOT_ROWS, HALF), bf16),
            pltpu.VMEM((2, SLOT_ROWS, HALF), bf16),
            pltpu.VMEM((2, SLOT_ROWS, HALF), bf16),
            pltpu.VMEM((2, SLOT_ROWS, HALF), f32),
            pltpu.VMEM((2, SLOT_ROWS, HALF), f32),
            pltpu.VMEM((2, block, TILE), bf16),
            pltpu.VMEM((2, block, TILE), bf16),
            pltpu.VMEM((SLOT_ROWS, width), bf16),
            dma((6,)),
            dma((2,)),
            dma((2,)),
            dma((2, 2)),
            dma((6,)),
            dma((6,)),
            dma((6,)),
            dma((6,)),
            dma((2, 2)),
        ],
        compiler_params=pltpu.CompilerParams(
            collective_id=1, has_side_effects=True, vmem_limit_bytes=58 * 2**20
        ),
        name="experts",
    )(
        attended_head,
        stream,
        modulation,
        expert_in,
        expert_out,
        query_tags,
        picks,
        used,
        router,
    )


def on_device(
    stream,
    query_input,
    key_input,
    value_input,
    sample_id,
    timestep,
    class_id,
    class_table,
    mod_weight,
    router_weight,
    expert_in,
    expert_out,
    picked,
    counts,
):
    head_query, keys, values, query_tags, key_tags, modulation, spans = exchange(
        query_input,
        key_input,
        value_input,
        mod_weight,
        class_table,
        class_id,
        timestep,
        sample_id,
    )
    attended_head = local_attention(spans, head_query, query_tags, keys, key_tags, values)
    return feed_forward(
        attended_head,
        stream,
        modulation,
        expert_in,
        expert_out,
        query_tags,
        picked[:, 0, :].T,
        counts.T,
        router_weight.T,
    )


def solution(mesh):
    return jax.shard_map(
        on_device,
        mesh=mesh,
        in_specs=(
            P(("exp", "seq"), None),
            P(("exp", "seq"), None),
            P(("exp", "seq"), None),
            P(("exp", "seq"), None),
            P(),
            P(),
            P(),
            P(None, "seq"),
            P(None, ("seq", "exp")),
            P(),
            P("seq", None, "exp"),
            P("seq", "exp", None),
            P(None, ("exp", "seq"), None),
            P(None, ("exp", "seq")),
        ),
        out_specs=P(("exp", "seq"), None),
        check_vma=False,
    )
```
